256 devices in a mesh: dp: 64 (over y, z, core), seq: 4 (over x).
Axes of the slice: x: 4, y: 4, z: 8, core: 2. Of those that a mesh axis runs over, the one named last changes fastest.
Arguments:
- audio: bfloat16 [192, 100, 1280], P('dp', None, 'seq'), may hold values from -10 to 10
- counts: int32 [64], P('dp'), may hold values from 1 to 3, as said below
- lengths: int32 [192], P('dp'), may hold values from 2 to 100, as said below
- positions: int32 [192, 50], P('dp'), may hold values from 0 to 159, as said below
- w_qkv: bfloat16 [3, 1280, 1280], P(None, None, 'seq'), may hold values from -8 to 8
- w_out: bfloat16 [1280, 1280], P('seq'), may hold values from -0.15625 to 0.15625
- w_proj: bfloat16 [1280, 3584], P(None, 'seq'), may hold values from -0.15625 to 0.15625
- cotangent: bfloat16 [10240, 3584], P(('dp', 'seq')), may hold values from -0.0625 to 0.0625
Outputs:
- embeds: bfloat16 [10240, 3584], P(('dp', 'seq'))
- grad_qkv: float32 [3, 1280, 1280], P(None, 'dp', 'seq')
- grad_out: float32 [1280, 1280], P('seq', 'dp')
The draws below stay inside these ranges and needn't reach their ends.
Inputs may be any that keep to these rules, and one draw needn't show every extreme that they name: `counts`: for i below 32, entries i and i + 32 sum to at most 4. `lengths`: even. `positions`: the 150 entries of the blocks of one index of dp all differ.
All inputs are finite; a program needn't handle non-finite values.
Results may differ from the reference program's by a relative error of at most 0.023.
Values may be sent and summed in bfloat16 or wider, within the bound.
A program may use at most 128 MiB of HBM per device.

```python
import jax
import jax.numpy as jnp
from jax import lax

D = 1280
H = 20
HS = 64
ADAPT = 3584
W = 100
P_SIZE = 50
BLK_DEV = 2
CAP = 3
SEQ_ROWS = 160
N_DP = 64


def draw_counts(key, part):
    key = jax.random.fold_in(key, 11)
    half_axis = N_DP // 2
    top_count = 2 * BLK_DEV - 1
    first_key, second_key, order_key = jax.random.split(key, 3)
    leading = jax.random.randint(first_key, (half_axis,), 1, top_count + 1)
    leading = leading.at[0].set(top_count)
    partner = jax.random.randint(second_key, (half_axis,), 1, 2 * BLK_DEV - leading + 1)
    flipped = jax.random.randint(order_key, (half_axis,), 0, 2) == 1
    lower_half = jnp.where(flipped, partner, leading)
    upper_half = jnp.where(flipped, leading, partner)
    return jnp.concatenate([lower_half, upper_half]).astype(jnp.int32)


def draw_lengths(key, part):
    key = jax.random.fold_in(key, 12)
    short_key, kind_key = jax.random.split(key)
    total_slots = N_DP * CAP
    shorter = 2 * jax.random.randint(short_key, (total_slots,), 1, W // 2 + 1)
    complete = jax.random.randint(kind_key, (total_slots,), 0, 4) < 3
    drawn = jnp.where(complete, W, shorter)
    return drawn.at[0].set(W).astype(jnp.int32)


def draw_positions(key, part):
    key = jax.random.fold_in(key, 13)
    live_rows = CAP * P_SIZE

    def one_group(group_key):
        pick_key, order_key = jax.random.split(group_key)
        chosen = jax.random.permutation(pick_key, SEQ_ROWS - 1)[:live_rows - 1].astype(jnp.int32)
        chosen = jnp.concatenate([chosen, jnp.full((1,), SEQ_ROWS - 1, jnp.int32)])
        return jax.random.permutation(order_key, chosen).reshape(CAP, P_SIZE)
    group_keys = jax.random.split(key, N_DP)
    return jax.vmap(one_group)(group_keys).reshape(N_DP * CAP, P_SIZE).astype(jnp.int32)


def draw_audio(key, part):
    key = jax.random.fold_in(key, 14)
    array_shape = (N_DP * CAP, W, D)
    return jnp.clip(jax.random.normal(key, array_shape, jnp.float32), -6.0, 6.0).astype(jnp.bfloat16)


def draw_w_qkv(key, part):
    key = jax.random.fold_in(key, 15)
    deviation = D ** (-0.5)
    return (jnp.clip(jax.random.normal(key, (3, D, D), jnp.float32), -6.0, 6.0) * deviation).astype(jnp.bfloat16)


def block_scale(stream_key, shape, pieces, low, high):
    level = 1.0
    for axis_at, parts in pieces:
        draws = jax.random.uniform(jax.random.fold_in(jax.random.fold_in(stream_key, 6), axis_at), (parts,), jnp.float32, low / len(pieces), high / len(pieces))
        level = level * jnp.repeat(jnp.exp(draws), shape[axis_at] // parts).reshape((-1,) + (1,) * (len(shape) - 1 - axis_at))
    return level


def bell_draw(stream_key, dims, scale, most, cuts=(), kind=jnp.bfloat16):
    entries = jax.random.normal(stream_key, dims, jnp.float32) * scale
    if len(cuts) > 0:
        entries = block_scale(stream_key, dims, cuts, -0.22, 0.18) * entries
    return jnp.clip(entries, min=-most, max=most).astype(kind)


def setup_inputs(seed: int = 0) -> dict:
    key_of = jax.random.split(jax.random.key(seed), 9)
    audio = draw_audio(jax.random.fold_in(key_of[8], 71), 0)
    counts = draw_counts(jax.random.fold_in(key_of[8], 71), 0)
    lengths = draw_lengths(jax.random.fold_in(key_of[8], 71), 0)
    positions = draw_positions(jax.random.fold_in(key_of[8], 71), 0)
    w_qkv = draw_w_qkv(jax.random.fold_in(key_of[8], 71), 0)
    w_out = bell_draw(key_of[5], (D, D), D ** -0.5, 0.15625, ((0, 4),))
    w_proj = bell_draw(key_of[6], (D, ADAPT), D ** -0.5, 0.15625, ((1, 4),))
    cotangent = bell_draw(key_of[7], (N_DP * SEQ_ROWS, ADAPT), (1.0 / (N_DP * CAP * P_SIZE) ** 0.5), 0.0625, ((0, 256),))
    return dict(audio=audio, counts=counts, lengths=lengths, positions=positions, w_qkv=w_qkv, w_out=w_out, w_proj=w_proj, cotangent=cotangent)


EPSILON = 1e-05

def normalize(row_block):
    average = lax.optimization_barrier(jnp.mean(row_block, axis=-1, keepdims=True))
    centred = row_block - average
    spread = lax.optimization_barrier(jnp.mean(centred * centred, axis=-1, keepdims=True))
    inverse = lax.rsqrt(spread + EPSILON)
    return (centred * inverse, inverse)

def attend_forward(queries, keys_in, values_in, key_ok, scaling):
    scores = jnp.einsum('bqhd,bkhd->bhqk', queries.astype(jnp.float32), keys_in.astype(jnp.float32)) * scaling
    scores = jnp.where(key_ok[:, None, None, :], scores, jnp.float32(-1e+30))
    row_top = lax.optimization_barrier(jnp.max(scores, axis=-1, keepdims=True))
    powered = jnp.exp(scores - row_top)
    weights = powered / lax.optimization_barrier(jnp.sum(powered, axis=-1, keepdims=True))
    weights_half = weights.astype(jnp.bfloat16)
    attended = jnp.einsum('bhqk,bkhd->bqhd', weights_half.astype(jnp.float32), values_in.astype(jnp.float32))
    return (weights, weights_half, attended.astype(jnp.bfloat16))

def attend_backward(queries, keys_in, values_in, weights, weights_half, mixed_grad, scaling):
    prob_grad = jnp.einsum('bqhd,bkhd->bhqk', mixed_grad.astype(jnp.float32), values_in.astype(jnp.float32))
    score_grad = weights * (prob_grad - lax.optimization_barrier(jnp.sum(weights * prob_grad, axis=-1, keepdims=True)))
    score_half = score_grad.astype(jnp.bfloat16).astype(jnp.float32)
    query_grad = jnp.einsum('bhqk,bkhd->bqhd', score_half, keys_in.astype(jnp.float32)) * scaling
    key_grad = jnp.einsum('bhqk,bqhd->bkhd', score_half, queries.astype(jnp.float32)) * scaling
    value_grad = jnp.einsum('bhqk,bqhd->bkhd', weights_half.astype(jnp.float32), mixed_grad.astype(jnp.float32))
    return (query_grad.astype(jnp.bfloat16), key_grad.astype(jnp.bfloat16), value_grad.astype(jnp.bfloat16))

def reference(audio, counts, lengths, positions, w_qkv, w_out, w_proj, cotangent):
    scaling = HS ** (-0.5)

    def group_pass(totals, group):
        audio_group, count_group, length_group, position_group, cotangent_group = group
        total_qkv, total_out = totals
        slot_index = jnp.arange(CAP, dtype=jnp.int32)
        live_length = jnp.where(slot_index < count_group, length_group, 0)
        full_audio = audio_group.astype(jnp.float32)
        normed_half = normalize(full_audio)[0].astype(jnp.bfloat16).reshape(CAP * W, D)
        projections = [jnp.dot(normed_half, w_qkv[which], preferred_element_type=jnp.float32).astype(jnp.bfloat16).reshape(CAP, W, H, HS) for which in range(3)]
        key_ok = jnp.arange(W, dtype=jnp.int32)[None, :] < jnp.maximum(live_length, 1)[:, None]
        weights, weights_half, attended = attend_forward(projections[0], projections[1], projections[2], key_ok, scaling)
        attended_rows = attended.reshape(CAP * W, D)
        hidden = full_audio.reshape(CAP * W, D) + jnp.dot(attended_rows, w_out, preferred_element_type=jnp.float32)
        pooled = lax.optimization_barrier(jnp.mean(hidden.reshape(CAP, P_SIZE, 2, D), axis=2))
        normed_rows, inverse = normalize(pooled)
        adapted = normed_rows.astype(jnp.bfloat16).reshape(CAP * P_SIZE, D)
        adapter_rows = jnp.dot(adapted, w_proj, preferred_element_type=jnp.float32).astype(jnp.bfloat16)
        row_live = (jnp.arange(P_SIZE, dtype=jnp.int32)[None, :] < (live_length // 2)[:, None]).reshape(CAP * P_SIZE, 1)
        target = position_group.reshape(CAP * P_SIZE).astype(jnp.int32)
        placed = jnp.where(row_live, adapter_rows, jnp.zeros_like(adapter_rows))
        slot_table = jnp.zeros((SEQ_ROWS, ADAPT), jnp.bfloat16).at[target].set(placed)
        row_grads = jnp.where(row_live, cotangent_group[target], jnp.zeros_like(adapter_rows))
        adapted_grad = jnp.dot(row_grads, w_proj.T, preferred_element_type=jnp.float32).astype(jnp.bfloat16)
        grad_rows = adapted_grad.astype(jnp.float32).reshape(CAP, P_SIZE, D)
        pooled_grad = inverse * (grad_rows - lax.optimization_barrier(jnp.mean(grad_rows, axis=-1, keepdims=True)) - normed_rows * lax.optimization_barrier(jnp.mean(grad_rows * normed_rows, axis=-1, keepdims=True)))
        attention_grad = jnp.repeat(pooled_grad * 0.5, 2, axis=1).astype(jnp.bfloat16).reshape(CAP * W, D)
        total_out = total_out + jnp.dot(attended_rows.T, attention_grad, preferred_element_type=jnp.float32)
        mixed_grad = jnp.dot(attention_grad, w_out.T, preferred_element_type=jnp.float32).astype(jnp.bfloat16).reshape(CAP, W, H, HS)
        backward = attend_backward(projections[0], projections[1], projections[2], weights, weights_half, mixed_grad, scaling)
        qkv_terms = jnp.stack([jnp.dot(normed_half.T, grad_part.reshape(CAP * W, D), preferred_element_type=jnp.float32) for grad_part in backward])
        total_qkv = total_qkv + qkv_terms
        return ((total_qkv, total_out), slot_table)
    start_totals = (jnp.zeros((3, D, D), jnp.float32), jnp.zeros((D, D), jnp.float32))
    groups = (audio.reshape(N_DP, CAP, W, D), counts, lengths.reshape(N_DP, CAP), positions.reshape(N_DP, CAP, P_SIZE), cotangent.reshape(N_DP, SEQ_ROWS, ADAPT))
    totals, slot_tables = lax.scan(group_pass, start_totals, groups)
    embeds = slot_tables.reshape(N_DP * SEQ_ROWS, ADAPT)
    return (embeds, totals[0], totals[1])
```

```python
import functools

import jax
import jax.numpy as jnp
from jax import lax
from jax.experimental import pallas as pl
from jax.experimental.pallas import tpu as pltpu
from jax.sharding import PartitionSpec as P

MESH = pl.DeviceIdType.MESH
F32 = jnp.float32
BF16 = jnp.bfloat16
EPSILON = 1e-05
SCALING = 0.125
PARTS = (
    (0, 0, 160, "ABa"),
    (1, 0, 160, "BAb"),
    (2, 0, 160, "aAB"),
    (3, 0, 160, "bBA"),
    (4, 0, 80, "ABa"),
    (4, 80, 80, "BAb"),
)


def dot(a, b):
    return jnp.dot(a, b, preferred_element_type=F32)


def dot_nt(a, b):
    return lax.dot_general(a, b, (((1,), (1,)), ((), ())), preferred_element_type=F32)


def dot_tn(a, b):
    return lax.dot_general(a, b, (((0,), (0,)), ((), ())), preferred_element_type=F32)


def fold(rows, width, extra):
    pieces = [rows[:, i : i + width] for i in range(0, rows.shape[1], width)]
    if extra:
        pieces.append(jnp.zeros((extra, width), F32))
    return jnp.concatenate(pieces, axis=0).astype(BF16)


def unfold(folded, count):
    wide = folded.astype(F32)
    return jnp.concatenate([wide[40 * i : 40 * i + 40] for i in range(count)], axis=1)


def normalize(rows):
    centred = rows - jnp.mean(rows, axis=-1, keepdims=True)
    inverse = lax.rsqrt(jnp.mean(centred * centred, axis=-1, keepdims=True) + EPSILON)
    return centred * inverse, inverse


def received_shape(part, step):
    _, _, rows, order = part
    before = order[:step]
    y_done = sum(letter in "AB" for letter in before)
    z_done = any(letter in "ab" for letter in before)
    if order[step] in "AB":
        return (2 if y_done == 0 else 1, 1 if z_done else 2, rows, 128)
    return ((4, 2, 1)[y_done], 1, rows, 128)


def kernel(whole, *refs):
    (counts, lengths, positions, audio, cotangent, w_qkv, w_out, w_proj) = refs[:8]
    embeds, grad_qkv, grad_out = refs[8:11]
    (
        wq, wo, wp, tmp, aud, cot_s, cot_r, gt_s, gt_r, t_s, t_r, ag_a, ad_a, e_s, e_r,
        nb, nt, pj, q2s, qr_s, k_s, v_s, prob, attp_s, agt, mgp, dqk, dvs, grad, core_r, total, final,
        z_s, z_r, f_s, f_r, w_sem, x_send, x_recv, c_send, c_recv, r_send, r_recv, z_send, z_recv,
    ) = refs[11 : 11 + 45]
    r_bufs = refs[11 + 45 :]

    dp = lax.axis_index("dp")
    x = lax.axis_index("seq")
    y = dp // 16
    z = (dp // 2) % 8
    c = dp % 2
    par = z % 2
    zp = z // 2

    def at(yy, zz, cc):
        return (yy * 16 + zz * 2 + cc, x)

    peers = [(dp, (x + k) % 4) for k in (1, 2, 3)]
    partner = {
        "A": at(y ^ 1, z, c),
        "B": at(y ^ 3, z, c),
        "a": at(y, z ^ 1, c),
        "b": at(y, (z + 7 + 2 * par) % 8, c),
    }
    core_peer = at(y, z, 1 - c)
    z_peers = [at(y, z ^ (2 * k), c) for k in (1, 2, 3)]

    weight_copies = []
    for s in range(4):
        weight_copies.append((w_qkv.at[:, pl.ds(320 * s, 256)], wq.at[:, pl.ds(256 * s, 256)]))
        weight_copies.append((w_qkv.at[:, pl.ds(320 * s + 256, 64)], wq.at[:, pl.ds(1024 + 64 * s, 64)]))
    weight_copies.append((w_out, wo))
    weight_copies.append((w_proj, wp))
    weight_copies = [
        pltpu.make_async_copy(src, dst, w_sem.at[i]) for i, (src, dst) in enumerate(weight_copies)
    ]
    for copy in weight_copies:
        copy.start()

    barrier = pltpu.get_barrier_semaphore()
    everyone = peers + ([core_peer] + list(partner.values()) + z_peers if whole else [])
    for device in everyone:
        pl.semaphore_signal(barrier, inc=1, device_id=device, device_id_type=MESH)

    lane = lax.broadcasted_iota(jnp.int32, (112, 128), 1)
    low = lane < 64
    tmp[...] = jnp.zeros_like(tmp)
    pj[...] = jnp.zeros_like(pj)
    mgp[...] = jnp.zeros_like(mgp)
    for b in range(3):
        tmp[b, 0:100, 0:320] = audio[b].astype(F32)
        packed = tmp[b, 0:64, 256:384] + pltpu.roll(tmp[b, 64:128, 256:384], 64, 1)
        own = jnp.concatenate([tmp[b, 0:112, 0:128], tmp[b, 0:112, 128:256], packed], axis=0)
        aud[x, b] = own.astype(BF16)
    cot_rows = cotangent[...].astype(F32)
    for t in range(4):
        cot_s[t] = fold(cot_rows[:, 896 * t : 896 * t + 896], 128, 8)
    cot_r[x] = cot_s[x]

    pl.semaphore_wait(barrier, len(everyone))

    started = []

    def to_peers(slot, source, target):
        copies = []
        for k in (1, 2, 3):
            there = (x + k) % 4
            copy = pltpu.make_async_remote_copy(
                src_ref=source(there),
                dst_ref=target(k),
                send_sem=x_send.at[slot, k - 1],
                recv_sem=x_recv.at[slot, k - 1],
                device_id=(dp, there),
                device_id_type=MESH,
            )
            copy.start()
            copies.append(copy)
        started.extend(copies)
        return copies

    def arrive(copies):
        for copy in copies:
            copy.wait_recv()

    audio_copies = []
    for b in range(3):
        block = aud.at[x, b]
        audio_copies.append(to_peers(b, lambda there: block, lambda k: block))
        if b == 1:
            cot_copies = to_peers(3, lambda there: cot_s.at[there], lambda k: cot_r.at[x])

    pos_pad = jnp.concatenate([positions[...].astype(F32), jnp.zeros((13, 50), F32)], axis=0).astype(BF16)
    frame_row = lax.broadcasted_iota(jnp.int32, (50, 112), 0)
    frame_col = lax.broadcasted_iota(jnp.int32, (50, 112), 1)
    spread = jnp.where(frame_row == frame_col // 2, 1.0, 0.0).astype(BF16)
    pos_lanes = dot(pos_pad, spread)
    frame_row_t = lax.broadcasted_iota(jnp.int32, (112, 50), 0)
    frame_col_t = lax.broadcasted_iota(jnp.int32, (112, 50), 1)
    spread_t = jnp.where(frame_row_t // 2 == frame_col_t, 1.0, 0.0).astype(BF16)
    pos_sub = dot_nt(spread_t, pos_pad)
    lives = [jnp.where(b < counts[0], lengths[b], 0) for b in range(3)]

    def place(b, first, count):
        row = lax.broadcasted_iota(jnp.int32, (count, 112), 0) + first
        frame = lax.broadcasted_iota(jnp.int32, (count, 112), 1)
        hit = (row.astype(F32) == pos_lanes[b : b + 1, :]) & (frame < lives[b])
        return jnp.where(hit, 1.0, 0.0).astype(BF16)

    def unplace(b):
        frame = lax.broadcasted_iota(jnp.int32, (112, 160), 0)
        row = lax.broadcasted_iota(jnp.int32, (112, 160), 1)
        hit = (row.astype(F32) == pos_sub[:, b : b + 1]) & (frame < lives[b])
        return jnp.where(hit, 1.0, 0.0).astype(BF16)

    def split_heads(tile):
        return jnp.concatenate([jnp.where(low, tile, 0.0), jnp.where(low, 0.0, tile)], axis=0).astype(BF16)

    for copy in weight_copies[:8]:
        copy.wait()

    attp = [jnp.zeros((160, 128), F32) for _ in range(3)]
    pooled_audio = jnp.zeros((40, 1280), F32)

    def forward(b, attp, pooled_audio):
        arrive(audio_copies[b])
        tiles = []
        for s in range(4):
            tiles.append(aud[s, b, 0:112].astype(F32))
            tiles.append(aud[s, b, 112:224].astype(F32))
        for s in (0, 2):
            left = aud[s, b, 224:288].astype(F32)
            right = aud[s + 1, b, 224:288].astype(F32)
            left_turned = pltpu.roll(left, 64, 1)
            right_turned = pltpu.roll(right, 64, 1)
            top = jnp.where(low[0:64], left, right_turned)
            bottom = jnp.where(low[0:64], left_turned, right)
            tiles.append(jnp.concatenate([top, bottom[0:48]], axis=0))
        frames = jnp.concatenate(tiles, axis=1)
        pooled_audio = pooled_audio + dot(place(b, 40 * x, 40), frames.astype(BF16))
        normed = normalize(frames)[0].astype(BF16)
        nb[112 * b : 112 * b + 112, :] = normed
        for j in range(3):
            pj[j, :, 0:320] = dot(normed, wq[j])
        k_s[b] = pj[1].astype(BF16)
        v_s[b] = pj[2].astype(BF16)
        key_limit = jnp.maximum(lives[b], 1)
        placed = place(b, 0, 160)
        for g in range(3):
            cols = slice(128 * g, 128 * g + 128)
            q_tile = pj[0, :, cols]
            if g < 2:
                queries = split_heads(q_tile)
                q2s[b, g] = queries
            else:
                queries = q_tile.astype(BF16)
                qr_s[b] = queries
            rows = queries.shape[0]
            scores = dot_nt(queries, k_s[b, :, cols]) * SCALING
            key = lax.broadcasted_iota(jnp.int32, (rows, 112), 1)
            scores = jnp.where(key < key_limit, scores, -1e30)
            powered = jnp.exp(scores - jnp.max(scores, axis=-1, keepdims=True))
            weights = powered * (1.0 / jnp.sum(powered, axis=-1, keepdims=True))
            prob[b, g, 0:rows] = weights
            mixed = dot(weights.astype(BF16), v_s[b, :, cols])
            if g < 2:
                mixed = jnp.where(low, mixed[0:112], mixed[112:224])
            attp[g] = attp[g] + dot(placed, mixed.astype(BF16))
        return attp, pooled_audio

    attp, pooled_audio = forward(0, attp, pooled_audio)
    attp, pooled_audio = forward(1, attp, pooled_audio)

    weight_copies[9].wait()
    arrive(cot_copies)
    row_grads = jnp.concatenate([unfold(cot_r[s], 7) for s in range(4)], axis=0).astype(BF16)
    adapter_terms = dot_nt(row_grads, wp[...])
    for t in range(4):
        gt_s[t] = fold(adapter_terms[40 * t : 40 * t + 40], 640, 0)
    gt_copies = to_peers(4, lambda there: gt_s.at[there], lambda k: gt_r.at[k - 1])

    attp, pooled_audio = forward(2, attp, pooled_audio)
    for g in range(3):
        attp_s[g] = attp[g].astype(BF16)
    weight_copies[8].wait()
    head_terms = (
        dot(attp_s[0], wo[0:128]) + dot(attp_s[1], wo[128:256]) + dot(attp_s[2][:, 0:64], wo[256:320])
    )
    for t in range(4):
        t_s[t] = fold(head_terms[40 * t : 40 * t + 40], 640, 0)
    t_copies = to_peers(5, lambda there: t_s.at[there], lambda k: t_r.at[k - 1])

    nt[...] = nb[...].T
    pooled_audio = jnp.concatenate(
        [
            piece
            for s in range(4)
            for piece in (
                pooled_audio[:, 256 * s : 256 * s + 256],
                pooled_audio[:, 1024 + 64 * s : 1088 + 64 * s],
            )
        ],
        axis=1,
    )

    arrive(gt_copies)
    adapted_grad = gt_s[x].astype(F32)
    for k in range(3):
        adapted_grad = adapted_grad + gt_r[k].astype(F32)
    adapted_grad = unfold(adapted_grad.astype(BF16), 2)

    arrive(t_copies)
    attention = t_s[x].astype(F32)
    for k in range(3):
        attention = attention + t_r[k].astype(F32)
    attention = jnp.concatenate([attention[0:40], attention[40:80]], axis=1)
    normed_rows, inverse = normalize((pooled_audio + attention) * 0.5)
    pooled_grad = inverse * (
        adapted_grad
        - jnp.mean(adapted_grad, axis=-1, keepdims=True)
        - normed_rows * jnp.mean(adapted_grad * normed_rows, axis=-1, keepdims=True)
    )
    ag_a[x] = fold(pooled_grad * 0.5, 640, 0)
    ag_copies = to_peers(6, lambda there: ag_a.at[x], lambda k: ag_a.at[x])
    ad_a[x] = fold(normed_rows, 640, 0)
    ad_copies = to_peers(7, lambda there: ad_a.at[x], lambda k: ad_a.at[x])

    arrive(ag_copies)
    attention_grad = jnp.concatenate([unfold(ag_a[s], 2) for s in range(4)], axis=0).astype(BF16)
    agt[...] = attention_grad.T
    mgp[:, 0:320] = dot_nt(attention_grad, wo[...]).astype(BF16)

    for b in range(3):
        rows = slice(112 * b, 112 * b + 112)
        mixed_grad = dot(unplace(b), mgp[...])
        for g in range(3):
            cols = slice(128 * g, 128 * g + 128)
            tile = mixed_grad[:, cols]
            if g < 2:
                grads, queries, count = split_heads(tile), q2s[b, g], 224
            else:
                grads, queries, count = tile.astype(BF16), qr_s[b], 112
            weights = prob[b, g, 0:count]
            prob_grad = dot_nt(grads, v_s[b, :, cols])
            inner = jnp.sum(weights * prob_grad, axis=-1, keepdims=True)
            score_half = (weights * (prob_grad - inner)).astype(BF16)
            query_grad = dot(score_half, k_s[b, :, cols])
            if g < 2:
                query_grad = jnp.where(low, query_grad[0:112], query_grad[112:224])
            query_grad = query_grad * SCALING
            key_grad = dot_tn(score_half, queries) * SCALING
            value_grad = dot_tn(weights.astype(BF16), grads)
            dvs[rows, cols] = value_grad.astype(BF16)
            if g < 2:
                dqk[rows, cols] = query_grad.astype(BF16)
                dqk[rows, 256 + 128 * g : 384 + 128 * g] = key_grad.astype(BF16)
            else:
                dqk[rows, 512:640] = (query_grad + pltpu.roll(key_grad, 64, 1)).astype(BF16)

    attp_turned = pltpu.roll(attp_s[2].astype(F32), 64, 1).astype(BF16)
    core_copies = []
    for yy in range(4):
        features = jnp.concatenate(
            [nt[256 * yy : 256 * yy + 256, :], nt[1024 + 64 * yy : 1088 + 64 * yy, :]], axis=0
        )
        backs = agt[320 * yy : 320 * yy + 320, :]
        first = dot(features, dqk[...])
        value_part = dot(features, dvs[...])
        out_part = [dot(backs, attp_s[0]), dot(backs, attp_s[1]), dot(backs, attp_turned)]
        halves = (
            [first[:, 128 * t : 128 * t + 128] for t in range(5)],
            [value_part[:, 0:128], value_part[:, 128:256], out_part[0], out_part[1], value_part[:, 256:384] + out_part[2]],
        )
        for half in range(2):
            for t in range(5):
                for side in range(2):
                    grad[half, yy, t, side] = jnp.concatenate(
                        [halves[half][t][40 * i : 40 * i + 40] for i in range(side, 8, 2)], axis=0
                    ).astype(BF16)
        if whole:
            copy = pltpu.make_async_remote_copy(
                src_ref=grad.at[1 - c, yy],
                dst_ref=core_r.at[yy],
                send_sem=c_send.at[yy],
                recv_sem=c_recv.at[yy],
                device_id=core_peer,
                device_id_type=MESH,
            )
            copy.start()
            core_copies.append(copy)
    started.extend(core_copies)

    def start_embeds():
        arrive(ad_copies)
        adapted = jnp.concatenate([unfold(ad_a[s], 2) for s in range(4)], axis=0).astype(BF16)
        adapter_rows = dot(adapted, wp[...])
        for t in range(4):
            e_s[t] = fold(adapter_rows[40 * t : 40 * t + 40], 128, 8)
        e_r[x] = e_s[x]
        return to_peers(8, lambda there: e_s.at[there], lambda k: e_r.at[x])

    def finish_embeds(copies):
        arrive(copies)
        for s in range(4):
            embeds[:, 896 * s : 896 * s + 896] = unfold(e_r[s], 7).astype(BF16)

    if not whole:
        finish_embeds(start_embeds())
        grad_qkv[...] = grad[...].astype(F32)
        grad_out[...] = jnp.zeros_like(grad_out)
        for copy in started:
            copy.wait_send()
        return

    for yy in range(4):
        core_copies[yy].wait_recv()
        total[yy] = (grad[c, yy].astype(F32) + core_r[yy].astype(F32)).astype(BF16)

    def blocks(order, step):
        y_before = [letter for letter in order[:step] if letter in "AB"]
        z_done = any(letter in "ab" for letter in order[:step])
        letter = order[step]
        if letter in "AB":
            near = y ^ (1 if letter == "A" else 3)
            other = y ^ (3 if letter == "A" else 1)
            sides = (par, par) if z_done else (None, None)
            if y_before:
                return [near], [y], sides
            return [near, y ^ 2], [y, other], sides
        held = [0, 1, 2, 3]
        if len(y_before) == 1:
            held = [y, y ^ (3 if y_before[0] == "A" else 1)]
        elif len(y_before) == 2:
            held = [y]
        return held, held, (1 - par, par)

    def begin(p, step):
        tile, row, count, order = PARTS[p]
        send, _, (side, _) = blocks(order, step)
        landing = r_bufs[3 * p + step]
        copies = []
        for i, block in enumerate(send):
            pick = pl.ds(0, 2) if side is None else pl.ds(side, 1)
            copy = pltpu.make_async_remote_copy(
                src_ref=total.at[block, tile, pick, pl.ds(row, count)],
                dst_ref=landing.at[i],
                send_sem=r_send.at[p, step, i],
                recv_sem=r_recv.at[p, step, i],
                device_id=partner[order[step]],
                device_id_type=MESH,
            )
            copy.start()
            copies.append(copy)
        started.extend(copies)
        return copies

    def end(p, step, copies):
        tile, row, count, order = PARTS[p]
        _, keep, (_, side) = blocks(order, step)
        landing = r_bufs[3 * p + step]
        rows = pl.ds(row, count)
        arrive(copies)
        for i, block in enumerate(keep):
            if step == 2:
                final[tile, rows] = total[block, tile, par, rows].astype(F32) + landing[i, 0].astype(F32)
            elif side is None:
                for k in range(2):
                    kept = total[block, tile, k, rows].astype(F32) + landing[i, k].astype(F32)
                    total[block, tile, k, rows] = kept.astype(BF16)
            else:
                kept = total[block, tile, side, rows].astype(F32) + landing[i, 0].astype(F32)
                total[block, tile, side, rows] = kept.astype(BF16)

    flying = [begin(p, 0) for p in range(len(PARTS))]
    embed_copies = start_embeds()
    for step in (1, 2):
        for p in range(len(PARTS)):
            end(p, step - 1, flying[p])
            flying[p] = begin(p, step)
    for p in range(len(PARTS)):
        end(p, 2, flying[p])

    for j in range(4):
        z_s[j] = jnp.concatenate(
            [final[t, 40 * j : 40 * j + 40] for t in range(5)] + [jnp.zeros((8, 128), F32)], axis=0
        ).astype(BF16)
    z_copies = []
    for k in (1, 2, 3):
        copy = pltpu.make_async_remote_copy(
            src_ref=z_s.at[zp ^ k],
            dst_ref=z_r.at[k - 1],
            send_sem=z_send.at[k - 1],
            recv_sem=z_recv.at[k - 1],
            device_id=z_peers[k - 1],
            device_id_type=MESH,
        )
        copy.start()
        z_copies.append(copy)
    started.extend(z_copies)
    finish_embeds(embed_copies)
    arrive(z_copies)
    mine = z_s[zp].astype(F32)
    for k in range(3):
        mine = mine + z_r[k].astype(F32)
    first_core = c == 0
    own_tiles = []
    f_s[...] = jnp.zeros_like(f_s)
    for t in range(5):
        rows = mine[40 * t : 40 * t + 40]
        early, late = rows[0:20], rows[20:40]
        own_tiles.append(jnp.where(first_core, early, late))
        f_s[t, 0:20] = jnp.where(first_core, late, early).astype(BF16)
    copy = pltpu.make_async_remote_copy(
        src_ref=f_s,
        dst_ref=f_r,
        send_sem=c_send.at[4],
        recv_sem=c_recv.at[4],
        device_id=core_peer,
        device_id_type=MESH,
    )
    copy.start()
    started.append(copy)
    copy.wait_recv()
    for t in range(5):
        got = f_r[t, 0:20].astype(F32)
        left = jnp.where(first_core, own_tiles[t], got)
        right = jnp.where(first_core, got, own_tiles[t])
        if t < 2:
            cols = slice(128 * t, 128 * t + 128)
            grad_qkv[0, :, cols] = left
            grad_qkv[2, :, cols] = right
        elif t < 4:
            cols = slice(128 * t - 256, 128 * t - 128)
            grad_qkv[1, :, cols] = left
            grad_out[:, cols] = right
        else:
            grad_qkv[0, :, 256:320] = left[:, 0:64]
            grad_qkv[1, :, 256:320] = left[:, 64:128]
            grad_qkv[2, :, 256:320] = right[:, 0:64]
            grad_out[:, 256:320] = right[:, 64:128]
    for copy in started:
        copy.wait_send()


def call(whole, counts, lengths, positions, audio, cotangent, w_qkv, w_out, w_proj):
    vmem, dma = pltpu.VMEM, pltpu.SemaphoreType.DMA
    scratch = [
        vmem((3, 1280, 320), BF16),
        vmem((320, 1280), BF16),
        vmem((1280, 896), BF16),
        vmem((3, 128, 384), F32),
        vmem((4, 3, 288, 128), BF16),
        vmem((4, 288, 128), BF16),
        vmem((4, 288, 128), BF16),
        vmem((4, 80, 640), BF16),
        vmem((3, 80, 640), BF16),
        vmem((4, 80, 640), BF16),
        vmem((3, 80, 640), BF16),
        vmem((4, 80, 640), BF16),
        vmem((4, 80, 640), BF16),
        vmem((4, 288, 128), BF16),
        vmem((4, 288, 128), BF16),
        vmem((336, 1280), BF16),
        vmem((1280, 336), BF16),
        vmem((3, 112, 384), F32),
        vmem((3, 2, 224, 128), BF16),
        vmem((3, 112, 128), BF16),
        vmem((3, 112, 384), BF16),
        vmem((3, 112, 384), BF16),
        vmem((3, 3, 224, 112), F32),
        vmem((3, 160, 128), BF16),
        vmem((1280, 160), BF16),
        vmem((160, 384), BF16),
        vmem((336, 640), BF16),
        vmem((336, 384), BF16),
        vmem((2, 4, 5, 2, 160, 128), BF16),
        vmem((4, 5, 2, 160, 128), BF16),
        vmem((4, 5, 2, 160, 128), BF16),
        vmem((5, 160, 128), F32),
        vmem((4, 208, 128), BF16),
        vmem((3, 208, 128), BF16),
        vmem((5, 32, 128), BF16),
        vmem((5, 32, 128), BF16),
        dma((10,)),
        dma((9, 3)),
        dma((9, 3)),
        dma((5,)),
        dma((5,)),
        dma((6, 3, 4)),
        dma((6, 3, 4)),
        dma((3,)),
        dma((3,)),
    ]
    assert len(scratch) == 45
    scratch += [vmem(received_shape(part, step), BF16) for part in PARTS for step in range(3)]
    in_vmem = pl.BlockSpec(memory_space=pltpu.VMEM)
    in_smem = pl.BlockSpec(memory_space=pltpu.SMEM)
    anywhere = pl.BlockSpec(memory_space=pl.ANY)
    gq = (3, 20, 320) if whole else (2, 4, 5, 2, 160, 128)
    return pl.pallas_call(
        functools.partial(kernel, whole),
        out_shape=(
            jax.ShapeDtypeStruct((40, 3584), BF16),
            jax.ShapeDtypeStruct(gq, F32),
            jax.ShapeDtypeStruct((20, 320), F32),
        ),
        in_specs=[in_smem, in_smem, in_vmem, in_vmem, in_vmem, anywhere, anywhere, anywhere],
        out_specs=(in_vmem, in_vmem, in_vmem),
        scratch_shapes=scratch,
        compiler_params=pltpu.CompilerParams(
            collective_id=0, has_side_effects=True, vmem_limit_bytes=56 * 2**20
        ),
        name="sublayer",
    )(counts, lengths, positions, audio, cotangent, w_qkv, w_out, w_proj)


def shards(audio, counts, lengths, positions, w_qkv, w_out, w_proj, cotangent):
    embeds, grad_qkv, grad_out = call(
        True, counts, lengths, positions, audio, cotangent, w_qkv, w_out, w_proj
    )
    return embeds, grad_qkv, grad_out.T


def solution(mesh):
    in_specs = (
        P("dp", None, "seq"),
        P("dp"),
        P("dp"),
        P("dp", None),
        P(None, None, "seq"),
        P("seq", None),
        P(None, "seq"),
        P(("dp", "seq"), None),
    )
    out_specs = (P(("dp", "seq"), None), P(None, "dp", "seq"), P("seq", "dp"))
    return jax.shard_map(shards, mesh=mesh, in_specs=in_specs, out_specs=out_specs, check_vma=False)
```

```python
import functools

import jax
import jax.numpy as jnp
from jax import lax
from jax.experimental import pallas as pl
from jax.experimental.pallas import tpu as pltpu
from jax.sharding import PartitionSpec as P

MESH = pl.DeviceIdType.MESH
F32 = jnp.float32
BF16 = jnp.bfloat16
EPSILON = 1e-05
SCALING = 0.125
PARTS = (
    (0, 0, 160, "ABa"),
    (1, 0, 160, "BAb"),
    (2, 0, 160, "aAB"),
    (3, 0, 160, "bBA"),
    (4, 0, 80, "ABa"),
    (4, 80, 80, "BAb"),
)


def dot(a, b):
    return jnp.dot(a, b, preferred_element_type=F32)


def dot_nt(a, b):
    return lax.dot_general(a, b, (((1,), (1,)), ((), ())), preferred_element_type=F32)


def dot_tn(a, b):
    return lax.dot_general(a, b, (((0,), (0,)), ((), ())), preferred_element_type=F32)


def fold(rows, width, extra):
    pieces = [rows[:, i : i + width] for i in range(0, rows.shape[1], width)]
    if extra:
        pieces.append(jnp.zeros((extra, width), F32))
    return jnp.concatenate(pieces, axis=0).astype(BF16)


def unfold(folded, count):
    wide = folded.astype(F32)
    return jnp.concatenate([wide[40 * i : 40 * i + 40] for i in range(count)], axis=1)


def normalize(rows):
    centred = rows - jnp.mean(rows, axis=-1, keepdims=True)
    inverse = lax.rsqrt(jnp.mean(centred * centred, axis=-1, keepdims=True) + EPSILON)
    return centred * inverse, inverse


def received_shape(part, step):
    _, _, rows, order = part
    before = order[:step]
    y_done = sum(letter in "AB" for letter in before)
    z_done = any(letter in "ab" for letter in before)
    if order[step] in "AB":
        return (2 if y_done == 0 else 1, 1 if z_done else 2, rows, 128)
    return ((4, 2, 1)[y_done], 1, rows, 128)


def kernel(whole, *refs):
    (counts, lengths, positions, audio, cotangent, w_qkv, w_out, w_proj) = refs[:8]
    embeds, grad_qkv, grad_out = refs[8:11]
    (
        wq, wo, wp, tmp, aud, cot_s, cot_r, gt_s, gt_r, t_s, t_r, ag_a, ad_a, e_s, e_r, cot_v, aud_v, emb,
        nb, nt, pj, q2s, qr_s, k_s, v_s, prob, attp_s, agt, mgp, dqk, dvs, grad, core_r, total, final,
        z_s, z_r, f_s, f_r, w_sem, x_send, x_recv, c_send, c_recv, r_send, r_recv, z_send, z_recv,
    ) = refs[11 : 11 + 48]
    r_bufs = refs[11 + 48 :]

    dp = lax.axis_index("dp")
    x = lax.axis_index("seq")
    y = dp // 16
    z = (dp // 2) % 8
    c = dp % 2
    par = z % 2
    zp = z // 2

    def at(yy, zz, cc):
        return (yy * 16 + zz * 2 + cc, x)

    peers = [(dp, (x + k) % 4) for k in (1, 2, 3)]
    partner = {
        "A": at(y ^ 1, z, c),
        "B": at(y ^ 3, z, c),
        "a": at(y, z ^ 1, c),
        "b": at(y, (z + 7 + 2 * par) % 8, c),
    }
    core_peer = at(y, z, 1 - c)
    z_peers = [at(y, z ^ (2 * k), c) for k in (1, 2, 3)]

    input_copies = [
        pltpu.make_async_copy(src, dst, w_sem.at[3 + i])
        for i, (src, dst) in enumerate(((cotangent, cot_v), (audio, aud_v)))
    ]
    weight_copies = [
        pltpu.make_async_copy(src, dst, w_sem.at[i])
        for i, (src, dst) in enumerate(((w_qkv, wq), (w_out, wo), (w_proj, wp)))
    ]
    for copy in input_copies:
        copy.start()

    barrier = pltpu.get_barrier_semaphore()
    everyone = peers + ([core_peer] + list(partner.values()) + z_peers if whole else [])
    for device in everyone:
        pl.semaphore_signal(barrier, inc=1, device_id=device, device_id_type=MESH)

    for i in (2, 0, 1):
        weight_copies[i].start()

    lane = lax.broadcasted_iota(jnp.int32, (112, 128), 1)
    low = lane < 64
    low_half = low[0:64]
    tmp[...] = jnp.zeros_like(tmp)
    pj[...] = jnp.zeros_like(pj)
    mgp[...] = jnp.zeros_like(mgp)
    input_copies[0].wait()
    cot_rows = cot_v[...].astype(F32)
    for t in range(4):
        cot_s[t] = fold(cot_rows[:, 896 * t : 896 * t + 896], 128, 8)
    cot_r[x] = cot_s[x]

    def pack_audio(b):
        tmp[b, 0:100, 0:320] = aud_v[b].astype(F32)
        first, second, third = (tmp[b, :, 128 * i : 128 * i + 128] for i in range(3))
        second_turned = pltpu.roll(second, 64, 1)
        packed = third[0:64] + pltpu.roll(third[64:128], 64, 1)
        packed_odd = jnp.where(low_half, first[0:64], pltpu.roll(first[64:128], 64, 1))
        even = jnp.concatenate([first[0:112], second[0:112], packed], axis=0)
        odd = jnp.concatenate(
            [
                jnp.where(low, pltpu.roll(first, 64, 1)[0:112], second_turned[0:112]),
                jnp.where(low, second_turned[0:112], pltpu.roll(third, 64, 1)[0:112]),
                packed_odd,
            ],
            axis=0,
        )
        aud[x, b] = jnp.where(x % 2 == 0, even, odd).astype(BF16)

    input_copies[1].wait()
    pack_audio(0)

    pl.semaphore_wait(barrier, len(everyone))

    started = []
    def to_peers(slot, source, target):
        copies = []
        for k in (1, 2, 3):
            there = (x + k) % 4
            copy = pltpu.make_async_remote_copy(
                src_ref=source(there),
                dst_ref=target(k),
                send_sem=x_send.at[slot, k - 1],
                recv_sem=x_recv.at[slot, k - 1],
                device_id=(dp, there),
                device_id_type=MESH,
            )
            copy.start()
            copies.append(copy)
        started.extend(copies)
        return copies

    def arrive(copies):
        for copy in copies:
            copy.wait_recv()

    audio_copies = []
    cot_copies = to_peers(3, lambda there: cot_s.at[there], lambda k: cot_r.at[x])
    for b in range(3):
        if b > 0:
            pack_audio(b)
        block = aud.at[x, b]
        audio_copies.append(to_peers(b, lambda there: block, lambda k: block))

    pos_pad = jnp.concatenate([positions[...].astype(F32), jnp.zeros((13, 50), F32)], axis=0).astype(BF16)
    frame_row = lax.broadcasted_iota(jnp.int32, (50, 112), 0)
    frame_col = lax.broadcasted_iota(jnp.int32, (50, 112), 1)
    spread = jnp.where(frame_row == frame_col // 2, 1.0, 0.0).astype(BF16)
    pos_lanes = dot(pos_pad, spread)
    frame_row_t = lax.broadcasted_iota(jnp.int32, (112, 50), 0)
    frame_col_t = lax.broadcasted_iota(jnp.int32, (112, 50), 1)
    spread_t = jnp.where(frame_row_t // 2 == frame_col_t, 1.0, 0.0).astype(BF16)
    pos_sub = dot_nt(spread_t, pos_pad)
    lives = [jnp.where(b < counts[0], lengths[b], 0) for b in range(3)]

    def place(b, first, count):
        row = lax.broadcasted_iota(jnp.int32, (count, 112), 0) + first
        frame = lax.broadcasted_iota(jnp.int32, (count, 112), 1)
        hit = (row.astype(F32) == pos_lanes[b : b + 1, :]) & (frame < lives[b])
        return jnp.where(hit, 1.0, 0.0).astype(BF16)

    def unplace(b):
        frame = lax.broadcasted_iota(jnp.int32, (112, 160), 0)
        row = lax.broadcasted_iota(jnp.int32, (112, 160), 1)
        hit = (row.astype(F32) == pos_sub[:, b : b + 1]) & (frame < lives[b])
        return jnp.where(hit, 1.0, 0.0).astype(BF16)

    def split_heads(tile):
        return jnp.concatenate([jnp.where(low, tile, 0.0), jnp.where(low, 0.0, tile)], axis=0).astype(BF16)

    weight_copies[0].wait()

    attp = [jnp.zeros((160, 128), F32) for _ in range(3)]
    pooled_audio = jnp.zeros((40, 1280), F32)

    def forward(b, attp, pooled_audio):
        arrive(audio_copies[b])
        tiles = []
        for s in (0, 2):
            left = aud[s, b, 224:288].astype(F32)
            right = aud[s + 1, b, 224:288].astype(F32)
            top = jnp.where(low_half, left, pltpu.roll(right, 64, 1))
            bottom = jnp.where(low_half, pltpu.roll(left, 64, 1), right)
            tiles.append(aud[s, b, 0:112].astype(F32))
            tiles.append(aud[s, b, 112:224].astype(F32))
            tiles.append(jnp.concatenate([top, bottom[0:48]], axis=0))
            tiles.append(aud[s + 1, b, 0:112].astype(F32))
            tiles.append(aud[s + 1, b, 112:224].astype(F32))
        frames = jnp.concatenate(tiles, axis=1)
        pooled_audio = pooled_audio + dot(place(b, 40 * x, 40), frames.astype(BF16))
        normed = normalize(frames)[0].astype(BF16)
        nb[112 * b : 112 * b + 112, :] = normed
        for j in range(3):
            pj[j, :, 0:320] = dot_nt(normed, wq[j])
        k_s[b] = pj[1].astype(BF16)
        v_s[b] = pj[2].astype(BF16)
        key_limit = jnp.maximum(lives[b], 1)
        placed = place(b, 0, 160)
        for g in range(3):
            cols = slice(128 * g, 128 * g + 128)
            q_tile = pj[0, :, cols]
            if g < 2:
                queries = split_heads(q_tile)
                q2s[b, g] = queries
            else:
                queries = q_tile.astype(BF16)
                qr_s[b] = queries
            rows = queries.shape[0]
            scores = dot_nt(queries, k_s[b, :, cols]) * SCALING
            key = lax.broadcasted_iota(jnp.int32, (rows, 112), 1)
            scores = jnp.where(key < key_limit, scores, -1e30)
            powered = jnp.exp(scores - jnp.max(scores, axis=-1, keepdims=True))
            weights = powered * (1.0 / jnp.sum(powered, axis=-1, keepdims=True))
            prob[b, g, 0:rows] = weights
            mixed = dot(weights.astype(BF16), v_s[b, :, cols])
            if g < 2:
                mixed = jnp.where(low, mixed[0:112], mixed[112:224])
            attp[g] = attp[g] + dot(placed, mixed.astype(BF16))
        return attp, pooled_audio

    attp, pooled_audio = forward(0, attp, pooled_audio)

    weight_copies[2].wait()
    arrive(cot_copies)
    row_grads = jnp.concatenate([unfold(cot_r[s], 7) for s in range(4)], axis=0).astype(BF16)
    adapter_terms = dot_nt(row_grads, wp[...])
    for t in range(4):
        gt_s[t] = fold(adapter_terms[40 * t : 40 * t + 40], 640, 0)
    attp, pooled_audio = forward(1, attp, pooled_audio)
    gt_copies = to_peers(4, lambda there: gt_s.at[there], lambda k: gt_r.at[k - 1])

    attp, pooled_audio = forward(2, attp, pooled_audio)
    for g in range(3):
        attp_s[g] = attp[g].astype(BF16)
    weight_copies[1].wait()
    head_terms = (
        dot(attp_s[0], wo[0:128]) + dot(attp_s[1], wo[128:256]) + dot(attp_s[2][:, 0:64], wo[256:320])
    )
    for t in range(4):
        t_s[t] = fold(head_terms[40 * t : 40 * t + 40], 640, 0)
    t_copies = to_peers(5, lambda there: t_s.at[there], lambda k: t_r.at[k - 1])

    nt[...] = nb[...].T

    arrive(gt_copies)
    adapted_grad = gt_s[x].astype(F32)
    for k in range(3):
        adapted_grad = adapted_grad + gt_r[k].astype(F32)
    adapted_grad = unfold(adapted_grad.astype(BF16), 2)

    arrive(t_copies)
    attention = t_s[x].astype(F32)
    for k in range(3):
        attention = attention + t_r[k].astype(F32)
    attention = jnp.concatenate([attention[0:40], attention[40:80]], axis=1)
    normed_rows, inverse = normalize((pooled_audio + attention) * 0.5)
    pooled_grad = inverse * (
        adapted_grad
        - jnp.mean(adapted_grad, axis=-1, keepdims=True)
        - normed_rows * jnp.mean(adapted_grad * normed_rows, axis=-1, keepdims=True)
    )
    ag_a[x] = fold(pooled_grad * 0.5, 640, 0)
    ag_copies = to_peers(6, lambda there: ag_a.at[x], lambda k: ag_a.at[x])
    ad_a[x] = fold(normed_rows, 640, 0)
    ad_copies = to_peers(7, lambda there: ad_a.at[x], lambda k: ad_a.at[x])

    arrive(ag_copies)
    attention_grad = jnp.concatenate([unfold(ag_a[s], 2) for s in range(4)], axis=0).astype(BF16)
    agt[...] = attention_grad.T
    mgp[:, 0:320] = dot_nt(attention_grad, wo[...]).astype(BF16)

    for b in range(3):
        rows = slice(112 * b, 112 * b + 112)
        mixed_grad = dot(unplace(b), mgp[...])
        for g in range(3):
            cols = slice(128 * g, 128 * g + 128)
            tile = mixed_grad[:, cols]
            if g < 2:
                grads, queries, count = split_heads(tile), q2s[b, g], 224
            else:
                grads, queries, count = tile.astype(BF16), qr_s[b], 112
            weights = prob[b, g, 0:count]
            prob_grad = dot_nt(grads, v_s[b, :, cols])
            inner = jnp.sum(weights * prob_grad, axis=-1, keepdims=True)
            score_half = (weights * (prob_grad - inner)).astype(BF16)
            query_grad = dot(score_half, k_s[b, :, cols])
            if g < 2:
                query_grad = jnp.where(low, query_grad[0:112], query_grad[112:224])
            query_grad = query_grad * SCALING
            key_grad = dot_tn(score_half, queries) * SCALING
            value_grad = dot_tn(weights.astype(BF16), grads)
            dvs[rows, cols] = value_grad.astype(BF16)
            if g < 2:
                dqk[rows, cols] = query_grad.astype(BF16)
                dqk[rows, 256 + 128 * g : 384 + 128 * g] = key_grad.astype(BF16)
            else:
                dqk[rows, 512:640] = (query_grad + pltpu.roll(key_grad, 64, 1)).astype(BF16)

    attp_turned = pltpu.roll(attp_s[2].astype(F32), 64, 1).astype(BF16)
    core_copies = []
    for yy in range(4):
        features = nt[320 * yy : 320 * yy + 320, :]
        backs = agt[320 * yy : 320 * yy + 320, :]
        first = dot(features, dqk[...])
        value_part = dot(features, dvs[...])
        out_part = [dot(backs, attp_s[0]), dot(backs, attp_s[1]), dot(backs, attp_turned)]
        halves = (
            [first[:, 128 * t : 128 * t + 128] for t in range(5)],
            [value_part[:, 0:128], value_part[:, 128:256], out_part[0], out_part[1], value_part[:, 256:384] + out_part[2]],
        )
        for half in range(2):
            for t in range(5):
                for side in range(2):
                    grad[half, yy, t, side] = jnp.concatenate(
                        [halves[half][t][40 * i : 40 * i + 40] for i in range(side, 8, 2)], axis=0
                    ).astype(BF16)
        if whole:
            copy = pltpu.make_async_remote_copy(
                src_ref=grad.at[1 - c, yy],
                dst_ref=core_r.at[yy],
                send_sem=c_send.at[yy],
                recv_sem=c_recv.at[yy],
                device_id=core_peer,
                device_id_type=MESH,
            )
            copy.start()
            core_copies.append(copy)
    started.extend(core_copies)

    def start_embeds():
        arrive(ad_copies)
        adapted = jnp.concatenate([unfold(ad_a[s], 2) for s in range(4)], axis=0).astype(BF16)
        adapter_rows = dot(adapted, wp[...])
        for t in range(4):
            e_s[t] = fold(adapter_rows[40 * t : 40 * t + 40], 128, 8)
        e_r[x] = e_s[x]
        return to_peers(8, lambda there: e_s.at[there], lambda k: e_r.at[x])

    def finish_embeds(copies):
        arrive(copies)
        for s in range(4):
            emb[:, 896 * s : 896 * s + 896] = unfold(e_r[s], 7).astype(BF16)
        copy = pltpu.make_async_copy(emb, embeds, w_sem.at[5])
        copy.start()
        return copy

    if not whole:
        finish_embeds(start_embeds()).wait()
        grad_qkv[...] = grad[...].astype(F32)
        grad_out[...] = jnp.zeros_like(grad_out)
        for copy in started:
            copy.wait_send()
        return

    for yy in range(4):
        core_copies[yy].wait_recv()
        total[yy] = (grad[c, yy].astype(F32) + core_r[yy].astype(F32)).astype(BF16)

    def blocks(order, step):
        y_before = [letter for letter in order[:step] if letter in "AB"]
        z_done = any(letter in "ab" for letter in order[:step])
        letter = order[step]
        if letter in "AB":
            near = y ^ (1 if letter == "A" else 3)
            other = y ^ (3 if letter == "A" else 1)
            sides = (par, par) if z_done else (None, None)
            if y_before:
                return [near], [y], sides
            return [near, y ^ 2], [y, other], sides
        held = [0, 1, 2, 3]
        if len(y_before) == 1:
            held = [y, y ^ (3 if y_before[0] == "A" else 1)]
        elif len(y_before) == 2:
            held = [y]
        return held, held, (1 - par, par)

    def begin(p, step):
        tile, row, count, order = PARTS[p]
        send, _, (side, _) = blocks(order, step)
        landing = r_bufs[3 * p + step]
        copies = []
        for i, block in enumerate(send):
            pick = pl.ds(0, 2) if side is None else pl.ds(side, 1)
            copy = pltpu.make_async_remote_copy(
                src_ref=total.at[block, tile, pick, pl.ds(row, count)],
                dst_ref=landing.at[i],
                send_sem=r_send.at[p, step, i],
                recv_sem=r_recv.at[p, step, i],
                device_id=partner[order[step]],
                device_id_type=MESH,
            )
            copy.start()
            copies.append(copy)
        started.extend(copies)
        return copies

    def end(p, step, copies):
        tile, row, count, order = PARTS[p]
        _, keep, (_, side) = blocks(order, step)
        landing = r_bufs[3 * p + step]
        rows = pl.ds(row, count)
        arrive(copies)
        for i, block in enumerate(keep):
            if step == 2:
                final[tile, rows] = total[block, tile, par, rows].astype(F32) + landing[i, 0].astype(F32)
            elif side is None:
                for k in range(2):
                    kept = total[block, tile, k, rows].astype(F32) + landing[i, k].astype(F32)
                    total[block, tile, k, rows] = kept.astype(BF16)
            else:
                kept = total[block, tile, side, rows].astype(F32) + landing[i, 0].astype(F32)
                total[block, tile, side, rows] = kept.astype(BF16)

    flying = [begin(p, 0) for p in range(len(PARTS))]
    embed_copies = start_embeds()
    for p in range(len(PARTS)):
        end(p, 0, flying[p])
        flying[p] = begin(p, 1)
    for p in range(len(PARTS)):
        end(p, 1, flying[p])
        flying[p] = begin(p, 2)
    for p in range(len(PARTS)):
        end(p, 2, flying[p])

    for j in range(4):
        z_s[j] = jnp.concatenate(
            [final[t, 40 * j : 40 * j + 40] for t in range(5)] + [jnp.zeros((8, 128), F32)], axis=0
        ).astype(BF16)
    z_copies = []
    for k in (1, 2, 3):
        copy = pltpu.make_async_remote_copy(
            src_ref=z_s.at[zp ^ k],
            dst_ref=z_r.at[k - 1],
            send_sem=z_send.at[k - 1],
            recv_sem=z_recv.at[k - 1],
            device_id=z_peers[k - 1],
            device_id_type=MESH,
        )
        copy.start()
        z_copies.append(copy)
    started.extend(z_copies)
    embeds_copy = finish_embeds(embed_copies)
    arrive(z_copies)
    mine = z_s[zp].astype(F32)
    for k in range(3):
        mine = mine + z_r[k].astype(F32)
    first_core = c == 0
    own_tiles = []
    f_s[...] = jnp.zeros_like(f_s)
    for t in range(5):
        rows = mine[40 * t : 40 * t + 40]
        early, late = rows[0:20], rows[20:40]
        own_tiles.append(jnp.where(first_core, early, late))
        f_s[t, 0:20] = jnp.where(first_core, late, early).astype(BF16)
    copy = pltpu.make_async_remote_copy(
        src_ref=f_s,
        dst_ref=f_r,
        send_sem=c_send.at[4],
        recv_sem=c_recv.at[4],
        device_id=core_peer,
        device_id_type=MESH,
    )
    copy.start()
    started.append(copy)
    arrive([copy])
    for t in range(5):
        got = f_r[t, 0:20].astype(F32)
        left = jnp.where(first_core, own_tiles[t], got)
        right = jnp.where(first_core, got, own_tiles[t])
        if t < 2:
            cols = slice(128 * t, 128 * t + 128)
            grad_qkv[0, :, cols] = left
            grad_qkv[2, :, cols] = right
        elif t < 4:
            cols = slice(128 * t - 256, 128 * t - 128)
            grad_qkv[1, :, cols] = left
            grad_out[:, cols] = right
        else:
            grad_qkv[0, :, 256:320] = left[:, 0:64]
            grad_qkv[1, :, 256:320] = left[:, 64:128]
            grad_qkv[2, :, 256:320] = right[:, 0:64]
            grad_out[:, 256:320] = right[:, 64:128]
    embeds_copy.wait()
    for copy in started:
        copy.wait_send()


def call(whole, counts, lengths, positions, audio, cotangent, w_qkv, w_out, w_proj):
    vmem, dma = pltpu.VMEM, pltpu.SemaphoreType.DMA
    scratch = [
        vmem((3, 320, 1280), BF16),
        vmem((320, 1280), BF16),
        vmem((1280, 896), BF16),
        vmem((3, 128, 384), F32),
        vmem((4, 3, 288, 128), BF16),
        vmem((4, 288, 128), BF16),
        vmem((4, 288, 128), BF16),
        vmem((4, 80, 640), BF16),
        vmem((3, 80, 640), BF16),
        vmem((4, 80, 640), BF16),
        vmem((3, 80, 640), BF16),
        vmem((4, 80, 640), BF16),
        vmem((4, 80, 640), BF16),
        vmem((4, 288, 128), BF16),
        vmem((4, 288, 128), BF16),
        vmem((40, 3584), BF16),
        vmem((3, 100, 320), BF16),
        vmem((40, 3584), BF16),
        vmem((336, 1280), BF16),
        vmem((1280, 336), BF16),
        vmem((3, 112, 384), F32),
        vmem((3, 2, 224, 128), BF16),
        vmem((3, 112, 128), BF16),
        vmem((3, 112, 384), BF16),
        vmem((3, 112, 384), BF16),
        vmem((3, 3, 224, 112), F32),
        vmem((3, 160, 128), BF16),
        vmem((1280, 160), BF16),
        vmem((160, 384), BF16),
        vmem((336, 640), BF16),
        vmem((336, 384), BF16),
        vmem((2, 4, 5, 2, 160, 128), BF16),
        vmem((4, 5, 2, 160, 128), BF16),
        vmem((4, 5, 2, 160, 128), BF16),
        vmem((5, 160, 128), F32),
        vmem((4, 208, 128), BF16),
        vmem((3, 208, 128), BF16),
        vmem((5, 32, 128), BF16),
        vmem((5, 32, 128), BF16),
        dma((6,)),
        dma((9, 3)),
        dma((9, 3)),
        dma((5,)),
        dma((5,)),
        dma((6, 3, 4)),
        dma((6, 3, 4)),
        dma((3,)),
        dma((3,)),
    ]
    assert len(scratch) == 48
    scratch += [vmem(received_shape(part, step), BF16) for part in PARTS for step in range(3)]
    in_vmem = pl.BlockSpec(memory_space=pltpu.VMEM)
    in_smem = pl.BlockSpec(memory_space=pltpu.SMEM)
    anywhere = pl.BlockSpec(memory_space=pl.ANY)
    gq = (3, 20, 320) if whole else (2, 4, 5, 2, 160, 128)
    return pl.pallas_call(
        functools.partial(kernel, whole),
        out_shape=(
            jax.ShapeDtypeStruct((40, 3584), BF16),
            jax.ShapeDtypeStruct(gq, F32),
            jax.ShapeDtypeStruct((20, 320), F32),
        ),
        in_specs=[in_smem, in_smem, in_vmem] + [anywhere] * 5,
        out_specs=(anywhere, in_vmem, in_vmem),
        scratch_shapes=scratch,
        compiler_params=pltpu.CompilerParams(
            collective_id=0, has_side_effects=True, vmem_limit_bytes=60 * 2**20
        ),
        name="sublayer",
    )(counts, lengths, positions, audio, cotangent, w_qkv, w_out, w_proj)


def write_out(*refs):
    sources, targets, sems = refs[:3], refs[3:6], refs[6]
    copies = [pltpu.make_async_copy(sources[i], targets[i], sems.at[i]) for i in range(3)]
    for copy in copies:
        copy.start()
    for copy in copies:
        copy.wait()


def results(*parts):
    anywhere = pl.BlockSpec(memory_space=pl.ANY)
    return pl.pallas_call(
        write_out,
        out_shape=tuple(jax.ShapeDtypeStruct(part.shape, part.dtype) for part in parts),
        in_specs=[anywhere] * 3,
        out_specs=(anywhere,) * 3,
        scratch_shapes=[pltpu.SemaphoreType.DMA((3,))],
        name="results",
    )(*parts)


def shards(audio, counts, lengths, positions, w_qkv, w_out, w_proj, cotangent):
    embeds, grad_qkv, grad_out = call(
        True, counts, lengths, positions, audio, cotangent, jnp.swapaxes(w_qkv, 1, 2), w_out, w_proj
    )
    embeds, grad_qkv, grad_out = results(embeds, grad_qkv, grad_out)
    return embeds, grad_qkv, grad_out.T


def solution(mesh):
    in_specs = (
        P("dp", None, "seq"),
        P("dp"),
        P("dp"),
        P("dp", None),
        P(None, None, "seq"),
        P("seq", None),
        P(None, "seq"),
        P(("dp", "seq"), None),
    )
    out_specs = (P(("dp", "seq"), None), P(None, "dp", "seq"), P("seq", "dp"))
    return jax.shard_map(shards, mesh=mesh, in_specs=in_specs, out_specs=out_specs, check_vma=False)
```

```python
import jax
import jax.numpy as jnp
from jax import lax
from jax.experimental import pallas as pl
from jax.experimental.pallas import tpu as pltpu
from jax.sharding import PartitionSpec as P

MESH = pl.DeviceIdType.MESH
F32 = jnp.float32
BF16 = jnp.bfloat16
EPSILON = 1e-05
SCALING = 0.125
PARTS = (
    (0, 0, 160, "ABa"),
    (1, 0, 160, "BAb"),
    (2, 0, 160, "aAB"),
    (3, 0, 160, "bBA"),
    (4, 0, 80, "ABa"),
    (4, 80, 80, "BAb"),
)


TURNS = (2, 3, 0, 1, 4, 5)
Z_GROUPS = (((0, 1), 0, 80), ((2, 3), 80, 80), ((4,), 160, 48))


def dot(a, b):
    return jnp.dot(a, b, preferred_element_type=F32)


def dot_nt(a, b):
    return lax.dot_general(a, b, (((1,), (1,)), ((), ())), preferred_element_type=F32)


def dot_tn(a, b):
    return lax.dot_general(a, b, (((0,), (0,)), ((), ())), preferred_element_type=F32)


def fold(rows, width, extra):
    pieces = [rows[:, i : i + width] for i in range(0, rows.shape[1], width)]
    if extra:
        pieces.append(jnp.zeros((extra, width), F32))
    return jnp.concatenate(pieces, axis=0).astype(BF16)


def unfold(folded, count):
    wide = folded.astype(F32)
    return jnp.concatenate([wide[40 * i : 40 * i + 40] for i in range(count)], axis=1)


def normalize(rows):
    centred = rows - jnp.mean(rows, axis=-1, keepdims=True)
    inverse = lax.rsqrt(jnp.mean(centred * centred, axis=-1, keepdims=True) + EPSILON)
    return centred * inverse, inverse


def received_shape(part, step):
    _, _, rows, order = part
    before = order[:step]
    y_done = sum(letter in "AB" for letter in before)
    z_done = any(letter in "ab" for letter in before)
    if order[step] in "AB":
        return (2 if y_done == 0 else 1, 1 if z_done else 2, rows, 128)
    return ((4, 2, 1)[y_done], 1, rows, 128)


def kernel(*refs):
    (counts, lengths, positions, audio, cotangent, w_qkv, w_out, w_proj) = refs[:8]
    embeds, grad_qkv, grad_out = refs[8:11]
    (
        wq, wo, wp, tmp, aud, cot_s, cot_r, gt_s, gt_r, t_s, t_r, ag_a, ad_a, e_s, e_r, cot_v, aud_v, emb,
        nb, nt, pj, q2s, qr_s, k_s, v_s, prob, attp_s, agt, mgp, local, other, total, final,
        z_s, z_r, f_s, f_r, w_sem, x_send, x_recv, c_send, c_recv, r_send, r_recv, z_send, z_recv,
    ) = refs[11 : 11 + 46]
    r_bufs = refs[11 + 46 :]

    dp = lax.axis_index("dp")
    x = lax.axis_index("seq")
    y = dp // 16
    z = (dp // 2) % 8
    c = dp % 2
    par = z % 2
    zp = z // 2

    def at(yy, zz, cc):
        return (yy * 16 + zz * 2 + cc, x)

    peers = [(dp, (x + k) % 4) for k in (1, 2, 3)]
    partner = {
        "A": at(y ^ 1, z, c),
        "B": at(y ^ 3, z, c),
        "a": at(y, z ^ 1, c),
        "b": at(y, (z + 7 + 2 * par) % 8, c),
    }
    core_peer = at(y, z, 1 - c)
    z_peers = [at(y, z ^ (2 * k), c) for k in (1, 2, 3)]

    input_copies = [
        pltpu.make_async_copy(src, dst, w_sem.at[3 + i])
        for i, (src, dst) in enumerate(((cotangent, cot_v), (audio, aud_v)))
    ]
    weight_copies = [
        pltpu.make_async_copy(src, dst, w_sem.at[i])
        for i, (src, dst) in enumerate(((w_qkv, wq), (w_out, wo), (w_proj, wp)))
    ]
    for copy in input_copies:
        copy.start()

    barrier = pltpu.get_barrier_semaphore()
    everyone = peers + [core_peer] + list(partner.values()) + z_peers
    for device in everyone:
        pl.semaphore_signal(barrier, inc=1, device_id=device, device_id_type=MESH)

    for i in (2, 0, 1):
        weight_copies[i].start()

    lane = lax.broadcasted_iota(jnp.int32, (112, 128), 1)
    low = lane < 64
    low_half = low[0:64]
    tmp[...] = jnp.zeros_like(tmp)
    pj[...] = jnp.zeros_like(pj)
    mgp[...] = jnp.zeros_like(mgp)
    local[1, :, 384:640] = jnp.zeros((336, 256), BF16)
    input_copies[0].wait()
    cot_rows = cot_v[...].astype(F32)
    for t in range(4):
        cot_s[t] = fold(cot_rows[:, 896 * t : 896 * t + 896], 128, 8)
    cot_r[x] = cot_s[x]

    def pack_audio(b):
        tmp[b, 0:100, 0:320] = aud_v[b].astype(F32)
        first, second, third = (tmp[b, :, 128 * i : 128 * i + 128] for i in range(3))
        second_turned = pltpu.roll(second, 64, 1)
        packed = third[0:64] + pltpu.roll(third[64:128], 64, 1)
        packed_odd = jnp.where(low_half, first[0:64], pltpu.roll(first[64:128], 64, 1))
        even = jnp.concatenate([first[0:112], second[0:112], packed], axis=0)
        odd = jnp.concatenate(
            [
                jnp.where(low, pltpu.roll(first, 64, 1)[0:112], second_turned[0:112]),
                jnp.where(low, second_turned[0:112], pltpu.roll(third, 64, 1)[0:112]),
                packed_odd,
            ],
            axis=0,
        )
        aud[x, b] = jnp.where(x % 2 == 0, even, odd).astype(BF16)

    input_copies[1].wait()
    pack_audio(0)

    pl.semaphore_wait(barrier, len(everyone))

    started = []
    def to_peers(slot, source, target):
        copies = []
        for k in (1, 2, 3):
            there = (x + k) % 4
            copy = pltpu.make_async_remote_copy(
                src_ref=source(there),
                dst_ref=target(k),
                send_sem=x_send.at[slot, k - 1],
                recv_sem=x_recv.at[slot, k - 1],
                device_id=(dp, there),
                device_id_type=MESH,
            )
            copy.start()
            copies.append(copy)
        started.extend(copies)
        return copies

    def to_core(slot, source, target):
        copy = pltpu.make_async_remote_copy(
            src_ref=source,
            dst_ref=target,
            send_sem=c_send.at[slot],
            recv_sem=c_recv.at[slot],
            device_id=core_peer,
            device_id_type=MESH,
        )
        copy.start()
        started.append(copy)
        return copy

    def arrive(copies):
        for copy in copies:
            copy.wait_recv()

    audio_copies = []
    cot_copies = to_peers(3, lambda there: cot_s.at[there], lambda k: cot_r.at[x])
    for b in range(3):
        if b > 0:
            pack_audio(b)
        block = aud.at[x, b]
        audio_copies.append(to_peers(b, lambda there: block, lambda k: block))

    pos_pad = jnp.concatenate([positions[...].astype(F32), jnp.zeros((13, 50), F32)], axis=0).astype(BF16)
    frame_row = lax.broadcasted_iota(jnp.int32, (50, 112), 0)
    frame_col = lax.broadcasted_iota(jnp.int32, (50, 112), 1)
    spread = jnp.where(frame_row == frame_col // 2, 1.0, 0.0).astype(BF16)
    pos_lanes = dot(pos_pad, spread)
    frame_row_t = lax.broadcasted_iota(jnp.int32, (112, 50), 0)
    frame_col_t = lax.broadcasted_iota(jnp.int32, (112, 50), 1)
    spread_t = jnp.where(frame_row_t // 2 == frame_col_t, 1.0, 0.0).astype(BF16)
    pos_sub = dot_nt(spread_t, pos_pad)
    lives = [jnp.where(b < counts[0], lengths[b], 0) for b in range(3)]

    def place(b, first, count):
        row = lax.broadcasted_iota(jnp.int32, (count, 112), 0) + first
        frame = lax.broadcasted_iota(jnp.int32, (count, 112), 1)
        hit = (row.astype(F32) == pos_lanes[b : b + 1, :]) & (frame < lives[b])
        return jnp.where(hit, 1.0, 0.0).astype(BF16)

    def unplace(b):
        frame = lax.broadcasted_iota(jnp.int32, (112, 160), 0)
        row = lax.broadcasted_iota(jnp.int32, (112, 160), 1)
        hit = (row.astype(F32) == pos_sub[:, b : b + 1]) & (frame < lives[b])
        return jnp.where(hit, 1.0, 0.0).astype(BF16)

    def split_heads(tile):
        return jnp.concatenate([jnp.where(low, tile, 0.0), jnp.where(low, 0.0, tile)], axis=0).astype(BF16)

    weight_copies[0].wait()

    attp = [jnp.zeros((160, 128), F32) for _ in range(3)]
    pooled_audio = jnp.zeros((40, 1280), F32)

    def forward(b, attp, pooled_audio):
        arrive(audio_copies[b])
        tiles = []
        for s in (0, 2):
            left = aud[s, b, 224:288].astype(F32)
            right = aud[s + 1, b, 224:288].astype(F32)
            top = jnp.where(low_half, left, pltpu.roll(right, 64, 1))
            bottom = jnp.where(low_half, pltpu.roll(left, 64, 1), right)
            tiles.append(aud[s, b, 0:112].astype(F32))
            tiles.append(aud[s, b, 112:224].astype(F32))
            tiles.append(jnp.concatenate([top, bottom[0:48]], axis=0))
            tiles.append(aud[s + 1, b, 0:112].astype(F32))
            tiles.append(aud[s + 1, b, 112:224].astype(F32))
        frames = jnp.concatenate(tiles, axis=1)
        pooled_audio = pooled_audio + dot(place(b, 40 * x, 40), frames.astype(BF16))
        normed = normalize(frames)[0].astype(BF16)
        nb[112 * b : 112 * b + 112, :] = normed
        for j in range(3):
            pj[j, :, 0:320] = dot_nt(normed, wq[j])
        k_s[b] = pj[1].astype(BF16)
        v_s[b] = pj[2].astype(BF16)
        key_limit = jnp.maximum(lives[b], 1)
        placed = place(b, 0, 160)
        for g in range(3):
            cols = slice(128 * g, 128 * g + 128)
            q_tile = pj[0, :, cols]
            if g < 2:
                queries = split_heads(q_tile)
                q2s[b, g] = queries
            else:
                queries = q_tile.astype(BF16)
                qr_s[b] = queries
            rows = queries.shape[0]
            scores = dot_nt(queries, k_s[b, :, cols]) * SCALING
            key = lax.broadcasted_iota(jnp.int32, (rows, 112), 1)
            scores = jnp.where(key < key_limit, scores, -1e30)
            powered = jnp.exp(scores - jnp.max(scores, axis=-1, keepdims=True))
            weights = powered * (1.0 / jnp.sum(powered, axis=-1, keepdims=True))
            prob[b, g, 0:rows] = weights
            mixed = dot(weights.astype(BF16), v_s[b, :, cols])
            if g < 2:
                mixed = jnp.where(low, mixed[0:112], mixed[112:224])
            attp[g] = attp[g] + dot(placed, mixed.astype(BF16))
        return attp, pooled_audio

    attp, pooled_audio = forward(0, attp, pooled_audio)

    weight_copies[2].wait()
    arrive(cot_copies)
    row_grads = jnp.concatenate([unfold(cot_r[s], 7) for s in range(4)], axis=0).astype(BF16)
    adapter_terms = dot_nt(row_grads, wp[...])
    for t in range(4):
        gt_s[t] = fold(adapter_terms[40 * t : 40 * t + 40], 640, 0)
    attp, pooled_audio = forward(1, attp, pooled_audio)
    gt_copies = to_peers(4, lambda there: gt_s.at[there], lambda k: gt_r.at[k - 1])

    attp, pooled_audio = forward(2, attp, pooled_audio)
    attp = [part.astype(BF16) for part in attp]
    for g in range(2):
        attp_s[c, :, 128 * g : 128 * g + 128] = attp[g]
    attp_s[c, :, 256:384] = pltpu.roll(attp[2].astype(F32), 64, 1).astype(BF16)
    weight_copies[1].wait()
    head_terms = (
        dot(attp[0], wo[0:128]) + dot(attp[1], wo[128:256]) + dot(attp[2][:, 0:64], wo[256:320])
    )
    for t in range(4):
        t_s[t] = fold(head_terms[40 * t : 40 * t + 40], 640, 0)
    t_copies = to_peers(5, lambda there: t_s.at[there], lambda k: t_r.at[k - 1])

    nt[c] = nb[...].T
    core_copies = [to_core(0, nt.at[c], nt.at[c]), to_core(1, attp_s.at[c], attp_s.at[c])]

    arrive(gt_copies)
    adapted_grad = gt_s[x].astype(F32)
    for k in range(3):
        adapted_grad = adapted_grad + gt_r[k].astype(F32)
    adapted_grad = unfold(adapted_grad.astype(BF16), 2)

    arrive(t_copies)
    attention = t_s[x].astype(F32)
    for k in range(3):
        attention = attention + t_r[k].astype(F32)
    attention = jnp.concatenate([attention[0:40], attention[40:80]], axis=1)
    normed_rows, inverse = normalize((pooled_audio + attention) * 0.5)
    pooled_grad = inverse * (
        adapted_grad
        - jnp.mean(adapted_grad, axis=-1, keepdims=True)
        - normed_rows * jnp.mean(adapted_grad * normed_rows, axis=-1, keepdims=True)
    )
    ag_a[x] = fold(pooled_grad * 0.5, 640, 0)
    ag_copies = to_peers(6, lambda there: ag_a.at[x], lambda k: ag_a.at[x])
    ad_a[x] = fold(normed_rows, 640, 0)
    arrive(ag_copies)
    ad_copies = to_peers(7, lambda there: ad_a.at[x], lambda k: ad_a.at[x])
    attention_grad = jnp.concatenate([unfold(ag_a[s], 2) for s in range(4)], axis=0).astype(BF16)
    agt[c] = attention_grad.T
    core_copies.append(to_core(2, agt.at[c], agt.at[c]))
    mgp[:, 0:320] = dot_nt(attention_grad, wo[...]).astype(BF16)

    for b in range(3):
        rows = slice(112 * b, 112 * b + 112)
        mixed_grad = dot(unplace(b), mgp[...])
        for g in range(3):
            cols = slice(128 * g, 128 * g + 128)
            tile = mixed_grad[:, cols]
            if g < 2:
                grads, queries, count = split_heads(tile), q2s[b, g], 224
            else:
                grads, queries, count = tile.astype(BF16), qr_s[b], 112
            weights = prob[b, g, 0:count]
            prob_grad = dot_nt(grads, v_s[b, :, cols])
            inner = jnp.sum(weights * prob_grad, axis=-1, keepdims=True)
            score_half = (weights * (prob_grad - inner)).astype(BF16)
            query_grad = dot(score_half, k_s[b, :, cols])
            if g < 2:
                query_grad = jnp.where(low, query_grad[0:112], query_grad[112:224])
            query_grad = query_grad * SCALING
            key_grad = dot_tn(score_half, queries) * SCALING
            value_grad = dot_tn(weights.astype(BF16), grads)
            local[1, rows, cols] = value_grad.astype(BF16)
            if g < 2:
                local[0, rows, cols] = query_grad.astype(BF16)
                local[0, rows, 256 + 128 * g : 384 + 128 * g] = key_grad.astype(BF16)
            else:
                local[0, rows, 512:640] = (query_grad + pltpu.roll(key_grad, 64, 1)).astype(BF16)
        block = pl.ds(112 * b, 112)
        core_copies.append(to_core(3 + b, local.at[1 - c, block], other.at[block]))

    def start_embeds():
        arrive(ad_copies)
        adapted = jnp.concatenate([unfold(ad_a[s], 2) for s in range(4)], axis=0).astype(BF16)
        adapter_rows = dot(adapted, wp[...])
        for t in range(4):
            e_s[t] = fold(adapter_rows[40 * t : 40 * t + 40], 128, 8)
        e_r[x] = e_s[x]
        return to_peers(8, lambda there: e_s.at[there], lambda k: e_r.at[x])

    def finish_embeds(copies):
        arrive(copies)
        for s in range(4):
            emb[:, 896 * s : 896 * s + 896] = unfold(e_r[s], 7).astype(BF16)
        copy = pltpu.make_async_copy(emb, embeds, w_sem.at[5])
        copy.start()
        return copy

    def blocks(order, step):
        y_before = [letter for letter in order[:step] if letter in "AB"]
        z_done = any(letter in "ab" for letter in order[:step])
        letter = order[step]
        if letter in "AB":
            near = y ^ (1 if letter == "A" else 3)
            beyond = y ^ (3 if letter == "A" else 1)
            sides = (par, par) if z_done else (None, None)
            if y_before:
                return [near], [y], sides
            return [y ^ 2, near], [beyond, y], sides
        held = [y ^ 2, y ^ 1, y ^ 3, y]
        if len(y_before) == 1:
            held = [y ^ (3 if y_before[0] == "A" else 1), y]
        elif len(y_before) == 2:
            held = [y]
        return held, held, (1 - par, par)

    def begin(p, step, only=None):
        tile, row, count, order = PARTS[p]
        send, _, (side, _) = blocks(order, step)
        landing = r_bufs[3 * p + step]
        copies = []
        for i, block in enumerate(send):
            if only is not None and i != only:
                continue
            pick = pl.ds(0, 2) if side is None else pl.ds(side, 1)
            copy = pltpu.make_async_remote_copy(
                src_ref=total.at[block, tile, pick, pl.ds(row, count)],
                dst_ref=landing.at[i],
                send_sem=r_send.at[p, step, i],
                recv_sem=r_recv.at[p, step, i],
                device_id=partner[order[step]],
                device_id_type=MESH,
            )
            copy.start()
            copies.append(copy)
        started.extend(copies)
        return copies

    def end(p, step, copies):
        tile, row, count, order = PARTS[p]
        _, keep, (_, side) = blocks(order, step)
        landing = r_bufs[3 * p + step]
        rows = pl.ds(row, count)
        arrive(copies)
        for i, block in enumerate(keep):
            if step == 2:
                final[tile, rows] = total[block, tile, par, rows].astype(F32) + landing[i, 0].astype(F32)
            elif side is None:
                for k in range(2):
                    kept = total[block, tile, k, rows].astype(F32) + landing[i, k].astype(F32)
                    total[block, tile, k, rows] = kept.astype(BF16)
            else:
                kept = total[block, tile, side, rows].astype(F32) + landing[i, 0].astype(F32)
                total[block, tile, side, rows] = kept.astype(BF16)

    arrive(core_copies)
    flying = {(p, 0): [] for p in range(len(PARTS))}
    turns = (y ^ 2, y ^ 1, y ^ 3, y)
    for turn, yy in enumerate(turns):
        rows = pl.ds(pl.multiple_of(320 * yy, 64), 320)

        def store(tile, values):
            for side in range(2):
                total[yy, tile, side] = jnp.concatenate(
                    [values[40 * i : 40 * i + 40] for i in range(side, 8, 2)], axis=0
                ).astype(BF16)

        @pl.when(c == 0)
        def _():
            part = dot(nt[0, rows], local[0]) + dot(nt[1, rows], other[...])
            for t in range(5):
                store(t, part[:, 128 * t : 128 * t + 128])

        @pl.when(c == 1)
        def _():
            value_part = dot(nt[1, rows], local[1, :, 0:384]) + dot(nt[0, rows], other[:, 0:384])
            out_part = dot(agt[0, rows], attp_s[0]) + dot(agt[1, rows], attp_s[1])
            store(0, value_part[:, 0:128])
            store(1, value_part[:, 128:256])
            store(2, out_part[:, 0:128])
            store(3, out_part[:, 128:256])
            store(4, value_part[:, 256:384] + out_part[:, 256:384])

        for p, part in enumerate(PARTS):
            slots = {"A": (0, 1, None, None), "B": (0, None, 1, None)}.get(part[3][0], (0, 1, 2, 3))
            if slots[turn] is not None:
                flying[p, 0] += begin(p, 0, slots[turn])
    embed_copies = start_embeds()
    z_copies = []

    def last_exchange(group):
        tiles, first, count = Z_GROUPS[group]
        fill = count - 40 * len(tiles)
        for j in range(4):
            pieces = [final[t, 40 * j : 40 * j + 40] for t in tiles]
            if fill:
                pieces.append(jnp.zeros((fill, 128), F32))
            z_s[j, first : first + count] = jnp.concatenate(pieces, axis=0).astype(BF16)
        for k in (1, 2, 3):
            copy = pltpu.make_async_remote_copy(
                src_ref=z_s.at[zp ^ k, pl.ds(first, count)],
                dst_ref=z_r.at[k - 1, pl.ds(first, count)],
                send_sem=z_send.at[group, k - 1],
                recv_sem=z_recv.at[group, k - 1],
                device_id=z_peers[k - 1],
                device_id_type=MESH,
            )
            copy.start()
            z_copies.append(copy)
            started.append(copy)

    for p in TURNS:
        end(p, 0, flying[p, 0])
        flying[p, 1] = begin(p, 1)
    for p in TURNS:
        end(p, 1, flying[p, 1])
        flying[p, 2] = begin(p, 2)
    for group, members in ((1, (2, 3)), (0, (0, 1)), (2, (4, 5))):
        for p in members:
            end(p, 2, flying[p, 2])
        last_exchange(group)
    embeds_copy = finish_embeds(embed_copies)
    arrive(z_copies)
    mine = z_s[zp].astype(F32)
    for k in range(3):
        mine = mine + z_r[k].astype(F32)
    first_core = c == 0
    own_tiles = []
    f_s[...] = jnp.zeros_like(f_s)
    for t in range(5):
        rows = mine[40 * t : 40 * t + 40]
        early, late = rows[0:20], rows[20:40]
        own_tiles.append(jnp.where(first_core, early, late))
        f_s[t, 0:20] = jnp.where(first_core, late, early).astype(BF16)
    arrive([to_core(6, f_s, f_r)])
    for t in range(5):
        got = f_r[t, 0:20].astype(F32)
        left = jnp.where(first_core, own_tiles[t], got)
        right = jnp.where(first_core, got, own_tiles[t])
        if t < 2:
            cols = slice(128 * t, 128 * t + 128)
            grad_qkv[0, :, cols] = left
            grad_qkv[2, :, cols] = right
        elif t < 4:
            cols = slice(128 * t - 256, 128 * t - 128)
            grad_qkv[1, :, cols] = left
            grad_out[:, cols] = right
        else:
            grad_qkv[0, :, 256:320] = left[:, 0:64]
            grad_qkv[1, :, 256:320] = left[:, 64:128]
            grad_qkv[2, :, 256:320] = right[:, 0:64]
            grad_out[:, 256:320] = right[:, 64:128]
    embeds_copy.wait()
    for copy in started:
        copy.wait_send()


def call(counts, lengths, positions, audio, cotangent, w_qkv, w_out, w_proj):
    vmem, dma = pltpu.VMEM, pltpu.SemaphoreType.DMA
    scratch = [
        vmem((3, 320, 1280), BF16),
        vmem((320, 1280), BF16),
        vmem((1280, 896), BF16),
        vmem((3, 128, 384), F32),
        vmem((4, 3, 288, 128), BF16),
        vmem((4, 288, 128), BF16),
        vmem((4, 288, 128), BF16),
        vmem((4, 80, 640), BF16),
        vmem((3, 80, 640), BF16),
        vmem((4, 80, 640), BF16),
        vmem((3, 80, 640), BF16),
        vmem((4, 80, 640), BF16),
        vmem((4, 80, 640), BF16),
        vmem((4, 288, 128), BF16),
        vmem((4, 288, 128), BF16),
        vmem((40, 3584), BF16),
        vmem((3, 100, 320), BF16),
        vmem((40, 3584), BF16),
        vmem((336, 1280), BF16),
        vmem((2, 1280, 336), BF16),
        vmem((3, 112, 384), F32),
        vmem((3, 2, 224, 128), BF16),
        vmem((3, 112, 128), BF16),
        vmem((3, 112, 384), BF16),
        vmem((3, 112, 384), BF16),
        vmem((3, 3, 224, 112), F32),
        vmem((2, 160, 384), BF16),
        vmem((2, 1280, 160), BF16),
        vmem((160, 384), BF16),
        vmem((2, 336, 640), BF16),
        vmem((336, 640), BF16),
        vmem((4, 5, 2, 160, 128), BF16),
        vmem((5, 160, 128), F32),
        vmem((4, 208, 128), BF16),
        vmem((3, 208, 128), BF16),
        vmem((5, 32, 128), BF16),
        vmem((5, 32, 128), BF16),
        dma((6,)),
        dma((9, 3)),
        dma((9, 3)),
        dma((7,)),
        dma((7,)),
        dma((6, 3, 4)),
        dma((6, 3, 4)),
        dma((3, 3)),
        dma((3, 3)),
    ]
    assert len(scratch) == 46
    scratch += [vmem(received_shape(part, step), BF16) for part in PARTS for step in range(3)]
    in_vmem = pl.BlockSpec(memory_space=pltpu.VMEM)
    in_smem = pl.BlockSpec(memory_space=pltpu.SMEM)
    anywhere = pl.BlockSpec(memory_space=pl.ANY)
    return pl.pallas_call(
        kernel,
        out_shape=(
            jax.ShapeDtypeStruct((40, 3584), BF16),
            jax.ShapeDtypeStruct((3, 20, 320), F32),
            jax.ShapeDtypeStruct((20, 320), F32),
        ),
        in_specs=[in_smem, in_smem, in_vmem] + [anywhere] * 5,
        out_specs=(anywhere, in_vmem, in_vmem),
        scratch_shapes=scratch,
        compiler_params=pltpu.CompilerParams(
            collective_id=0, has_side_effects=True, vmem_limit_bytes=60 * 2**20
        ),
        name="sublayer",
    )(counts, lengths, positions, audio, cotangent, w_qkv, w_out, w_proj)


def write_out(*refs):
    for source, target in zip(refs[:3], refs[3:]):
        target[...] = source[...]


def results(*parts):
    in_vmem = pl.BlockSpec(memory_space=pltpu.VMEM)
    return pl.pallas_call(
        write_out,
        out_shape=tuple(jax.ShapeDtypeStruct(part.shape, part.dtype) for part in parts),
        in_specs=[in_vmem] * 3,
        out_specs=(in_vmem,) * 3,
        name="results",
    )(*parts)


def shards(audio, counts, lengths, positions, w_qkv, w_out, w_proj, cotangent):
    embeds, grad_qkv, grad_out = call(
        counts, lengths, positions, audio, cotangent, jnp.swapaxes(w_qkv, 1, 2), w_out, w_proj
    )
    embeds, grad_qkv, grad_out = results(embeds, grad_qkv, grad_out)
    return embeds, grad_qkv, grad_out.T


def solution(mesh):
    in_specs = (
        P("dp", None, "seq"),
        P("dp"),
        P("dp"),
        P("dp", None),
        P(None, None, "seq"),
        P("seq", None),
        P(None, "seq"),
        P(("dp", "seq"), None),
    )
    out_specs = (P(("dp", "seq"), None), P(None, "dp", "seq"), P("seq", "dp"))
    return jax.shard_map(shards, mesh=mesh, in_specs=in_specs, out_specs=out_specs, check_vma=False)
```

```python
import jax
import jax.numpy as jnp
from jax import lax
from jax.experimental import pallas as pl
from jax.experimental.pallas import tpu as pltpu
from jax.sharding import PartitionSpec as P

MESH = pl.DeviceIdType.MESH
F32 = jnp.float32
BF16 = jnp.bfloat16
EPSILON = 1e-05
SCALING = 0.125
PARTS = tuple(
    (tile, row, 80, order)
    for row, orders in ((0, ("ABa", "BAb", "aAB", "bBA", "ABa")), (80, ("ABa", "BAb", "aAB", "bBA", "BAb")))
    for tile, order in enumerate(orders)
)
TURNS = (2, 3, 0, 1, 4, 7, 8, 5, 6, 9)
Z_GROUPS = (((0, 1), 0, 80), ((2, 3), 80, 80), ((4,), 160, 48))


def dot(a, b):
    return jnp.dot(a, b, preferred_element_type=F32)


def dot_nt(a, b):
    return lax.dot_general(a, b, (((1,), (1,)), ((), ())), preferred_element_type=F32)


def dot_tn(a, b):
    return lax.dot_general(a, b, (((0,), (0,)), ((), ())), preferred_element_type=F32)


def fold(rows, width, extra):
    pieces = [rows[:, i : i + width] for i in range(0, rows.shape[1], width)]
    if extra:
        pieces.append(jnp.zeros((extra, width), F32))
    return jnp.concatenate(pieces, axis=0).astype(BF16)


def unfold(folded, count):
    wide = folded.astype(F32)
    return jnp.concatenate([wide[40 * i : 40 * i + 40] for i in range(count)], axis=1)


def normalize(rows):
    centred = rows - jnp.mean(rows, axis=-1, keepdims=True)
    inverse = lax.rsqrt(jnp.mean(centred * centred, axis=-1, keepdims=True) + EPSILON)
    return centred * inverse, inverse


def received_shape(part, step):
    _, _, rows, order = part
    before = order[:step]
    y_done = sum(letter in "AB" for letter in before)
    z_done = any(letter in "ab" for letter in before)
    if order[step] in "AB":
        return (2 if y_done == 0 else 1, 1 if z_done else 2, rows, 128)
    return ((4, 2, 1)[y_done], 1, rows, 128)


def kernel(*refs):
    (counts, lengths, positions, audio, cotangent, w_qkv, w_out, w_proj) = refs[:8]
    embeds, grad_qkv, grad_out = refs[8:11]
    (
        wq, wo, wp, tmp, aud, cot_s, cot_r, gt_s, gt_r, t_s, t_r, ag_a, ad_a, e_s, e_r, cot_v, aud_v, emb,
        nb, nt, pj, q2s, qr_s, k_s, v_s, prob, attp_s, agt, mgp, local, other, total, final, prob_t, up_s,
        z_s, z_r, f_s, f_r, w_sem, x_send, x_recv, c_send, c_recv, r_send, r_recv, z_send, z_recv,
    ) = refs[11 : 11 + 48]
    r_bufs = refs[11 + 48 :]

    dp = lax.axis_index("dp")
    x = lax.axis_index("seq")
    y = dp // 16
    z = (dp // 2) % 8
    c = dp % 2
    par = z % 2
    zp = z // 2

    def at(yy, zz, cc):
        return (yy * 16 + zz * 2 + cc, x)

    peers = [(dp, (x + k) % 4) for k in (1, 2, 3)]
    partner = {
        "A": at(y ^ 1, z, c),
        "B": at(y ^ 3, z, c),
        "a": at(y, z ^ 1, c),
        "b": at(y, (z + 7 + 2 * par) % 8, c),
    }
    core_peer = at(y, z, 1 - c)
    z_peers = [at(y, z ^ (2 * k), c) for k in (1, 2, 3)]

    input_copies = [
        pltpu.make_async_copy(src, dst, w_sem.at[3 + i])
        for i, (src, dst) in enumerate(((cotangent, cot_v), (audio, aud_v)))
    ]
    weight_copies = [
        pltpu.make_async_copy(src, dst, w_sem.at[i])
        for i, (src, dst) in enumerate(((w_qkv, wq), (w_out, wo), (w_proj, wp)))
    ]
    for copy in input_copies:
        copy.start()

    barrier = pltpu.get_barrier_semaphore()
    everyone = peers + [core_peer] + list(partner.values()) + z_peers
    for device in everyone:
        pl.semaphore_signal(barrier, inc=1, device_id=device, device_id_type=MESH)

    for i in (2, 0, 1):
        weight_copies[i].start()

    lane = lax.broadcasted_iota(jnp.int32, (112, 128), 1)
    low = lane < 64
    low_half = low[0:64]
    tmp[...] = jnp.zeros_like(tmp)
    pj[...] = jnp.zeros_like(pj)
    mgp[...] = jnp.zeros_like(mgp)
    local[1, :, 384:640] = jnp.zeros((336, 256), BF16)
    input_copies[0].wait()
    cot_rows = cot_v[...].astype(F32)
    for t in range(4):
        cot_s[t] = fold(cot_rows[:, 896 * t : 896 * t + 896], 128, 8)
    cot_r[x] = cot_s[x]

    def pack_audio(b):
        tmp[b, 0:100, 0:320] = aud_v[b].astype(F32)
        first, second, third = (tmp[b, :, 128 * i : 128 * i + 128] for i in range(3))
        second_turned = pltpu.roll(second, 64, 1)
        packed = third[0:64] + pltpu.roll(third[64:128], 64, 1)
        packed_odd = jnp.where(low_half, first[0:64], pltpu.roll(first[64:128], 64, 1))
        even = jnp.concatenate([first[0:112], second[0:112], packed], axis=0)
        odd = jnp.concatenate(
            [
                jnp.where(low, pltpu.roll(first, 64, 1)[0:112], second_turned[0:112]),
                jnp.where(low, second_turned[0:112], pltpu.roll(third, 64, 1)[0:112]),
                packed_odd,
            ],
            axis=0,
        )
        aud[x, b] = jnp.where(x % 2 == 0, even, odd).astype(BF16)

    input_copies[1].wait()
    pack_audio(0)

    pl.semaphore_wait(barrier, len(everyone))

    started = []
    def to_peers(slot, source, target):
        copies = []
        for k in (1, 2, 3):
            there = (x + k) % 4
            copy = pltpu.make_async_remote_copy(
                src_ref=source(there),
                dst_ref=target(k),
                send_sem=x_send.at[slot, k - 1],
                recv_sem=x_recv.at[slot, k - 1],
                device_id=(dp, there),
                device_id_type=MESH,
            )
            copy.start()
            copies.append(copy)
        started.extend(copies)
        return copies

    def to_core(slot, source, target):
        copy = pltpu.make_async_remote_copy(
            src_ref=source,
            dst_ref=target,
            send_sem=c_send.at[slot],
            recv_sem=c_recv.at[slot],
            device_id=core_peer,
            device_id_type=MESH,
        )
        copy.start()
        started.append(copy)
        return copy

    def arrive(copies):
        for copy in copies:
            copy.wait_recv()

    audio_copies = []
    cot_copies = to_peers(3, lambda there: cot_s.at[there], lambda k: cot_r.at[x])
    for b in range(3):
        if b > 0:
            pack_audio(b)
        block = aud.at[x, b]
        audio_copies.append(to_peers(b, lambda there: block, lambda k: block))

    pos_pad = jnp.concatenate([positions[...].astype(F32), jnp.zeros((13, 50), F32)], axis=0).astype(BF16)
    frame_row = lax.broadcasted_iota(jnp.int32, (50, 112), 0)
    frame_col = lax.broadcasted_iota(jnp.int32, (50, 112), 1)
    spread = jnp.where(frame_row == frame_col // 2, 1.0, 0.0).astype(BF16)
    pos_lanes = dot(pos_pad, spread)
    frame_row_t = lax.broadcasted_iota(jnp.int32, (112, 50), 0)
    frame_col_t = lax.broadcasted_iota(jnp.int32, (112, 50), 1)
    spread_t = jnp.where(frame_row_t // 2 == frame_col_t, 1.0, 0.0).astype(BF16)
    pos_sub = dot_nt(spread_t, pos_pad)
    lives = [jnp.where(b < counts[0], lengths[b], 0) for b in range(3)]

    def place(b, first, count):
        row = lax.broadcasted_iota(jnp.int32, (count, 112), 0) + first
        frame = lax.broadcasted_iota(jnp.int32, (count, 112), 1)
        hit = (row.astype(F32) == pos_lanes[b : b + 1, :]) & (frame < lives[b])
        return jnp.where(hit, 1.0, 0.0).astype(BF16)

    def unplace(b):
        frame = lax.broadcasted_iota(jnp.int32, (112, 160), 0)
        row = lax.broadcasted_iota(jnp.int32, (112, 160), 1)
        hit = (row.astype(F32) == pos_sub[:, b : b + 1]) & (frame < lives[b])
        return jnp.where(hit, 1.0, 0.0).astype(BF16)

    def split_heads(tile):
        return jnp.concatenate([jnp.where(low, tile, 0.0), jnp.where(low, 0.0, tile)], axis=0).astype(BF16)

    weight_copies[0].wait()

    attp = [jnp.zeros((160, 128), F32) for _ in range(3)]
    pooled_audio = jnp.zeros((40, 1280), F32)

    def forward(b, attp, pooled_audio):
        arrive(audio_copies[b])
        tiles = []
        for s in (0, 2):
            left = aud[s, b, 224:288].astype(F32)
            right = aud[s + 1, b, 224:288].astype(F32)
            top = jnp.where(low_half, left, pltpu.roll(right, 64, 1))
            bottom = jnp.where(low_half, pltpu.roll(left, 64, 1), right)
            tiles.append(aud[s, b, 0:112].astype(F32))
            tiles.append(aud[s, b, 112:224].astype(F32))
            tiles.append(jnp.concatenate([top, bottom[0:48]], axis=0))
            tiles.append(aud[s + 1, b, 0:112].astype(F32))
            tiles.append(aud[s + 1, b, 112:224].astype(F32))
        frames = jnp.concatenate(tiles, axis=1)
        pooled_audio = pooled_audio + dot(place(b, 40 * x, 40), frames.astype(BF16))
        normed = normalize(frames)[0].astype(BF16)
        nb[112 * b : 112 * b + 112, :] = normed
        for j in range(3):
            pj[j, :, 0:320] = dot_nt(normed, wq[j])
        k_s[b] = pj[1].astype(BF16)
        v_s[b] = pj[2].astype(BF16)
        key_limit = jnp.maximum(lives[b], 1)
        placed = place(b, 0, 160)
        for g in range(3):
            cols = slice(128 * g, 128 * g + 128)
            q_tile = pj[0, :, cols]
            if g < 2:
                queries = split_heads(q_tile)
                q2s[b, g] = queries
            else:
                queries = q_tile.astype(BF16)
                qr_s[b] = queries
            rows = queries.shape[0]
            scores = dot_nt(queries, k_s[b, :, cols]) * SCALING
            key = lax.broadcasted_iota(jnp.int32, (rows, 112), 1)
            scores = jnp.where(key < key_limit, scores, -1e30)
            powered = jnp.exp(scores - jnp.max(scores, axis=-1, keepdims=True))
            weights = powered * (1.0 / jnp.sum(powered, axis=-1, keepdims=True))
            prob[b, g, 0:rows] = weights
            scores_t = dot_nt(k_s[b, :, cols], queries) * SCALING
            key_t = lax.broadcasted_iota(jnp.int32, (112, rows), 0)
            scores_t = jnp.where(key_t < key_limit, scores_t, -1e30)
            powered_t = jnp.exp(scores_t - jnp.max(scores_t, axis=0, keepdims=True))
            prob_t[b, g, :, 0:rows] = powered_t * (1.0 / jnp.sum(powered_t, axis=0, keepdims=True))
            mixed = dot(weights.astype(BF16), v_s[b, :, cols])
            if g < 2:
                mixed = jnp.where(low, mixed[0:112], mixed[112:224])
            attp[g] = attp[g] + dot(placed, mixed.astype(BF16))
        return attp, pooled_audio

    attp, pooled_audio = forward(0, attp, pooled_audio)

    weight_copies[2].wait()
    arrive(cot_copies)
    row_grads = jnp.concatenate([unfold(cot_r[s], 7) for s in range(4)], axis=0).astype(BF16)
    adapter_terms = dot_nt(row_grads, wp[...])
    for t in range(4):
        gt_s[t] = fold(adapter_terms[40 * t : 40 * t + 40], 640, 0)
    attp, pooled_audio = forward(1, attp, pooled_audio)
    gt_copies = to_peers(4, lambda there: gt_s.at[there], lambda k: gt_r.at[k - 1])

    attp, pooled_audio = forward(2, attp, pooled_audio)
    attp = [part.astype(BF16) for part in attp]
    for g in range(2):
        attp_s[c, :, 128 * g : 128 * g + 128] = attp[g]
    attp_s[c, :, 256:384] = pltpu.roll(attp[2].astype(F32), 64, 1).astype(BF16)
    weight_copies[1].wait()
    head_terms = (
        dot(attp[0], wo[0:128]) + dot(attp[1], wo[128:256]) + dot(attp[2][:, 0:64], wo[256:320])
    )
    for t in range(4):
        t_s[t] = fold(head_terms[40 * t : 40 * t + 40], 640, 0)
    t_copies = to_peers(5, lambda there: t_s.at[there], lambda k: t_r.at[k - 1])

    nt[c] = nb[...].T
    for b in range(3):
        up_s[b] = unplace(b)
    core_copies = [to_core(0, nt.at[c], nt.at[c]), to_core(1, attp_s.at[c], attp_s.at[c])]

    arrive(gt_copies)
    adapted_grad = gt_s[x].astype(F32)
    for k in range(3):
        adapted_grad = adapted_grad + gt_r[k].astype(F32)
    adapted_grad = unfold(adapted_grad.astype(BF16), 2)

    arrive(t_copies)
    attention = t_s[x].astype(F32)
    for k in range(3):
        attention = attention + t_r[k].astype(F32)
    attention = jnp.concatenate([attention[0:40], attention[40:80]], axis=1)
    normed_rows, inverse = normalize((pooled_audio + attention) * 0.5)
    pooled_grad = inverse * (
        adapted_grad
        - jnp.mean(adapted_grad, axis=-1, keepdims=True)
        - normed_rows * jnp.mean(adapted_grad * normed_rows, axis=-1, keepdims=True)
    )
    ag_a[x] = fold(pooled_grad * 0.5, 640, 0)
    ag_copies = to_peers(6, lambda there: ag_a.at[x], lambda k: ag_a.at[x])
    ad_a[x] = fold(normed_rows, 640, 0)
    arrive(ag_copies)
    attention_grad = jnp.concatenate([unfold(ag_a[s], 2) for s in range(4)], axis=0).astype(BF16)
    mgp[:, 0:320] = dot_nt(attention_grad, wo[...]).astype(BF16)
    pairs = [(b, g) for b in range(3) for g in range(3)]
    grads, prob_grads, prob_grads_t, halves, halves_t = {}, {}, {}, {}, {}
    for b in range(3):
        mixed_grad = dot(up_s[b], mgp[...])
        for g in range(3):
            tile = mixed_grad[:, 128 * g : 128 * g + 128]
            grads[b, g] = split_heads(tile) if g < 2 else tile.astype(BF16)
    for b, g in pairs:
        cols = slice(128 * g, 128 * g + 128)
        prob_grads[b, g] = dot_nt(grads[b, g], v_s[b, :, cols])
        prob_grads_t[b, g] = dot_nt(v_s[b, :, cols], grads[b, g])
    for b, g in pairs:
        count = 224 if g < 2 else 112
        weights, weights_t = prob[b, g, 0:count], prob_t[b, g, :, 0:count]
        inner = jnp.sum(weights * prob_grads[b, g], axis=-1, keepdims=True)
        inner_t = jnp.sum(weights_t * prob_grads_t[b, g], axis=0, keepdims=True)
        halves[b, g] = (weights * (prob_grads[b, g] - inner)).astype(BF16)
        halves_t[b, g] = (weights_t * (prob_grads_t[b, g] - inner_t)).astype(BF16)
    for b in range(3):
        rows = slice(112 * b, 112 * b + 112)
        for g in range(3):
            cols = slice(128 * g, 128 * g + 128)
            count = 224 if g < 2 else 112
            query_grad = dot(halves[b, g], k_s[b, :, cols])
            if g < 2:
                query_grad = jnp.where(low, query_grad[0:112], query_grad[112:224])
            query_grad = query_grad * SCALING
            key_grad = dot(halves_t[b, g], q2s[b, g] if g < 2 else qr_s[b]) * SCALING
            value_grad = dot(prob_t[b, g, :, 0:count].astype(BF16), grads[b, g])
            local[1, rows, cols] = value_grad.astype(BF16)
            if g < 2:
                local[0, rows, cols] = query_grad.astype(BF16)
                local[0, rows, 256 + 128 * g : 384 + 128 * g] = key_grad.astype(BF16)
            else:
                local[0, rows, 512:640] = (query_grad + pltpu.roll(key_grad, 64, 1)).astype(BF16)
    agt[c] = attention_grad.T
    core_copies.append(to_core(2, local.at[1 - c], other))
    core_copies.append(to_core(3, agt.at[c], agt.at[c]))
    ad_copies = to_peers(7, lambda there: ad_a.at[x], lambda k: ad_a.at[x])

    def start_embeds():
        arrive(ad_copies)
        adapted = jnp.concatenate([unfold(ad_a[s], 2) for s in range(4)], axis=0).astype(BF16)
        adapter_rows = dot(adapted, wp[...])
        for t in range(4):
            e_s[t] = fold(adapter_rows[40 * t : 40 * t + 40], 128, 8)
        e_r[x] = e_s[x]
        return to_peers(8, lambda there: e_s.at[there], lambda k: e_r.at[x])

    def finish_embeds(copies):
        arrive(copies)
        for s in range(4):
            emb[:, 896 * s : 896 * s + 896] = unfold(e_r[s], 7).astype(BF16)
        copy = pltpu.make_async_copy(emb, embeds, w_sem.at[5])
        copy.start()
        return copy

    def blocks(order, step):
        y_before = [letter for letter in order[:step] if letter in "AB"]
        z_done = any(letter in "ab" for letter in order[:step])
        letter = order[step]
        if letter in "AB":
            near = y ^ (1 if letter == "A" else 3)
            beyond = y ^ (3 if letter == "A" else 1)
            sides = (par, par) if z_done else (None, None)
            if y_before:
                return [near], [y], sides
            return [y ^ 2, near], [beyond, y], sides
        held = [y ^ 2, y ^ 1, y ^ 3, y]
        if len(y_before) == 1:
            held = [y ^ (3 if y_before[0] == "A" else 1), y]
        elif len(y_before) == 2:
            held = [y]
        return held, held, (1 - par, par)

    def begin(p, step, only=None):
        tile, row, count, order = PARTS[p]
        send, _, (side, _) = blocks(order, step)
        landing = r_bufs[3 * p + step]
        copies = []
        for i, block in enumerate(send):
            if only is not None and i != only:
                continue
            pick = pl.ds(0, 2) if side is None else pl.ds(side, 1)
            copy = pltpu.make_async_remote_copy(
                src_ref=total.at[block, tile, pick, pl.ds(row, count)],
                dst_ref=landing.at[i],
                send_sem=r_send.at[p, step, i],
                recv_sem=r_recv.at[p, step, i],
                device_id=partner[order[step]],
                device_id_type=MESH,
            )
            copy.start()
            copies.append(copy)
        started.extend(copies)
        return copies

    def end(p, step, copies):
        tile, row, count, order = PARTS[p]
        _, keep, (_, side) = blocks(order, step)
        landing = r_bufs[3 * p + step]
        rows = pl.ds(row, count)
        arrive(copies)
        for i, block in enumerate(keep):
            if step == 2:
                final[tile, rows] = total[block, tile, par, rows].astype(F32) + landing[i, 0].astype(F32)
            elif side is None:
                for k in range(2):
                    kept = total[block, tile, k, rows].astype(F32) + landing[i, k].astype(F32)
                    total[block, tile, k, rows] = kept.astype(BF16)
            else:
                kept = total[block, tile, side, rows].astype(F32) + landing[i, 0].astype(F32)
                total[block, tile, side, rows] = kept.astype(BF16)

    arrive(core_copies)
    flying = {(p, 0): [] for p in range(len(PARTS))}
    turns = (y ^ 2, y ^ 1, y ^ 3, y)
    for turn, yy in enumerate(turns):
        rows = pl.ds(pl.multiple_of(320 * yy, 64), 320)

        def store(tile, values):
            for side in range(2):
                total[yy, tile, side] = jnp.concatenate(
                    [values[40 * i : 40 * i + 40] for i in range(side, 8, 2)], axis=0
                ).astype(BF16)

        @pl.when(c == 0)
        def _():
            part = dot(nt[0, rows], local[0]) + dot(nt[1, rows], other[...])
            for t in range(5):
                store(t, part[:, 128 * t : 128 * t + 128])

        @pl.when(c == 1)
        def _():
            value_part = dot(nt[1, rows], local[1, :, 0:384]) + dot(nt[0, rows], other[:, 0:384])
            out_part = dot(agt[0, rows], attp_s[0]) + dot(agt[1, rows], attp_s[1])
            store(0, value_part[:, 0:128])
            store(1, value_part[:, 128:256])
            store(2, out_part[:, 0:128])
            store(3, out_part[:, 128:256])
            store(4, value_part[:, 256:384] + out_part[:, 256:384])

        for p, part in enumerate(PARTS):
            slots = {"A": (0, 1, None, None), "B": (0, None, 1, None)}.get(part[3][0], (0, 1, 2, 3))
            if slots[turn] is not None:
                flying[p, 0] += begin(p, 0, slots[turn])
    embed_copies = start_embeds()
    z_copies = []

    def last_exchange(group):
        tiles, first, count = Z_GROUPS[group]
        fill = count - 40 * len(tiles)
        for j in range(4):
            pieces = [final[t, 40 * j : 40 * j + 40] for t in tiles]
            if fill:
                pieces.append(jnp.zeros((fill, 128), F32))
            z_s[j, first : first + count] = jnp.concatenate(pieces, axis=0).astype(BF16)
        for k in (1, 2, 3):
            copy = pltpu.make_async_remote_copy(
                src_ref=z_s.at[zp ^ k, pl.ds(first, count)],
                dst_ref=z_r.at[k - 1, pl.ds(first, count)],
                send_sem=z_send.at[group, k - 1],
                recv_sem=z_recv.at[group, k - 1],
                device_id=z_peers[k - 1],
                device_id_type=MESH,
            )
            copy.start()
            z_copies.append(copy)
            started.append(copy)

    for p in TURNS:
        end(p, 0, flying[p, 0])
        flying[p, 1] = begin(p, 1)
    for p in TURNS:
        end(p, 1, flying[p, 1])
        flying[p, 2] = begin(p, 2)
    for group, members in ((1, (2, 3, 7, 8)), (0, (0, 1, 5, 6)), (2, (4, 9))):
        for p in members:
            end(p, 2, flying[p, 2])
        last_exchange(group)
    embeds_copy = finish_embeds(embed_copies)
    arrive(z_copies)
    mine = z_s[zp].astype(F32)
    for k in range(3):
        mine = mine + z_r[k].astype(F32)
    first_core = c == 0
    own_tiles = []
    f_s[...] = jnp.zeros_like(f_s)
    for t in range(5):
        rows = mine[40 * t : 40 * t + 40]
        early, late = rows[0:20], rows[20:40]
        own_tiles.append(jnp.where(first_core, early, late))
        f_s[t, 0:20] = jnp.where(first_core, late, early).astype(BF16)
    arrive([to_core(4, f_s, f_r)])
    for t in range(5):
        got = f_r[t, 0:20].astype(F32)
        left = jnp.where(first_core, own_tiles[t], got)
        right = jnp.where(first_core, got, own_tiles[t])
        if t < 2:
            cols = slice(128 * t, 128 * t + 128)
            grad_qkv[0, :, cols] = left
            grad_qkv[2, :, cols] = right
        elif t < 4:
            cols = slice(128 * t - 256, 128 * t - 128)
            grad_qkv[1, :, cols] = left
            grad_out[:, cols] = right
        else:
            grad_qkv[0, :, 256:320] = left[:, 0:64]
            grad_qkv[1, :, 256:320] = left[:, 64:128]
            grad_qkv[2, :, 256:320] = right[:, 0:64]
            grad_out[:, 256:320] = right[:, 64:128]
    embeds_copy.wait()
    for copy in started:
        copy.wait_send()


def call(counts, lengths, positions, audio, cotangent, w_qkv, w_out, w_proj):
    vmem, dma = pltpu.VMEM, pltpu.SemaphoreType.DMA
    scratch = [
        vmem((3, 320, 1280), BF16),
        vmem((320, 1280), BF16),
        vmem((1280, 896), BF16),
        vmem((3, 128, 384), F32),
        vmem((4, 3, 288, 128), BF16),
        vmem((4, 288, 128), BF16),
        vmem((4, 288, 128), BF16),
        vmem((4, 80, 640), BF16),
        vmem((3, 80, 640), BF16),
        vmem((4, 80, 640), BF16),
        vmem((3, 80, 640), BF16),
        vmem((4, 80, 640), BF16),
        vmem((4, 80, 640), BF16),
        vmem((4, 288, 128), BF16),
        vmem((4, 288, 128), BF16),
        vmem((40, 3584), BF16),
        vmem((3, 100, 320), BF16),
        vmem((40, 3584), BF16),
        vmem((336, 1280), BF16),
        vmem((2, 1280, 336), BF16),
        vmem((3, 112, 384), F32),
        vmem((3, 2, 224, 128), BF16),
        vmem((3, 112, 128), BF16),
        vmem((3, 112, 384), BF16),
        vmem((3, 112, 384), BF16),
        vmem((3, 3, 224, 112), F32),
        vmem((2, 160, 384), BF16),
        vmem((2, 1280, 160), BF16),
        vmem((160, 384), BF16),
        vmem((2, 336, 640), BF16),
        vmem((336, 640), BF16),
        vmem((4, 5, 2, 160, 128), BF16),
        vmem((5, 160, 128), F32),
        vmem((3, 3, 112, 224), F32),
        vmem((3, 112, 160), BF16),
        vmem((4, 208, 128), BF16),
        vmem((3, 208, 128), BF16),
        vmem((5, 32, 128), BF16),
        vmem((5, 32, 128), BF16),
        dma((6,)),
        dma((9, 3)),
        dma((9, 3)),
        dma((5,)),
        dma((5,)),
        dma((len(PARTS), 3, 4)),
        dma((len(PARTS), 3, 4)),
        dma((3, 3)),
        dma((3, 3)),
    ]
    assert len(scratch) == 48
    scratch += [vmem(received_shape(part, step), BF16) for part in PARTS for step in range(3)]
    in_vmem = pl.BlockSpec(memory_space=pltpu.VMEM)
    in_smem = pl.BlockSpec(memory_space=pltpu.SMEM)
    anywhere = pl.BlockSpec(memory_space=pl.ANY)
    return pl.pallas_call(
        kernel,
        out_shape=(
            jax.ShapeDtypeStruct((40, 3584), BF16),
            jax.ShapeDtypeStruct((3, 20, 320), F32),
            jax.ShapeDtypeStruct((20, 320), F32),
        ),
        in_specs=[in_smem, in_smem, in_vmem] + [anywhere] * 5,
        out_specs=(anywhere, in_vmem, in_vmem),
        scratch_shapes=scratch,
        compiler_params=pltpu.CompilerParams(
            collective_id=0, has_side_effects=True, vmem_limit_bytes=60 * 2**20
        ),
        name="sublayer",
    )(counts, lengths, positions, audio, cotangent, w_qkv, w_out, w_proj)


def write_out(*refs):
    for source, target in zip(refs[:3], refs[3:]):
        target[...] = source[...]


def results(*parts):
    in_vmem = pl.BlockSpec(memory_space=pltpu.VMEM)
    return pl.pallas_call(
        write_out,
        out_shape=tuple(jax.ShapeDtypeStruct(part.shape, part.dtype) for part in parts),
        in_specs=[in_vmem] * 3,
        out_specs=(in_vmem,) * 3,
        name="results",
    )(*parts)


def shards(audio, counts, lengths, positions, w_qkv, w_out, w_proj, cotangent):
    embeds, grad_qkv, grad_out = call(
        counts, lengths, positions, audio, cotangent, jnp.swapaxes(w_qkv, 1, 2), w_out, w_proj
    )
    embeds, grad_qkv, grad_out = results(embeds, grad_qkv, grad_out)
    return embeds, grad_qkv, grad_out.T


def solution(mesh):
    in_specs = (
        P("dp", None, "seq"),
        P("dp"),
        P("dp"),
        P("dp", None),
        P(None, None, "seq"),
        P("seq", None),
        P(None, "seq"),
        P(("dp", "seq"), None),
    )
    out_specs = (P(("dp", "seq"), None), P(None, "dp", "seq"), P("seq", "dp"))
    return jax.shard_map(shards, mesh=mesh, in_specs=in_specs, out_specs=out_specs, check_vma=False)
```

```python
import jax
import jax.numpy as jnp
from jax import lax
from jax.experimental import pallas as pl
from jax.experimental.pallas import tpu as pltpu
from jax.sharding import PartitionSpec as P

MESH = pl.DeviceIdType.MESH
F32 = jnp.float32
BF16 = jnp.bfloat16
EPSILON = 1e-05
SCALING = 0.125
PARTS = tuple(
    (tile, row, 80, order)
    for tile, orders in ((0, ("AaB", "BbA")), (1, ("aAB", "bBA")), (4, ("AaB", "BbA")), (2, ("AaB", "BbA")), (3, ("aAB", "bBA")))
    for row, order in zip((0, 80), orders)
)
WAVES = ((0, 1, 2, 3, 4, 5), (6, 7, 8, 9))
Z_GROUPS = (((0, 1, 4), 0, 128), ((2, 3), 128, 80))
TILE_ROWS = {0: 0, 1: 40, 4: 80, 2: 128, 3: 168}


def dot(a, b):
    return jnp.dot(a, b, preferred_element_type=F32)


def dot_nt(a, b):
    return lax.dot_general(a, b, (((1,), (1,)), ((), ())), preferred_element_type=F32)


def dot_tn(a, b):
    return lax.dot_general(a, b, (((0,), (0,)), ((), ())), preferred_element_type=F32)


def fold(rows, width, extra):
    pieces = [rows[:, i : i + width] for i in range(0, rows.shape[1], width)]
    if extra:
        pieces.append(jnp.zeros((extra, width), F32))
    return jnp.concatenate(pieces, axis=0).astype(BF16)


def unfold(folded, count):
    wide = folded.astype(F32)
    return jnp.concatenate([wide[40 * i : 40 * i + 40] for i in range(count)], axis=1)


def normalize(rows):
    centred = rows - jnp.mean(rows, axis=-1, keepdims=True)
    inverse = lax.rsqrt(jnp.mean(centred * centred, axis=-1, keepdims=True) + EPSILON)
    return centred * inverse, inverse


def received_shape(part, step):
    _, _, rows, order = part
    before = order[:step]
    y_done = sum(letter in "AB" for letter in before)
    z_done = any(letter in "ab" for letter in before)
    if order[step] in "AB":
        return (2 if y_done == 0 else 1, 1 if z_done else 2, rows, 128)
    return ((4, 2, 1)[y_done], 1, rows, 128)


def kernel(*refs):
    (counts, lengths, positions, audio, cotangent, w_qkv, w_out, w_proj) = refs[:8]
    embeds, grad_qkv, grad_out = refs[8:11]
    (
        wq, wo, wp, tmp, aud, cot_s, cot_r, gt_s, gt_r, t_s, t_r, ag_a, ad_a, e_s, e_r, cot_v, aud_v, emb,
        nb, nt, pj, q2s, qr_s, k_s, v_s, prob, attp_s, agt, mgp, local, other, total, final, prob_t, up_s,
        z_s, z_r, f_s, f_r, w_sem, x_send, x_recv, c_send, c_recv, r_send, r_recv, z_send, z_recv,
    ) = refs[11 : 11 + 48]
    r_bufs = refs[11 + 48 :]

    dp = lax.axis_index("dp")
    x = lax.axis_index("seq")
    y = dp // 16
    z = (dp // 2) % 8
    c = dp % 2
    par = z % 2
    zp = z // 2

    def at(yy, zz, cc):
        return (yy * 16 + zz * 2 + cc, x)

    peers = [(dp, (x + k) % 4) for k in (1, 2, 3)]
    partner = {
        "A": at(y ^ 1, z, c),
        "B": at(y ^ 3, z, c),
        "a": at(y, z ^ 1, c),
        "b": at(y, (z + 7 + 2 * par) % 8, c),
    }
    core_peer = at(y, z, 1 - c)
    z_peers = [at(y, z ^ (2 * k), c) for k in (1, 2, 3)]

    input_copies = [
        pltpu.make_async_copy(src, dst, w_sem.at[3 + i])
        for i, (src, dst) in enumerate(((cotangent, cot_v), (audio, aud_v)))
    ]
    weight_copies = [
        pltpu.make_async_copy(src, dst, w_sem.at[i])
        for i, (src, dst) in enumerate(((w_qkv, wq), (w_out, wo), (w_proj, wp)))
    ]
    for copy in input_copies:
        copy.start()

    barrier = pltpu.get_barrier_semaphore()
    everyone = peers + [core_peer] + list(partner.values()) + z_peers
    for device in everyone:
        pl.semaphore_signal(barrier, inc=1, device_id=device, device_id_type=MESH)

    for i in (2, 0, 1):
        weight_copies[i].start()

    lane = lax.broadcasted_iota(jnp.int32, (112, 128), 1)
    low = lane < 64
    low_half = low[0:64]
    tmp[...] = jnp.zeros_like(tmp)
    pj[...] = jnp.zeros_like(pj)
    mgp[...] = jnp.zeros_like(mgp)
    local[1, :, 384:640] = jnp.zeros((336, 256), BF16)
    input_copies[0].wait()
    cot_rows = cot_v[...].astype(F32)
    for t in range(4):
        cot_s[t] = fold(cot_rows[:, 896 * t : 896 * t + 896], 128, 8)
    cot_r[x] = cot_s[x]

    def pack_audio(b):
        tmp[b, 0:100, 0:320] = aud_v[b].astype(F32)
        first, second, third = (tmp[b, :, 128 * i : 128 * i + 128] for i in range(3))
        second_turned = pltpu.roll(second, 64, 1)
        packed = third[0:64] + pltpu.roll(third[64:128], 64, 1)
        packed_odd = jnp.where(low_half, first[0:64], pltpu.roll(first[64:128], 64, 1))
        even = jnp.concatenate([first[0:112], second[0:112], packed], axis=0)
        odd = jnp.concatenate(
            [
                jnp.where(low, pltpu.roll(first, 64, 1)[0:112], second_turned[0:112]),
                jnp.where(low, second_turned[0:112], pltpu.roll(third, 64, 1)[0:112]),
                packed_odd,
            ],
            axis=0,
        )
        aud[x, b] = jnp.where(x % 2 == 0, even, odd).astype(BF16)

    input_copies[1].wait()
    pack_audio(0)

    pl.semaphore_wait(barrier, len(everyone))

    started = []
    def to_peers(slot, source, target):
        copies = []
        for k in (1, 2, 3):
            there = (x + k) % 4
            copy = pltpu.make_async_remote_copy(
                src_ref=source(there),
                dst_ref=target(k),
                send_sem=x_send.at[slot, k - 1],
                recv_sem=x_recv.at[slot, k - 1],
                device_id=(dp, there),
                device_id_type=MESH,
            )
            copy.start()
            copies.append(copy)
        started.extend(copies)
        return copies

    def to_core(slot, source, target):
        copy = pltpu.make_async_remote_copy(
            src_ref=source,
            dst_ref=target,
            send_sem=c_send.at[slot],
            recv_sem=c_recv.at[slot],
            device_id=core_peer,
            device_id_type=MESH,
        )
        copy.start()
        started.append(copy)
        return copy

    def leave(copies):
        for copy in copies:
            copy.wait_send()
            started[:] = [other_copy for other_copy in started if other_copy is not copy]

    def arrive(copies):
        for copy in copies:
            copy.wait_recv()

    audio_copies = []
    cot_copies = to_peers(3, lambda there: cot_s.at[there], lambda k: cot_r.at[x])

    def send_audio(b):
        block = aud.at[x, b]
        audio_copies.append(to_peers(b, lambda there: block, lambda k: block))

    send_audio(0)
    pack_audio(1)
    pack_audio(2)
    leave(cot_copies)
    send_audio(1)
    send_audio(2)

    pos_pad = jnp.concatenate([positions[...].astype(F32), jnp.zeros((13, 50), F32)], axis=0).astype(BF16)
    frame_row = lax.broadcasted_iota(jnp.int32, (50, 112), 0)
    frame_col = lax.broadcasted_iota(jnp.int32, (50, 112), 1)
    spread = jnp.where(frame_row == frame_col // 2, 1.0, 0.0).astype(BF16)
    pos_lanes = dot(pos_pad, spread)
    frame_row_t = lax.broadcasted_iota(jnp.int32, (112, 50), 0)
    frame_col_t = lax.broadcasted_iota(jnp.int32, (112, 50), 1)
    spread_t = jnp.where(frame_row_t // 2 == frame_col_t, 1.0, 0.0).astype(BF16)
    pos_sub = dot_nt(spread_t, pos_pad)
    lives = [jnp.where(b < counts[0], lengths[b], 0) for b in range(3)]

    def place(b, first, count):
        row = lax.broadcasted_iota(jnp.int32, (count, 112), 0) + first
        frame = lax.broadcasted_iota(jnp.int32, (count, 112), 1)
        hit = (row.astype(F32) == pos_lanes[b : b + 1, :]) & (frame < lives[b])
        return jnp.where(hit, 1.0, 0.0).astype(BF16)

    def unplace(b):
        frame = lax.broadcasted_iota(jnp.int32, (112, 160), 0)
        row = lax.broadcasted_iota(jnp.int32, (112, 160), 1)
        hit = (row.astype(F32) == pos_sub[:, b : b + 1]) & (frame < lives[b])
        return jnp.where(hit, 1.0, 0.0).astype(BF16)

    def split_heads(tile):
        return jnp.concatenate([jnp.where(low, tile, 0.0), jnp.where(low, 0.0, tile)], axis=0).astype(BF16)

    weight_copies[0].wait()

    attp = [jnp.zeros((160, 128), F32) for _ in range(3)]
    pooled_audio = jnp.zeros((40, 1280), F32)

    def forward(b, attp, pooled_audio):
        arrive(audio_copies[b])
        tiles = []
        for s in (0, 2):
            left = aud[s, b, 224:288].astype(F32)
            right = aud[s + 1, b, 224:288].astype(F32)
            top = jnp.where(low_half, left, pltpu.roll(right, 64, 1))
            bottom = jnp.where(low_half, pltpu.roll(left, 64, 1), right)
            tiles.append(aud[s, b, 0:112].astype(F32))
            tiles.append(aud[s, b, 112:224].astype(F32))
            tiles.append(jnp.concatenate([top, bottom[0:48]], axis=0))
            tiles.append(aud[s + 1, b, 0:112].astype(F32))
            tiles.append(aud[s + 1, b, 112:224].astype(F32))
        frames = jnp.concatenate(tiles, axis=1)
        pooled_audio = pooled_audio + dot(place(b, 40 * x, 40), frames.astype(BF16))
        normed = normalize(frames)[0].astype(BF16)
        nb[112 * b : 112 * b + 112, :] = normed
        for j in range(3):
            pj[j, :, 0:320] = dot_nt(normed, wq[j])
        k_s[b] = pj[1].astype(BF16)
        v_s[b] = pj[2].astype(BF16)
        key_limit = jnp.maximum(lives[b], 1)
        placed = place(b, 0, 160)
        for g in range(3):
            cols = slice(128 * g, 128 * g + 128)
            q_tile = pj[0, :, cols]
            if g < 2:
                queries = split_heads(q_tile)
                q2s[b, g] = queries
            else:
                queries = q_tile.astype(BF16)
                qr_s[b] = queries
            rows = queries.shape[0]
            scores = dot_nt(queries, k_s[b, :, cols]) * SCALING
            key = lax.broadcasted_iota(jnp.int32, (rows, 112), 1)
            scores = jnp.where(key < key_limit, scores, -1e30)
            powered = jnp.exp(scores - jnp.max(scores, axis=-1, keepdims=True))
            weights = powered * (1.0 / jnp.sum(powered, axis=-1, keepdims=True))
            prob[b, g, 0:rows] = weights
            scores_t = dot_nt(k_s[b, :, cols], queries) * SCALING
            key_t = lax.broadcasted_iota(jnp.int32, (112, rows), 0)
            scores_t = jnp.where(key_t < key_limit, scores_t, -1e30)
            powered_t = jnp.exp(scores_t - jnp.max(scores_t, axis=0, keepdims=True))
            prob_t[b, g, :, 0:rows] = powered_t * (1.0 / jnp.sum(powered_t, axis=0, keepdims=True))
            mixed = dot(weights.astype(BF16), v_s[b, :, cols])
            if g < 2:
                mixed = jnp.where(low, mixed[0:112], mixed[112:224])
            attp[g] = attp[g] + dot(placed, mixed.astype(BF16))
        return attp, pooled_audio

    weight_copies[2].wait()
    arrive(cot_copies)
    row_grads = jnp.concatenate([unfold(cot_r[s], 7) for s in range(4)], axis=0).astype(BF16)
    adapter_terms = dot_nt(row_grads, wp[...])
    for t in range(4):
        gt_s[t] = fold(adapter_terms[40 * t : 40 * t + 40], 640, 0)
    attp, pooled_audio = forward(0, attp, pooled_audio)
    leave(audio_copies[1] + audio_copies[2])
    gt_copies = to_peers(4, lambda there: gt_s.at[there], lambda k: gt_r.at[k - 1])
    attp, pooled_audio = forward(1, attp, pooled_audio)
    attp, pooled_audio = forward(2, attp, pooled_audio)
    attp = [part.astype(BF16) for part in attp]
    for g in range(2):
        attp_s[c, :, 128 * g : 128 * g + 128] = attp[g]
    attp_s[c, :, 256:384] = pltpu.roll(attp[2].astype(F32), 64, 1).astype(BF16)
    weight_copies[1].wait()
    head_terms = (
        dot(attp[0], wo[0:128]) + dot(attp[1], wo[128:256]) + dot(attp[2][:, 0:64], wo[256:320])
    )
    for t in range(4):
        t_s[t] = fold(head_terms[40 * t : 40 * t + 40], 640, 0)
    t_copies = to_peers(5, lambda there: t_s.at[there], lambda k: t_r.at[k - 1])

    nt[c] = nb[...].T
    for b in range(3):
        up_s[b] = unplace(b)
    core_copies = [to_core(0, nt.at[c], nt.at[c]), to_core(1, attp_s.at[c], attp_s.at[c])]

    arrive(gt_copies)
    adapted_grad = gt_s[x].astype(F32)
    for k in range(3):
        adapted_grad = adapted_grad + gt_r[k].astype(F32)
    adapted_grad = unfold(adapted_grad.astype(BF16), 2)

    arrive(t_copies)
    attention = t_s[x].astype(F32)
    for k in range(3):
        attention = attention + t_r[k].astype(F32)
    attention = jnp.concatenate([attention[0:40], attention[40:80]], axis=1)
    normed_rows, inverse = normalize((pooled_audio + attention) * 0.5)
    pooled_grad = inverse * (
        adapted_grad
        - jnp.mean(adapted_grad, axis=-1, keepdims=True)
        - normed_rows * jnp.mean(adapted_grad * normed_rows, axis=-1, keepdims=True)
    )
    ag_a[x] = fold(pooled_grad * 0.5, 640, 0)
    ag_copies = to_peers(6, lambda there: ag_a.at[x], lambda k: ag_a.at[x])
    ad_a[x] = fold(normed_rows, 640, 0)
    arrive(ag_copies)
    attention_grad = jnp.concatenate([unfold(ag_a[s], 2) for s in range(4)], axis=0).astype(BF16)
    mgp[:, 0:320] = dot_nt(attention_grad, wo[...]).astype(BF16)
    pairs = [(b, g) for b in range(3) for g in range(3)]
    grads, prob_grads, prob_grads_t, halves, halves_t = {}, {}, {}, {}, {}
    for b in range(3):
        mixed_grad = dot(up_s[b], mgp[...])
        for g in range(3):
            tile = mixed_grad[:, 128 * g : 128 * g + 128]
            grads[b, g] = split_heads(tile) if g < 2 else tile.astype(BF16)
    for b, g in pairs:
        cols = slice(128 * g, 128 * g + 128)
        prob_grads[b, g] = dot_nt(grads[b, g], v_s[b, :, cols])
        prob_grads_t[b, g] = dot_nt(v_s[b, :, cols], grads[b, g])
    for b, g in pairs:
        count = 224 if g < 2 else 112
        weights, weights_t = prob[b, g, 0:count], prob_t[b, g, :, 0:count]
        inner = jnp.sum(weights * prob_grads[b, g], axis=-1, keepdims=True)
        inner_t = jnp.sum(weights_t * prob_grads_t[b, g], axis=0, keepdims=True)
        halves[b, g] = (weights * (prob_grads[b, g] - inner)).astype(BF16)
        halves_t[b, g] = (weights_t * (prob_grads_t[b, g] - inner_t)).astype(BF16)
    for b in range(3):
        rows = slice(112 * b, 112 * b + 112)
        for g in range(3):
            cols = slice(128 * g, 128 * g + 128)
            count = 224 if g < 2 else 112
            query_grad = dot(halves[b, g], k_s[b, :, cols])
            if g < 2:
                query_grad = jnp.where(low, query_grad[0:112], query_grad[112:224])
            query_grad = query_grad * SCALING
            key_grad = dot(halves_t[b, g], q2s[b, g] if g < 2 else qr_s[b]) * SCALING
            value_grad = dot(prob_t[b, g, :, 0:count].astype(BF16), grads[b, g])
            local[1, rows, cols] = value_grad.astype(BF16)
            if g < 2:
                local[0, rows, cols] = query_grad.astype(BF16)
                local[0, rows, 256 + 128 * g : 384 + 128 * g] = key_grad.astype(BF16)
            else:
                local[0, rows, 512:640] = (query_grad + pltpu.roll(key_grad, 64, 1)).astype(BF16)
    agt[c] = attention_grad.T
    core_copies.append(to_core(2, local.at[1 - c], other))
    core_copies.append(to_core(3, agt.at[c], agt.at[c]))
    ad_copies = to_peers(7, lambda there: ad_a.at[x], lambda k: ad_a.at[x])

    def start_embeds():
        arrive(ad_copies)
        adapted = jnp.concatenate([unfold(ad_a[s], 2) for s in range(4)], axis=0).astype(BF16)
        adapter_rows = dot(adapted, wp[...])
        for t in range(4):
            e_s[t] = fold(adapter_rows[40 * t : 40 * t + 40], 128, 8)
        e_r[x] = e_s[x]
        return to_peers(8, lambda there: e_s.at[there], lambda k: e_r.at[x])

    def finish_embeds(copies):
        arrive(copies)
        for s in range(4):
            emb[:, 896 * s : 896 * s + 896] = unfold(e_r[s], 7).astype(BF16)
        copy = pltpu.make_async_copy(emb, embeds, w_sem.at[5])
        copy.start()
        return copy

    def blocks(order, step):
        y_before = [letter for letter in order[:step] if letter in "AB"]
        z_done = any(letter in "ab" for letter in order[:step])
        letter = order[step]
        if letter in "AB":
            near = y ^ (1 if letter == "A" else 3)
            beyond = y ^ (3 if letter == "A" else 1)
            sides = (par, par) if z_done else (None, None)
            if y_before:
                return [near], [y], sides
            return [y ^ 2, near], [beyond, y], sides
        held = [y ^ 2, y ^ 1, y ^ 3, y]
        if len(y_before) == 1:
            held = [y ^ (3 if y_before[0] == "A" else 1), y]
        elif len(y_before) == 2:
            held = [y]
        return held, held, (1 - par, par)

    def begin(p, step, only=None):
        tile, row, count, order = PARTS[p]
        send, _, (side, _) = blocks(order, step)
        landing = r_bufs[3 * p + step]
        copies = []
        for i, block in enumerate(send):
            if only is not None and i != only:
                continue
            pick = pl.ds(0, 2) if side is None else pl.ds(side, 1)
            copy = pltpu.make_async_remote_copy(
                src_ref=total.at[block, tile, pick, pl.ds(row, count)],
                dst_ref=landing.at[i],
                send_sem=r_send.at[p, step, i],
                recv_sem=r_recv.at[p, step, i],
                device_id=partner[order[step]],
                device_id_type=MESH,
            )
            copy.start()
            copies.append(copy)
        started.extend(copies)
        return copies

    def end(p, step, copies):
        tile, row, count, order = PARTS[p]
        _, keep, (_, side) = blocks(order, step)
        landing = r_bufs[3 * p + step]
        rows = pl.ds(row, count)
        arrive(copies)
        for i, block in enumerate(keep):
            if step == 2:
                final[tile, rows] = total[block, tile, par, rows].astype(F32) + landing[i, 0].astype(F32)
            elif side is None:
                for k in range(2):
                    kept = total[block, tile, k, rows].astype(F32) + landing[i, k].astype(F32)
                    total[block, tile, k, rows] = kept.astype(BF16)
            else:
                kept = total[block, tile, side, rows].astype(F32) + landing[i, 0].astype(F32)
                total[block, tile, side, rows] = kept.astype(BF16)

    arrive(core_copies)
    flying = {(p, 0): [] for p in range(len(PARTS))}
    turns = (y ^ 2, y ^ 1, y ^ 3, y)
    for turn, yy in enumerate(turns):
        rows = pl.ds(pl.multiple_of(320 * yy, 64), 320)

        def store(tile, values):
            for side in range(2):
                total[yy, tile, side] = jnp.concatenate(
                    [values[40 * i : 40 * i + 40] for i in range(side, 8, 2)], axis=0
                ).astype(BF16)

        @pl.when(c == 0)
        def _():
            part = dot(nt[0, rows], local[0]) + dot(nt[1, rows], other[...])
            for t in range(5):
                store(t, part[:, 128 * t : 128 * t + 128])

        @pl.when(c == 1)
        def _():
            value_part = dot(nt[1, rows], local[1, :, 0:384]) + dot(nt[0, rows], other[:, 0:384])
            out_part = dot(agt[0, rows], attp_s[0]) + dot(agt[1, rows], attp_s[1])
            store(0, value_part[:, 0:128])
            store(1, value_part[:, 128:256])
            store(2, out_part[:, 0:128])
            store(3, out_part[:, 128:256])
            store(4, value_part[:, 256:384] + out_part[:, 256:384])

        for p in WAVES[0]:
            slots = {"A": (0, 1, None, None), "B": (0, None, 1, None)}.get(PARTS[p][3][0], (0, 1, 2, 3))
            if slots[turn] is not None:
                flying[p, 0] += begin(p, 0, slots[turn])
    z_copies = []

    def last_exchange(wave):
        tiles, first, count = Z_GROUPS[wave]
        fill = count - 40 * len(tiles)
        for j in range(4):
            pieces = [final[t, 40 * j : 40 * j + 40] for t in tiles]
            if fill:
                pieces.append(jnp.zeros((fill, 128), F32))
            z_s[j, first : first + count] = jnp.concatenate(pieces, axis=0).astype(BF16)
        for k in (1, 2, 3):
            copy = pltpu.make_async_remote_copy(
                src_ref=z_s.at[zp ^ k, pl.ds(first, count)],
                dst_ref=z_r.at[k - 1, pl.ds(first, count)],
                send_sem=z_send.at[wave, k - 1],
                recv_sem=z_recv.at[wave, k - 1],
                device_id=z_peers[k - 1],
                device_id_type=MESH,
            )
            copy.start()
            z_copies.append(copy)
            started.append(copy)

    def step(wave, number):
        for p in WAVES[wave]:
            end(p, number - 1, flying[p, number - 1])
            if number < 3:
                flying[p, number] = begin(p, number)

    for p in WAVES[0]:
        leave(flying[p, 0])
    for p in WAVES[1]:
        flying[p, 0] = begin(p, 0)
    step(0, 1)
    step(1, 1)
    embed_copies = start_embeds()
    step(0, 2)
    step(1, 2)
    step(0, 3)
    last_exchange(0)
    step(1, 3)
    last_exchange(1)
    embeds_copy = finish_embeds(embed_copies)
    arrive(z_copies)
    mine = z_s[zp].astype(F32)
    for k in range(3):
        mine = mine + z_r[k].astype(F32)
    first_core = c == 0
    own_tiles = []
    f_s[...] = jnp.zeros_like(f_s)
    for t in range(5):
        rows = mine[TILE_ROWS[t] : TILE_ROWS[t] + 40]
        early, late = rows[0:20], rows[20:40]
        own_tiles.append(jnp.where(first_core, early, late))
        f_s[t, 0:20] = jnp.where(first_core, late, early).astype(BF16)
    arrive([to_core(4, f_s, f_r)])
    for t in range(5):
        got = f_r[t, 0:20].astype(F32)
        left = jnp.where(first_core, own_tiles[t], got)
        right = jnp.where(first_core, got, own_tiles[t])
        if t < 2:
            cols = slice(128 * t, 128 * t + 128)
            grad_qkv[0, :, cols] = left
            grad_qkv[2, :, cols] = right
        elif t < 4:
            cols = slice(128 * t - 256, 128 * t - 128)
            grad_qkv[1, :, cols] = left
            grad_out[:, cols] = right
        else:
            grad_qkv[0, :, 256:320] = left[:, 0:64]
            grad_qkv[1, :, 256:320] = left[:, 64:128]
            grad_qkv[2, :, 256:320] = right[:, 0:64]
            grad_out[:, 256:320] = right[:, 64:128]
    embeds_copy.wait()
    for copy in started:
        copy.wait_send()


def call(counts, lengths, positions, audio, cotangent, w_qkv, w_out, w_proj):
    vmem, dma = pltpu.VMEM, pltpu.SemaphoreType.DMA
    scratch = [
        vmem((3, 320, 1280), BF16),
        vmem((320, 1280), BF16),
        vmem((1280, 896), BF16),
        vmem((3, 128, 384), F32),
        vmem((4, 3, 288, 128), BF16),
        vmem((4, 288, 128), BF16),
        vmem((4, 288, 128), BF16),
        vmem((4, 80, 640), BF16),
        vmem((3, 80, 640), BF16),
        vmem((4, 80, 640), BF16),
        vmem((3, 80, 640), BF16),
        vmem((4, 80, 640), BF16),
        vmem((4, 80, 640), BF16),
        vmem((4, 288, 128), BF16),
        vmem((4, 288, 128), BF16),
        vmem((40, 3584), BF16),
        vmem((3, 100, 320), BF16),
        vmem((40, 3584), BF16),
        vmem((336, 1280), BF16),
        vmem((2, 1280, 336), BF16),
        vmem((3, 112, 384), F32),
        vmem((3, 2, 224, 128), BF16),
        vmem((3, 112, 128), BF16),
        vmem((3, 112, 384), BF16),
        vmem((3, 112, 384), BF16),
        vmem((3, 3, 224, 112), F32),
        vmem((2, 160, 384), BF16),
        vmem((2, 1280, 160), BF16),
        vmem((160, 384), BF16),
        vmem((2, 336, 640), BF16),
        vmem((336, 640), BF16),
        vmem((4, 5, 2, 160, 128), BF16),
        vmem((5, 160, 128), F32),
        vmem((3, 3, 112, 224), F32),
        vmem((3, 112, 160), BF16),
        vmem((4, 208, 128), BF16),
        vmem((3, 208, 128), BF16),
        vmem((5, 32, 128), BF16),
        vmem((5, 32, 128), BF16),
        dma((6,)),
        dma((9, 3)),
        dma((9, 3)),
        dma((5,)),
        dma((5,)),
        dma((len(PARTS), 3, 4)),
        dma((len(PARTS), 3, 4)),
        dma((2, 3)),
        dma((2, 3)),
    ]
    assert len(scratch) == 48
    scratch += [vmem(received_shape(part, step), BF16) for part in PARTS for step in range(3)]
    in_vmem = pl.BlockSpec(memory_space=pltpu.VMEM)
    in_smem = pl.BlockSpec(memory_space=pltpu.SMEM)
    anywhere = pl.BlockSpec(memory_space=pl.ANY)
    return pl.pallas_call(
        kernel,
        out_shape=(
            jax.ShapeDtypeStruct((40, 3584), BF16),
            jax.ShapeDtypeStruct((3, 20, 320), F32),
            jax.ShapeDtypeStruct((20, 320), F32),
        ),
        in_specs=[in_smem, in_smem, in_vmem] + [anywhere] * 5,
        out_specs=(anywhere, in_vmem, in_vmem),
        scratch_shapes=scratch,
        compiler_params=pltpu.CompilerParams(
            collective_id=0, has_side_effects=True, vmem_limit_bytes=60 * 2**20
        ),
        name="sublayer",
    )(counts, lengths, positions, audio, cotangent, w_qkv, w_out, w_proj)


def write_out(*refs):
    for source, target in zip(refs[:3], refs[3:]):
        target[...] = source[...]


def results(*parts):
    in_vmem = pl.BlockSpec(memory_space=pltpu.VMEM)
    return pl.pallas_call(
        write_out,
        out_shape=tuple(jax.ShapeDtypeStruct(part.shape, part.dtype) for part in parts),
        in_specs=[in_vmem] * 3,
        out_specs=(in_vmem,) * 3,
        name="results",
    )(*parts)


def shards(audio, counts, lengths, positions, w_qkv, w_out, w_proj, cotangent):
    embeds, grad_qkv, grad_out = call(
        counts, lengths, positions, audio, cotangent, jnp.swapaxes(w_qkv, 1, 2), w_out, w_proj
    )
    embeds, grad_qkv, grad_out = results(embeds, grad_qkv, grad_out)
    return embeds, grad_qkv, grad_out.T


def solution(mesh):
    in_specs = (
        P("dp", None, "seq"),
        P("dp"),
        P("dp"),
        P("dp", None),
        P(None, None, "seq"),
        P("seq", None),
        P(None, "seq"),
        P(("dp", "seq"), None),
    )
    out_specs = (P(("dp", "seq"), None), P(None, "dp", "seq"), P("seq", "dp"))
    return jax.shard_map(shards, mesh=mesh, in_specs=in_specs, out_specs=out_specs, check_vma=False)
```

```python
import jax
import jax.numpy as jnp
from jax import lax
from jax.experimental import pallas as pl
from jax.experimental.pallas import tpu as pltpu
from jax.sharding import PartitionSpec as P

MESH = pl.DeviceIdType.MESH
F32 = jnp.float32
BF16 = jnp.bfloat16
EPSILON = 1e-05
SCALING = 0.125
PARTS = (
    (0, 0, 80, "AaB"),
    (0, 80, 80, "BbA"),
    (1, 0, 80, "aAB"),
    (1, 80, 80, "bBA"),
    (4, 0, 48, "AaB"),
    (4, 48, 48, "BbA"),
    (4, 96, 32, "aAB"),
    (4, 128, 32, "bBA"),
    (2, 0, 80, "AaB"),
    (2, 80, 80, "BbA"),
    (3, 0, 80, "aAB"),
    (3, 80, 80, "bBA"),
)
WAVES = ((0, 1, 2, 3, 4, 5, 6, 7), (8, 9, 10, 11))
Z_GROUPS = (((0, 1, 4), 0, 128), ((2, 3), 128, 80))
TILE_ROWS = {0: 0, 1: 40, 4: 80, 2: 128, 3: 168}


def dot(a, b):
    return jnp.dot(a, b, preferred_element_type=F32)


def dot_nt(a, b):
    return lax.dot_general(a, b, (((1,), (1,)), ((), ())), preferred_element_type=F32)


def dot_tn(a, b):
    return lax.dot_general(a, b, (((0,), (0,)), ((), ())), preferred_element_type=F32)


def fold(rows, width, extra):
    pieces = [rows[:, i : i + width] for i in range(0, rows.shape[1], width)]
    if extra:
        pieces.append(jnp.zeros((extra, width), F32))
    return jnp.concatenate(pieces, axis=0).astype(BF16)


def unfold(folded, count):
    wide = folded.astype(F32)
    return jnp.concatenate([wide[40 * i : 40 * i + 40] for i in range(count)], axis=1)


def normalize(rows):
    centred = rows - jnp.mean(rows, axis=-1, keepdims=True)
    inverse = lax.rsqrt(jnp.mean(centred * centred, axis=-1, keepdims=True) + EPSILON)
    return centred * inverse, inverse


def received_shape(part, step):
    _, _, rows, order = part
    before = order[:step]
    y_done = sum(letter in "AB" for letter in before)
    z_done = any(letter in "ab" for letter in before)
    if order[step] in "AB":
        return (2 if y_done == 0 else 1, 1 if z_done else 2, rows, 128)
    return ((4, 2, 1)[y_done], 1, rows, 128)


def kernel(*refs):
    (counts, lengths, positions, audio, cotangent, w_qkv, w_out, w_proj) = refs[:8]
    embeds, grad_qkv, grad_out = refs[8:11]
    (
        wq, wo, wp, tmp, aud, cot_s, cot_r, gt_s, gt_r, t_s, t_r, ag_a, ad_a, e_s, e_r, cot_v, aud_v, emb,
        nb, nt, pj, q2s, qr_s, k_s, v_s, prob, attp_s, agt, mgp, local, other, total, final, prob_t, up_s,
        z_s, z_r, f_s, f_r, w_sem, x_send, x_recv, c_send, c_recv, r_send, r_recv, z_send, z_recv,
    ) = refs[11 : 11 + 48]
    r_bufs = refs[11 + 48 :]

    dp = lax.axis_index("dp")
    x = lax.axis_index("seq")
    y = dp // 16
    z = (dp // 2) % 8
    c = dp % 2
    par = z % 2
    zp = z // 2

    def at(yy, zz, cc):
        return (yy * 16 + zz * 2 + cc, x)

    peers = [(dp, (x + k) % 4) for k in (1, 2, 3)]
    partner = {
        "A": at(y ^ 1, z, c),
        "B": at(y ^ 3, z, c),
        "a": at(y, z ^ 1, c),
        "b": at(y, (z + 7 + 2 * par) % 8, c),
    }
    core_peer = at(y, z, 1 - c)
    z_peers = [at(y, z ^ (2 * k), c) for k in (1, 2, 3)]

    input_copies = [
        pltpu.make_async_copy(src, dst, w_sem.at[3 + i])
        for i, (src, dst) in enumerate(((cotangent, cot_v), (audio, aud_v)))
    ]
    weight_copies = [
        pltpu.make_async_copy(src, dst, w_sem.at[i])
        for i, (src, dst) in enumerate(((w_qkv, wq), (w_out, wo), (w_proj, wp)))
    ]
    for copy in input_copies:
        copy.start()

    barrier = pltpu.get_barrier_semaphore()
    everyone = peers + [core_peer] + list(partner.values()) + z_peers
    for device in everyone:
        pl.semaphore_signal(barrier, inc=1, device_id=device, device_id_type=MESH)

    for i in (2, 0, 1):
        weight_copies[i].start()

    lane = lax.broadcasted_iota(jnp.int32, (112, 128), 1)
    low = lane < 64
    tmp[...] = jnp.zeros_like(tmp)
    pj[...] = jnp.zeros_like(pj)
    mgp[...] = jnp.zeros_like(mgp)
    local[1, :, 384:640] = jnp.zeros((336, 256), BF16)
    input_copies[0].wait()
    cot_rows = cot_v[...].astype(F32)
    for t in range(4):
        cot_s[t] = fold(cot_rows[:, 896 * t : 896 * t + 896], 128, 8)
    cot_r[x] = cot_s[x]

    def pack_audio(b):
        tmp[b, 0:100, 0:320] = aud_v[b].astype(F32)
        first, second, third = (tmp[b, 0:104, 128 * i : 128 * i + 128] for i in range(3))
        second_turned = pltpu.roll(second, 64, 1)
        blank = jnp.zeros((8, 128), F32)
        even_low = jnp.concatenate([third[56:104], blank], axis=0)
        odd_low = jnp.concatenate([first[56:104], blank], axis=0)
        packed = third[0:56] + pltpu.roll(even_low, 64, 1)
        packed_odd = jnp.where(low[0:56], first[0:56], pltpu.roll(odd_low, 64, 1))
        even = jnp.concatenate([first, second, packed, blank], axis=0)
        odd = jnp.concatenate(
            [
                jnp.where(low[0:104], pltpu.roll(first, 64, 1), second_turned),
                jnp.where(low[0:104], second_turned, pltpu.roll(third, 64, 1)),
                packed_odd,
                blank,
            ],
            axis=0,
        )
        aud[x, b] = jnp.where(x % 2 == 0, even, odd).astype(BF16)

    input_copies[1].wait()
    pack_audio(0)

    pl.semaphore_wait(barrier, len(everyone))

    started = []
    def to_peers(slot, source, target, steps=(1, 2, 3)):
        copies = []
        for k in steps:
            there = (x + k) % 4
            copy = pltpu.make_async_remote_copy(
                src_ref=source(there),
                dst_ref=target(k),
                send_sem=x_send.at[slot, k - 1],
                recv_sem=x_recv.at[slot, k - 1],
                device_id=(dp, there),
                device_id_type=MESH,
            )
            copy.start()
            copies.append(copy)
        started.extend(copies)
        return copies

    def to_core(slot, source, target):
        copy = pltpu.make_async_remote_copy(
            src_ref=source,
            dst_ref=target,
            send_sem=c_send.at[slot],
            recv_sem=c_recv.at[slot],
            device_id=core_peer,
            device_id_type=MESH,
        )
        copy.start()
        started.append(copy)
        return copy

    def leave(copies):
        for copy in copies:
            copy.wait_send()
            started[:] = [other_copy for other_copy in started if other_copy is not copy]

    def arrive(copies):
        for copy in copies:
            copy.wait_recv()

    audio_copies, passed = [], []
    cot_copies = to_peers(3, lambda there: cot_s.at[there], lambda k: cot_r.at[x])

    def send_audio(b):
        block = aud.at[x, b]
        audio_copies.append(to_peers(b, lambda there: block, lambda k: block, (1, 3)))

    def pass_audio(b):
        arrive(audio_copies[b])
        top = aud.at[(x + 3) % 4, b, pl.ds(0, 144)]
        bottom = aud.at[(x + 1) % 4, b, pl.ds(144, 128)]
        passed.append(
            to_peers(9 + b, lambda there: top, lambda k: top, (1,))
            + to_peers(9 + b, lambda there: bottom, lambda k: bottom, (3,))
        )

    send_audio(0)
    pack_audio(1)
    pack_audio(2)
    leave(cot_copies)
    send_audio(1)
    send_audio(2)

    pos_pad = jnp.concatenate([positions[...].astype(F32), jnp.zeros((13, 50), F32)], axis=0).astype(BF16)
    frame_row = lax.broadcasted_iota(jnp.int32, (50, 112), 0)
    frame_col = lax.broadcasted_iota(jnp.int32, (50, 112), 1)
    spread = jnp.where(frame_row == frame_col // 2, 1.0, 0.0).astype(BF16)
    pos_lanes = dot(pos_pad, spread)
    frame_row_t = lax.broadcasted_iota(jnp.int32, (112, 50), 0)
    frame_col_t = lax.broadcasted_iota(jnp.int32, (112, 50), 1)
    spread_t = jnp.where(frame_row_t // 2 == frame_col_t, 1.0, 0.0).astype(BF16)
    pos_sub = dot_nt(spread_t, pos_pad)
    lives = [jnp.where(b < counts[0], lengths[b], 0) for b in range(3)]

    def place(b, first, count):
        row = lax.broadcasted_iota(jnp.int32, (count, 112), 0) + first
        frame = lax.broadcasted_iota(jnp.int32, (count, 112), 1)
        hit = (row.astype(F32) == pos_lanes[b : b + 1, :]) & (frame < lives[b])
        return jnp.where(hit, 1.0, 0.0).astype(BF16)

    def unplace(b):
        frame = lax.broadcasted_iota(jnp.int32, (112, 160), 0)
        row = lax.broadcasted_iota(jnp.int32, (112, 160), 1)
        hit = (row.astype(F32) == pos_sub[:, b : b + 1]) & (frame < lives[b])
        return jnp.where(hit, 1.0, 0.0).astype(BF16)

    def split_heads(tile):
        return jnp.concatenate([jnp.where(low, tile, 0.0), jnp.where(low, 0.0, tile)], axis=0).astype(BF16)

    weight_copies[0].wait()

    attp = [jnp.zeros((160, 128), F32) for _ in range(3)]
    pooled_audio = jnp.zeros((40, 1280), F32)

    def forward(b, attp, pooled_audio):
        arrive(passed[b])
        tiles = []
        for s in (0, 2):
            left = aud[s, b].astype(F32)
            right = aud[s + 1, b].astype(F32)
            left_rest, right_rest = left[208:264], right[208:264]
            top = jnp.where(low[0:56], left_rest, pltpu.roll(right_rest, 64, 1))
            bottom = jnp.where(low[0:56], pltpu.roll(left_rest, 64, 1), right_rest)
            middle = jnp.concatenate([top, bottom[0:48]], axis=0)
            for tile in (left[0:104], left[104:208], middle, right[0:104], right[104:208]):
                tiles.append(jnp.concatenate([tile, jnp.zeros((8, 128), F32)], axis=0))
        frames = jnp.concatenate(tiles, axis=1)
        pooled_audio = pooled_audio + dot(place(b, 40 * x, 40), frames.astype(BF16))
        normed = normalize(frames)[0].astype(BF16)
        nb[112 * b : 112 * b + 112, :] = normed
        for j in range(3):
            pj[j, :, 0:320] = dot_nt(normed, wq[j])
        k_s[b] = pj[1].astype(BF16)
        v_s[b] = pj[2].astype(BF16)
        key_limit = jnp.maximum(lives[b], 1)
        placed = place(b, 0, 160)
        for g in range(3):
            cols = slice(128 * g, 128 * g + 128)
            q_tile = pj[0, :, cols]
            if g < 2:
                queries = split_heads(q_tile)
                q2s[b, g] = queries
            else:
                queries = q_tile.astype(BF16)
                qr_s[b] = queries
            rows = queries.shape[0]
            scores = dot_nt(queries, k_s[b, :, cols]) * SCALING
            key = lax.broadcasted_iota(jnp.int32, (rows, 112), 1)
            scores = jnp.where(key < key_limit, scores, -1e30)
            powered = jnp.exp(scores - jnp.max(scores, axis=-1, keepdims=True))
            weights = powered * (1.0 / jnp.sum(powered, axis=-1, keepdims=True))
            prob[b, g, 0:rows] = weights
            scores_t = dot_nt(k_s[b, :, cols], queries) * SCALING
            key_t = lax.broadcasted_iota(jnp.int32, (112, rows), 0)
            scores_t = jnp.where(key_t < key_limit, scores_t, -1e30)
            powered_t = jnp.exp(scores_t - jnp.max(scores_t, axis=0, keepdims=True))
            prob_t[b, g, :, 0:rows] = powered_t * (1.0 / jnp.sum(powered_t, axis=0, keepdims=True))
            mixed = dot(weights.astype(BF16), v_s[b, :, cols])
            if g < 2:
                mixed = jnp.where(low, mixed[0:112], mixed[112:224])
            attp[g] = attp[g] + dot(placed, mixed.astype(BF16))
        return attp, pooled_audio

    weight_copies[2].wait()
    pass_audio(0)
    arrive(cot_copies)
    row_grads = jnp.concatenate([unfold(cot_r[s], 7) for s in range(4)], axis=0).astype(BF16)
    adapter_terms = dot_nt(row_grads, wp[...])
    for t in range(4):
        gt_s[t] = fold(adapter_terms[40 * t : 40 * t + 40], 640, 0)
    pass_audio(1)
    pass_audio(2)
    attp, pooled_audio = forward(0, attp, pooled_audio)
    leave(passed[1] + passed[2])
    gt_copies = to_peers(4, lambda there: gt_s.at[there], lambda k: gt_r.at[k - 1])
    attp, pooled_audio = forward(1, attp, pooled_audio)
    attp, pooled_audio = forward(2, attp, pooled_audio)
    attp = [part.astype(BF16) for part in attp]
    for g in range(2):
        attp_s[c, :, 128 * g : 128 * g + 128] = attp[g]
    attp_s[c, :, 256:384] = pltpu.roll(attp[2].astype(F32), 64, 1).astype(BF16)
    weight_copies[1].wait()
    head_terms = (
        dot(attp[0], wo[0:128]) + dot(attp[1], wo[128:256]) + dot(attp[2][:, 0:64], wo[256:320])
    )
    for t in range(4):
        t_s[t] = fold(head_terms[40 * t : 40 * t + 40], 640, 0)
    t_copies = to_peers(5, lambda there: t_s.at[there], lambda k: t_r.at[k - 1])

    nt[c] = nb[...].T
    for b in range(3):
        up_s[b] = unplace(b)
    core_copies = [to_core(0, nt.at[c], nt.at[c]), to_core(1, attp_s.at[c], attp_s.at[c])]

    arrive(gt_copies)
    adapted_grad = gt_s[x].astype(F32)
    for k in range(3):
        adapted_grad = adapted_grad + gt_r[k].astype(F32)
    adapted_grad = unfold(adapted_grad.astype(BF16), 2)

    arrive(t_copies)
    attention = t_s[x].astype(F32)
    for k in range(3):
        attention = attention + t_r[k].astype(F32)
    attention = jnp.concatenate([attention[0:40], attention[40:80]], axis=1)
    normed_rows, inverse = normalize((pooled_audio + attention) * 0.5)
    pooled_grad = inverse * (
        adapted_grad
        - jnp.mean(adapted_grad, axis=-1, keepdims=True)
        - normed_rows * jnp.mean(adapted_grad * normed_rows, axis=-1, keepdims=True)
    )
    ag_a[x] = fold(pooled_grad * 0.5, 640, 0)
    ag_copies = to_peers(6, lambda there: ag_a.at[x], lambda k: ag_a.at[x])
    ad_a[x] = fold(normed_rows, 640, 0)
    arrive(ag_copies)
    attention_grad = jnp.concatenate([unfold(ag_a[s], 2) for s in range(4)], axis=0).astype(BF16)
    mgp[:, 0:320] = dot_nt(attention_grad, wo[...]).astype(BF16)
    pairs = [(b, g) for b in range(3) for g in range(3)]
    grads, prob_grads, prob_grads_t, halves, halves_t = {}, {}, {}, {}, {}
    for b in range(3):
        mixed_grad = dot(up_s[b], mgp[...])
        for g in range(3):
            tile = mixed_grad[:, 128 * g : 128 * g + 128]
            grads[b, g] = split_heads(tile) if g < 2 else tile.astype(BF16)
    for b, g in pairs:
        cols = slice(128 * g, 128 * g + 128)
        prob_grads[b, g] = dot_nt(grads[b, g], v_s[b, :, cols])
        prob_grads_t[b, g] = dot_nt(v_s[b, :, cols], grads[b, g])
    for b, g in pairs:
        count = 224 if g < 2 else 112
        weights, weights_t = prob[b, g, 0:count], prob_t[b, g, :, 0:count]
        inner = jnp.sum(weights * prob_grads[b, g], axis=-1, keepdims=True)
        inner_t = jnp.sum(weights_t * prob_grads_t[b, g], axis=0, keepdims=True)
        halves[b, g] = (weights * (prob_grads[b, g] - inner)).astype(BF16)
        halves_t[b, g] = (weights_t * (prob_grads_t[b, g] - inner_t)).astype(BF16)
    for b in range(3):
        rows = slice(112 * b, 112 * b + 112)
        for g in range(3):
            cols = slice(128 * g, 128 * g + 128)
            count = 224 if g < 2 else 112
            query_grad = dot(halves[b, g], k_s[b, :, cols])
            if g < 2:
                query_grad = jnp.where(low, query_grad[0:112], query_grad[112:224])
            query_grad = query_grad * SCALING
            key_grad = dot(halves_t[b, g], q2s[b, g] if g < 2 else qr_s[b]) * SCALING
            value_grad = dot(prob_t[b, g, :, 0:count].astype(BF16), grads[b, g])
            local[1, rows, cols] = value_grad.astype(BF16)
            if g < 2:
                local[0, rows, cols] = query_grad.astype(BF16)
                local[0, rows, 256 + 128 * g : 384 + 128 * g] = key_grad.astype(BF16)
            else:
                local[0, rows, 512:640] = (query_grad + pltpu.roll(key_grad, 64, 1)).astype(BF16)
    agt[c] = attention_grad.T
    core_copies.append(to_core(2, local.at[1 - c], other))
    core_copies.append(to_core(3, agt.at[c], agt.at[c]))
    ad_copies = to_peers(7, lambda there: ad_a.at[x], lambda k: ad_a.at[x])

    def start_embeds():
        arrive(ad_copies)
        adapted = jnp.concatenate([unfold(ad_a[s], 2) for s in range(4)], axis=0).astype(BF16)
        adapter_rows = dot(adapted, wp[...])
        for t in range(4):
            e_s[t] = fold(adapter_rows[40 * t : 40 * t + 40], 128, 8)
        e_r[x] = e_s[x]
        return to_peers(8, lambda there: e_s.at[there], lambda k: e_r.at[x])

    def finish_embeds(copies):
        arrive(copies)
        for s in range(4):
            emb[:, 896 * s : 896 * s + 896] = unfold(e_r[s], 7).astype(BF16)
        copy = pltpu.make_async_copy(emb, embeds, w_sem.at[5])
        copy.start()
        return copy

    def blocks(order, step):
        y_before = [letter for letter in order[:step] if letter in "AB"]
        z_done = any(letter in "ab" for letter in order[:step])
        letter = order[step]
        if letter in "AB":
            near = y ^ (1 if letter == "A" else 3)
            beyond = y ^ (3 if letter == "A" else 1)
            sides = (par, par) if z_done else (None, None)
            if y_before:
                return [near], [y], sides
            return [y ^ 2, near], [beyond, y], sides
        held = [y ^ 2, y ^ 1, y ^ 3, y]
        if len(y_before) == 1:
            held = [y ^ (3 if y_before[0] == "A" else 1), y]
        elif len(y_before) == 2:
            held = [y]
        return held, held, (1 - par, par)

    def begin(p, step, only=None):
        tile, row, count, order = PARTS[p]
        send, _, (side, _) = blocks(order, step)
        landing = r_bufs[3 * p + step]
        copies = []
        for i, block in enumerate(send):
            if only is not None and i != only:
                continue
            pick = pl.ds(0, 2) if side is None else pl.ds(side, 1)
            copy = pltpu.make_async_remote_copy(
                src_ref=total.at[block, tile, pick, pl.ds(row, count)],
                dst_ref=landing.at[i],
                send_sem=r_send.at[p, step, i],
                recv_sem=r_recv.at[p, step, i],
                device_id=partner[order[step]],
                device_id_type=MESH,
            )
            copy.start()
            copies.append(copy)
        started.extend(copies)
        return copies

    def end(p, step, copies):
        tile, row, count, order = PARTS[p]
        _, keep, (_, side) = blocks(order, step)
        landing = r_bufs[3 * p + step]
        rows = pl.ds(row, count)
        arrive(copies)
        for i, block in enumerate(keep):
            if step == 2:
                final[tile, rows] = total[block, tile, par, rows].astype(F32) + landing[i, 0].astype(F32)
            elif side is None:
                for k in range(2):
                    kept = total[block, tile, k, rows].astype(F32) + landing[i, k].astype(F32)
                    total[block, tile, k, rows] = kept.astype(BF16)
            else:
                kept = total[block, tile, side, rows].astype(F32) + landing[i, 0].astype(F32)
                total[block, tile, side, rows] = kept.astype(BF16)

    arrive(core_copies)
    flying = {(p, 0): [] for p in range(len(PARTS))}
    turns = (y ^ 2, y ^ 1, y ^ 3, y)
    for turn, yy in enumerate(turns):
        rows = pl.ds(pl.multiple_of(320 * yy, 64), 320)

        def store(tile, values):
            for side in range(2):
                total[yy, tile, side] = jnp.concatenate(
                    [values[40 * i : 40 * i + 40] for i in range(side, 8, 2)], axis=0
                ).astype(BF16)

        @pl.when(c == 0)
        def _():
            part = dot(nt[0, rows], local[0]) + dot(nt[1, rows], other[...])
            for t in range(5):
                store(t, part[:, 128 * t : 128 * t + 128])

        @pl.when(c == 1)
        def _():
            value_part = dot(nt[1, rows], local[1, :, 0:384]) + dot(nt[0, rows], other[:, 0:384])
            out_part = dot(agt[0, rows], attp_s[0]) + dot(agt[1, rows], attp_s[1])
            store(0, value_part[:, 0:128])
            store(1, value_part[:, 128:256])
            store(2, out_part[:, 0:128])
            store(3, out_part[:, 128:256])
            store(4, value_part[:, 256:384] + out_part[:, 256:384])

        for p in WAVES[0]:
            slots = {"A": (0, 1, None, None), "B": (0, None, 1, None)}.get(PARTS[p][3][0], (0, 1, 2, 3))
            if slots[turn] is not None:
                flying[p, 0] += begin(p, 0, slots[turn])
    z_copies = []

    def last_exchange(wave):
        tiles, first, count = Z_GROUPS[wave]
        fill = count - 40 * len(tiles)
        for j in range(4):
            pieces = [final[t, 40 * j : 40 * j + 40] for t in tiles]
            if fill:
                pieces.append(jnp.zeros((fill, 128), F32))
            z_s[j, first : first + count] = jnp.concatenate(pieces, axis=0).astype(BF16)
        for k in (1, 2, 3):
            copy = pltpu.make_async_remote_copy(
                src_ref=z_s.at[zp ^ k, pl.ds(first, count)],
                dst_ref=z_r.at[k - 1, pl.ds(first, count)],
                send_sem=z_send.at[wave, k - 1],
                recv_sem=z_recv.at[wave, k - 1],
                device_id=z_peers[k - 1],
                device_id_type=MESH,
            )
            copy.start()
            z_copies.append(copy)
            started.append(copy)

    def step(wave, number):
        for p in WAVES[wave]:
            end(p, number - 1, flying[p, number - 1])
            if number < 3:
                flying[p, number] = begin(p, number)

    for p in WAVES[0]:
        leave(flying[p, 0])
    for p in WAVES[1]:
        flying[p, 0] = begin(p, 0)
    step(0, 1)
    step(1, 1)
    embed_copies = start_embeds()
    step(0, 2)
    step(1, 2)
    step(0, 3)
    last_exchange(0)
    step(1, 3)
    last_exchange(1)
    embeds_copy = finish_embeds(embed_copies)
    arrive(z_copies)
    mine = z_s[zp].astype(F32)
    for k in range(3):
        mine = mine + z_r[k].astype(F32)
    first_core = c == 0
    own_tiles = []
    f_s[...] = jnp.zeros_like(f_s)
    for t in range(5):
        rows = mine[TILE_ROWS[t] : TILE_ROWS[t] + 40]
        early, late = rows[0:20], rows[20:40]
        own_tiles.append(jnp.where(first_core, early, late))
        f_s[t, 0:20] = jnp.where(first_core, late, early).astype(BF16)
    arrive([to_core(4, f_s, f_r)])
    for t in range(5):
        got = f_r[t, 0:20].astype(F32)
        left = jnp.where(first_core, own_tiles[t], got)
        right = jnp.where(first_core, got, own_tiles[t])
        if t < 2:
            cols = slice(128 * t, 128 * t + 128)
            grad_qkv[0, :, cols] = left
            grad_qkv[2, :, cols] = right
        elif t < 4:
            cols = slice(128 * t - 256, 128 * t - 128)
            grad_qkv[1, :, cols] = left
            grad_out[:, cols] = right
        else:
            grad_qkv[0, :, 256:320] = left[:, 0:64]
            grad_qkv[1, :, 256:320] = left[:, 64:128]
            grad_qkv[2, :, 256:320] = right[:, 0:64]
            grad_out[:, 256:320] = right[:, 64:128]
    embeds_copy.wait()
    for copy in started:
        copy.wait_send()


def call(counts, lengths, positions, audio, cotangent, w_qkv, w_out, w_proj):
    vmem, dma = pltpu.VMEM, pltpu.SemaphoreType.DMA
    scratch = [
        vmem((3, 320, 1280), BF16),
        vmem((320, 1280), BF16),
        vmem((1280, 896), BF16),
        vmem((3, 128, 384), F32),
        vmem((4, 3, 272, 128), BF16),
        vmem((4, 288, 128), BF16),
        vmem((4, 288, 128), BF16),
        vmem((4, 80, 640), BF16),
        vmem((3, 80, 640), BF16),
        vmem((4, 80, 640), BF16),
        vmem((3, 80, 640), BF16),
        vmem((4, 80, 640), BF16),
        vmem((4, 80, 640), BF16),
        vmem((4, 288, 128), BF16),
        vmem((4, 288, 128), BF16),
        vmem((40, 3584), BF16),
        vmem((3, 100, 320), BF16),
        vmem((40, 3584), BF16),
        vmem((336, 1280), BF16),
        vmem((2, 1280, 336), BF16),
        vmem((3, 112, 384), F32),
        vmem((3, 2, 224, 128), BF16),
        vmem((3, 112, 128), BF16),
        vmem((3, 112, 384), BF16),
        vmem((3, 112, 384), BF16),
        vmem((3, 3, 224, 112), F32),
        vmem((2, 160, 384), BF16),
        vmem((2, 1280, 160), BF16),
        vmem((160, 384), BF16),
        vmem((2, 336, 640), BF16),
        vmem((336, 640), BF16),
        vmem((4, 5, 2, 160, 128), BF16),
        vmem((5, 160, 128), F32),
        vmem((3, 3, 112, 224), F32),
        vmem((3, 112, 160), BF16),
        vmem((4, 208, 128), BF16),
        vmem((3, 208, 128), BF16),
        vmem((5, 32, 128), BF16),
        vmem((5, 32, 128), BF16),
        dma((6,)),
        dma((12, 3)),
        dma((12, 3)),
        dma((5,)),
        dma((5,)),
        dma((len(PARTS), 3, 4)),
        dma((len(PARTS), 3, 4)),
        dma((2, 3)),
        dma((2, 3)),
    ]
    assert len(scratch) == 48
    scratch += [vmem(received_shape(part, step), BF16) for part in PARTS for step in range(3)]
    in_vmem = pl.BlockSpec(memory_space=pltpu.VMEM)
    in_smem = pl.BlockSpec(memory_space=pltpu.SMEM)
    anywhere = pl.BlockSpec(memory_space=pl.ANY)
    return pl.pallas_call(
        kernel,
        out_shape=(
            jax.ShapeDtypeStruct((40, 3584), BF16),
            jax.ShapeDtypeStruct((3, 20, 320), F32),
            jax.ShapeDtypeStruct((20, 320), F32),
        ),
        in_specs=[in_smem, in_smem, in_vmem] + [anywhere] * 5,
        out_specs=(anywhere, in_vmem, in_vmem),
        scratch_shapes=scratch,
        compiler_params=pltpu.CompilerParams(
            collective_id=0, has_side_effects=True, vmem_limit_bytes=60 * 2**20
        ),
        name="sublayer",
    )(counts, lengths, positions, audio, cotangent, w_qkv, w_out, w_proj)


def write_out(*refs):
    for source, target in zip(refs[:3], refs[3:]):
        target[...] = source[...]


def results(*parts):
    in_vmem = pl.BlockSpec(memory_space=pltpu.VMEM)
    return pl.pallas_call(
        write_out,
        out_shape=tuple(jax.ShapeDtypeStruct(part.shape, part.dtype) for part in parts),
        in_specs=[in_vmem] * 3,
        out_specs=(in_vmem,) * 3,
        name="results",
    )(*parts)


def shards(audio, counts, lengths, positions, w_qkv, w_out, w_proj, cotangent):
    embeds, grad_qkv, grad_out = call(
        counts, lengths, positions, audio, cotangent, jnp.swapaxes(w_qkv, 1, 2), w_out, w_proj
    )
    embeds, grad_qkv, grad_out = results(embeds, grad_qkv, grad_out)
    return embeds, grad_qkv, grad_out.T


def solution(mesh):
    in_specs = (
        P("dp", None, "seq"),
        P("dp"),
        P("dp"),
        P("dp", None),
        P(None, None, "seq"),
        P("seq", None),
        P(None, "seq"),
        P(("dp", "seq"), None),
    )
    out_specs = (P(("dp", "seq"), None), P(None, "dp", "seq"), P("seq", "dp"))
    return jax.shard_map(shards, mesh=mesh, in_specs=in_specs, out_specs=out_specs, check_vma=False)
```

```python
import jax
import jax.numpy as jnp
from jax import lax
from jax.experimental import pallas as pl
from jax.experimental.pallas import tpu as pltpu
from jax.sharding import PartitionSpec as P

MESH = pl.DeviceIdType.MESH
F32 = jnp.float32
BF16 = jnp.bfloat16
EPSILON = 1e-05
SCALING = 0.125
PARTS = (
    (0, 0, 160, "ABa"),
    (1, 0, 160, "BAb"),
    (4, 0, 80, "AaB"),
    (4, 80, 80, "BbA"),
    (2, 0, 160, "aAB"),
    (3, 0, 160, "bBA"),
)
WAVES = ((0, 1, 2, 3, 4, 5), ())
Z_GROUPS = (((0, 1, 4), 0, 128), ((2, 3), 128, 80))
TILE_ROWS = {0: 0, 1: 40, 4: 80, 2: 128, 3: 168}


def dot(a, b):
    return jnp.dot(a, b, preferred_element_type=F32)


def dot_nt(a, b):
    return lax.dot_general(a, b, (((1,), (1,)), ((), ())), preferred_element_type=F32)


def dot_tn(a, b):
    return lax.dot_general(a, b, (((0,), (0,)), ((), ())), preferred_element_type=F32)


def fold(rows, width, extra):
    pieces = [rows[:, i : i + width] for i in range(0, rows.shape[1], width)]
    if extra:
        pieces.append(jnp.zeros((extra, width), F32))
    return jnp.concatenate(pieces, axis=0).astype(BF16)


def unfold(folded, count):
    wide = folded.astype(F32)
    return jnp.concatenate([wide[40 * i : 40 * i + 40] for i in range(count)], axis=1)


def normalize(rows):
    centred = rows - jnp.mean(rows, axis=-1, keepdims=True)
    inverse = lax.rsqrt(jnp.mean(centred * centred, axis=-1, keepdims=True) + EPSILON)
    return centred * inverse, inverse


def received_shape(part, step):
    _, _, rows, order = part
    before = order[:step]
    y_done = sum(letter in "AB" for letter in before)
    z_done = any(letter in "ab" for letter in before)
    if order[step] in "AB":
        return (2 if y_done == 0 else 1, 1 if z_done else 2, rows, 128)
    return ((4, 2, 1)[y_done], 1, rows, 128)


def kernel(*refs):
    (counts, lengths, positions, audio, cotangent, w_qkv, w_out, w_proj) = refs[:8]
    embeds, grad_qkv, grad_out = refs[8:11]
    (
        wq, wo, wp, tmp, aud, cot_s, cot_r, gt_s, gt_r, t_s, t_r, ag_a, ad_a, e_s, e_r, cot_v, aud_v, emb,
        nb, nt, pj, q2s, qr_s, k_s, v_s, prob, attp_s, agt, mgp, local, other, total, final, prob_t, up_s,
        z_s, z_r, f_s, f_r, w_sem, x_send, x_recv, c_send, c_recv, r_send, r_recv, z_send, z_recv,
    ) = refs[11 : 11 + 48]
    r_bufs = refs[11 + 48 :]

    dp = lax.axis_index("dp")
    x = lax.axis_index("seq")
    y = dp // 16
    z = (dp // 2) % 8
    c = dp % 2
    par = z % 2
    zp = z // 2

    def at(yy, zz, cc):
        return (yy * 16 + zz * 2 + cc, x)

    peers = [(dp, (x + k) % 4) for k in (1, 2, 3)]
    partner = {
        "A": at(y ^ 1, z, c),
        "B": at(y ^ 3, z, c),
        "a": at(y, z ^ 1, c),
        "b": at(y, (z + 7 + 2 * par) % 8, c),
    }
    core_peer = at(y, z, 1 - c)
    z_peers = [at(y, z ^ (2 * k), c) for k in (1, 2, 3)]

    input_copies = [
        pltpu.make_async_copy(src, dst, w_sem.at[3 + i])
        for i, (src, dst) in enumerate(((cotangent, cot_v), (audio, aud_v)))
    ]
    weight_copies = [
        pltpu.make_async_copy(src, dst, w_sem.at[i])
        for i, (src, dst) in enumerate(((w_qkv, wq), (w_out, wo), (w_proj, wp)))
    ]
    for copy in input_copies:
        copy.start()

    barrier = pltpu.get_barrier_semaphore()
    everyone = peers + [core_peer] + list(partner.values()) + z_peers
    for device in everyone:
        pl.semaphore_signal(barrier, inc=1, device_id=device, device_id_type=MESH)

    for i in (2, 0, 1):
        weight_copies[i].start()

    lane = lax.broadcasted_iota(jnp.int32, (112, 128), 1)
    low = lane < 64
    tmp[...] = jnp.zeros_like(tmp)
    pj[...] = jnp.zeros_like(pj)
    mgp[...] = jnp.zeros_like(mgp)
    local[1, :, 384:640] = jnp.zeros((336, 256), BF16)
    input_copies[0].wait()
    cot_rows = cot_v[...].astype(F32)
    for t in range(4):
        cot_s[t] = fold(cot_rows[:, 896 * t : 896 * t + 896], 128, 8)
    cot_r[x] = cot_s[x]

    def pack_audio(b):
        tmp[b, 0:100, 0:320] = aud_v[b].astype(F32)
        first, second, third = (tmp[b, 0:104, 128 * i : 128 * i + 128] for i in range(3))
        second_turned = pltpu.roll(second, 64, 1)
        blank = jnp.zeros((8, 128), F32)
        even_low = jnp.concatenate([third[56:104], blank], axis=0)
        odd_low = jnp.concatenate([first[56:104], blank], axis=0)
        packed = third[0:56] + pltpu.roll(even_low, 64, 1)
        packed_odd = jnp.where(low[0:56], first[0:56], pltpu.roll(odd_low, 64, 1))
        even = jnp.concatenate([first, second, packed, blank], axis=0)
        odd = jnp.concatenate(
            [
                jnp.where(low[0:104], pltpu.roll(first, 64, 1), second_turned),
                jnp.where(low[0:104], second_turned, pltpu.roll(third, 64, 1)),
                packed_odd,
                blank,
            ],
            axis=0,
        )
        aud[x, b] = jnp.where(x % 2 == 0, even, odd).astype(BF16)

    input_copies[1].wait()
    pack_audio(0)

    pl.semaphore_wait(barrier, len(everyone))

    started = []
    def to_peers(slot, source, target):
        copies = []
        for k in (1, 2, 3):
            there = (x + k) % 4
            copy = pltpu.make_async_remote_copy(
                src_ref=source(there),
                dst_ref=target(k),
                send_sem=x_send.at[slot, k - 1],
                recv_sem=x_recv.at[slot, k - 1],
                device_id=(dp, there),
                device_id_type=MESH,
            )
            copy.start()
            copies.append(copy)
        started.extend(copies)
        return copies

    def to_core(slot, source, target):
        copy = pltpu.make_async_remote_copy(
            src_ref=source,
            dst_ref=target,
            send_sem=c_send.at[slot],
            recv_sem=c_recv.at[slot],
            device_id=core_peer,
            device_id_type=MESH,
        )
        copy.start()
        started.append(copy)
        return copy

    def leave(copies):
        for copy in copies:
            copy.wait_send()
            started[:] = [other_copy for other_copy in started if other_copy is not copy]

    def arrive(copies):
        for copy in copies:
            copy.wait_recv()

    audio_copies = []
    cot_copies = to_peers(3, lambda there: cot_s.at[there], lambda k: cot_r.at[x])

    def send_audio(b):
        block = aud.at[x, b]
        audio_copies.append(to_peers(b, lambda there: block, lambda k: block))

    send_audio(0)
    pack_audio(1)
    pack_audio(2)
    leave(cot_copies)
    send_audio(1)
    send_audio(2)

    pos_pad = jnp.concatenate([positions[...].astype(F32), jnp.zeros((13, 50), F32)], axis=0).astype(BF16)
    frame_row = lax.broadcasted_iota(jnp.int32, (50, 112), 0)
    frame_col = lax.broadcasted_iota(jnp.int32, (50, 112), 1)
    spread = jnp.where(frame_row == frame_col // 2, 1.0, 0.0).astype(BF16)
    pos_lanes = dot(pos_pad, spread)
    frame_row_t = lax.broadcasted_iota(jnp.int32, (112, 50), 0)
    frame_col_t = lax.broadcasted_iota(jnp.int32, (112, 50), 1)
    spread_t = jnp.where(frame_row_t // 2 == frame_col_t, 1.0, 0.0).astype(BF16)
    pos_sub = dot_nt(spread_t, pos_pad)
    lives = [jnp.where(b < counts[0], lengths[b], 0) for b in range(3)]

    def place(b, first, count):
        row = lax.broadcasted_iota(jnp.int32, (count, 112), 0) + first
        frame = lax.broadcasted_iota(jnp.int32, (count, 112), 1)
        hit = (row.astype(F32) == pos_lanes[b : b + 1, :]) & (frame < lives[b])
        return jnp.where(hit, 1.0, 0.0).astype(BF16)

    def unplace(b):
        frame = lax.broadcasted_iota(jnp.int32, (112, 160), 0)
        row = lax.broadcasted_iota(jnp.int32, (112, 160), 1)
        hit = (row.astype(F32) == pos_sub[:, b : b + 1]) & (frame < lives[b])
        return jnp.where(hit, 1.0, 0.0).astype(BF16)

    def split_heads(tile):
        return jnp.concatenate([jnp.where(low, tile, 0.0), jnp.where(low, 0.0, tile)], axis=0).astype(BF16)

    weight_copies[0].wait()

    attp = [jnp.zeros((160, 128), F32) for _ in range(3)]
    pooled_audio = jnp.zeros((40, 1280), F32)

    def forward(b, attp, pooled_audio):
        arrive(audio_copies[b])
        tiles = []
        for s in (0, 2):
            left = aud[s, b].astype(F32)
            right = aud[s + 1, b].astype(F32)
            left_rest, right_rest = left[208:264], right[208:264]
            top = jnp.where(low[0:56], left_rest, pltpu.roll(right_rest, 64, 1))
            bottom = jnp.where(low[0:56], pltpu.roll(left_rest, 64, 1), right_rest)
            middle = jnp.concatenate([top, bottom[0:48]], axis=0)
            for tile in (left[0:104], left[104:208], middle, right[0:104], right[104:208]):
                tiles.append(jnp.concatenate([tile, jnp.zeros((8, 128), F32)], axis=0))
        frames = jnp.concatenate(tiles, axis=1)
        pooled_audio = pooled_audio + dot(place(b, 40 * x, 40), frames.astype(BF16))
        normed = normalize(frames)[0].astype(BF16)
        nb[112 * b : 112 * b + 112, :] = normed
        for j in range(3):
            pj[j, :, 0:320] = dot_nt(normed, wq[j])
        k_s[b] = pj[1].astype(BF16)
        v_s[b] = pj[2].astype(BF16)
        key_limit = jnp.maximum(lives[b], 1)
        placed = place(b, 0, 160)
        for g in range(3):
            cols = slice(128 * g, 128 * g + 128)
            q_tile = pj[0, :, cols]
            if g < 2:
                queries = split_heads(q_tile)
                q2s[b, g] = queries
            else:
                queries = q_tile.astype(BF16)
                qr_s[b] = queries
            rows = queries.shape[0]
            scores = dot_nt(queries, k_s[b, :, cols]) * SCALING
            key = lax.broadcasted_iota(jnp.int32, (rows, 112), 1)
            scores = jnp.where(key < key_limit, scores, -1e30)
            powered = jnp.exp(scores - jnp.max(scores, axis=-1, keepdims=True))
            weights = powered * (1.0 / jnp.sum(powered, axis=-1, keepdims=True))
            prob[b, g, 0:rows] = weights
            scores_t = dot_nt(k_s[b, :, cols], queries) * SCALING
            key_t = lax.broadcasted_iota(jnp.int32, (112, rows), 0)
            scores_t = jnp.where(key_t < key_limit, scores_t, -1e30)
            powered_t = jnp.exp(scores_t - jnp.max(scores_t, axis=0, keepdims=True))
            prob_t[b, g, :, 0:rows] = powered_t * (1.0 / jnp.sum(powered_t, axis=0, keepdims=True))
            mixed = dot(weights.astype(BF16), v_s[b, :, cols])
            if g < 2:
                mixed = jnp.where(low, mixed[0:112], mixed[112:224])
            attp[g] = attp[g] + dot(placed, mixed.astype(BF16))
        return attp, pooled_audio

    weight_copies[2].wait()
    arrive(cot_copies)
    row_grads = jnp.concatenate([unfold(cot_r[s], 7) for s in range(4)], axis=0).astype(BF16)
    adapter_terms = dot_nt(row_grads, wp[...])
    for t in range(4):
        gt_s[t] = fold(adapter_terms[40 * t : 40 * t + 40], 640, 0)
    attp, pooled_audio = forward(0, attp, pooled_audio)
    leave(audio_copies[1] + audio_copies[2])
    gt_copies = to_peers(4, lambda there: gt_s.at[there], lambda k: gt_r.at[k - 1])
    attp, pooled_audio = forward(1, attp, pooled_audio)
    attp, pooled_audio = forward(2, attp, pooled_audio)
    attp = [part.astype(BF16) for part in attp]
    for g in range(2):
        attp_s[c, :, 128 * g : 128 * g + 128] = attp[g]
    attp_s[c, :, 256:384] = pltpu.roll(attp[2].astype(F32), 64, 1).astype(BF16)
    weight_copies[1].wait()
    head_terms = (
        dot(attp[0], wo[0:128]) + dot(attp[1], wo[128:256]) + dot(attp[2][:, 0:64], wo[256:320])
    )
    for t in range(4):
        t_s[t] = fold(head_terms[40 * t : 40 * t + 40], 640, 0)
    t_copies = to_peers(5, lambda there: t_s.at[there], lambda k: t_r.at[k - 1])

    nt[c] = nb[...].T
    for b in range(3):
        up_s[b] = unplace(b)
    core_copies = [to_core(0, nt.at[c], nt.at[c]), to_core(1, attp_s.at[c], attp_s.at[c])]

    arrive(gt_copies)
    adapted_grad = gt_s[x].astype(F32)
    for k in range(3):
        adapted_grad = adapted_grad + gt_r[k].astype(F32)
    adapted_grad = unfold(adapted_grad.astype(BF16), 2)

    arrive(t_copies)
    attention = t_s[x].astype(F32)
    for k in range(3):
        attention = attention + t_r[k].astype(F32)
    attention = jnp.concatenate([attention[0:40], attention[40:80]], axis=1)
    normed_rows, inverse = normalize((pooled_audio + attention) * 0.5)
    pooled_grad = inverse * (
        adapted_grad
        - jnp.mean(adapted_grad, axis=-1, keepdims=True)
        - normed_rows * jnp.mean(adapted_grad * normed_rows, axis=-1, keepdims=True)
    )
    ag_a[x] = fold(pooled_grad * 0.5, 640, 0)
    ag_copies = to_peers(6, lambda there: ag_a.at[x], lambda k: ag_a.at[x])
    ad_a[x] = fold(normed_rows, 640, 0)
    arrive(ag_copies)
    attention_grad = jnp.concatenate([unfold(ag_a[s], 2) for s in range(4)], axis=0).astype(BF16)
    mgp[:, 0:320] = dot_nt(attention_grad, wo[...]).astype(BF16)
    pairs = [(b, g) for b in range(3) for g in range(3)]
    grads, prob_grads, prob_grads_t, halves, halves_t = {}, {}, {}, {}, {}
    for b in range(3):
        mixed_grad = dot(up_s[b], mgp[...])
        for g in range(3):
            tile = mixed_grad[:, 128 * g : 128 * g + 128]
            grads[b, g] = split_heads(tile) if g < 2 else tile.astype(BF16)
    for b, g in pairs:
        cols = slice(128 * g, 128 * g + 128)
        prob_grads[b, g] = dot_nt(grads[b, g], v_s[b, :, cols])
        prob_grads_t[b, g] = dot_nt(v_s[b, :, cols], grads[b, g])
    for b, g in pairs:
        count = 224 if g < 2 else 112
        weights, weights_t = prob[b, g, 0:count], prob_t[b, g, :, 0:count]
        inner = jnp.sum(weights * prob_grads[b, g], axis=-1, keepdims=True)
        inner_t = jnp.sum(weights_t * prob_grads_t[b, g], axis=0, keepdims=True)
        halves[b, g] = (weights * (prob_grads[b, g] - inner)).astype(BF16)
        halves_t[b, g] = (weights_t * (prob_grads_t[b, g] - inner_t)).astype(BF16)
    for b in range(3):
        rows = slice(112 * b, 112 * b + 112)
        for g in range(3):
            cols = slice(128 * g, 128 * g + 128)
            count = 224 if g < 2 else 112
            query_grad = dot(halves[b, g], k_s[b, :, cols])
            if g < 2:
                query_grad = jnp.where(low, query_grad[0:112], query_grad[112:224])
            query_grad = query_grad * SCALING
            key_grad = dot(halves_t[b, g], q2s[b, g] if g < 2 else qr_s[b]) * SCALING
            value_grad = dot(prob_t[b, g, :, 0:count].astype(BF16), grads[b, g])
            local[1, rows, cols] = value_grad.astype(BF16)
            if g < 2:
                local[0, rows, cols] = query_grad.astype(BF16)
                local[0, rows, 256 + 128 * g : 384 + 128 * g] = key_grad.astype(BF16)
            else:
                local[0, rows, 512:640] = (query_grad + pltpu.roll(key_grad, 64, 1)).astype(BF16)
    agt[c] = attention_grad.T
    core_copies.append(to_core(2, local.at[1 - c], other))
    core_copies.append(to_core(3, agt.at[c], agt.at[c]))
    ad_copies = to_peers(7, lambda there: ad_a.at[x], lambda k: ad_a.at[x])

    def start_embeds():
        arrive(ad_copies)
        adapted = jnp.concatenate([unfold(ad_a[s], 2) for s in range(4)], axis=0).astype(BF16)
        adapter_rows = dot(adapted, wp[...])
        for t in range(4):
            e_s[t] = fold(adapter_rows[40 * t : 40 * t + 40], 128, 8)
        e_r[x] = e_s[x]
        return to_peers(8, lambda there: e_s.at[there], lambda k: e_r.at[x])

    def finish_embeds(copies):
        arrive(copies)
        for s in range(4):
            emb[:, 896 * s : 896 * s + 896] = unfold(e_r[s], 7).astype(BF16)
        copy = pltpu.make_async_copy(emb, embeds, w_sem.at[5])
        copy.start()
        return copy

    def blocks(order, step):
        y_before = [letter for letter in order[:step] if letter in "AB"]
        z_done = any(letter in "ab" for letter in order[:step])
        letter = order[step]
        if letter in "AB":
            near = y ^ (1 if letter == "A" else 3)
            beyond = y ^ (3 if letter == "A" else 1)
            sides = (par, par) if z_done else (None, None)
            if y_before:
                return [near], [y], sides
            return [y ^ 2, near], [beyond, y], sides
        held = [y ^ 2, y ^ 1, y ^ 3, y]
        if len(y_before) == 1:
            held = [y ^ (3 if y_before[0] == "A" else 1), y]
        elif len(y_before) == 2:
            held = [y]
        return held, held, (1 - par, par)

    def begin(p, step, only=None):
        tile, row, count, order = PARTS[p]
        send, _, (side, _) = blocks(order, step)
        landing = r_bufs[3 * p + step]
        copies = []
        for i, block in enumerate(send):
            if only is not None and i != only:
                continue
            pick = pl.ds(0, 2) if side is None else pl.ds(side, 1)
            copy = pltpu.make_async_remote_copy(
                src_ref=total.at[block, tile, pick, pl.ds(row, count)],
                dst_ref=landing.at[i],
                send_sem=r_send.at[p, step, i],
                recv_sem=r_recv.at[p, step, i],
                device_id=partner[order[step]],
                device_id_type=MESH,
            )
            copy.start()
            copies.append(copy)
        started.extend(copies)
        return copies

    def end(p, step, copies):
        tile, row, count, order = PARTS[p]
        _, keep, (_, side) = blocks(order, step)
        landing = r_bufs[3 * p + step]
        rows = pl.ds(row, count)
        arrive(copies)
        for i, block in enumerate(keep):
            if step == 2:
                final[tile, rows] = total[block, tile, par, rows].astype(F32) + landing[i, 0].astype(F32)
            elif side is None:
                for k in range(2):
                    kept = total[block, tile, k, rows].astype(F32) + landing[i, k].astype(F32)
                    total[block, tile, k, rows] = kept.astype(BF16)
            else:
                kept = total[block, tile, side, rows].astype(F32) + landing[i, 0].astype(F32)
                total[block, tile, side, rows] = kept.astype(BF16)

    arrive(core_copies)
    flying = {(p, 0): [] for p in range(len(PARTS))}
    turns = (y ^ 2, y ^ 1, y ^ 3, y)
    for turn, yy in enumerate(turns):
        rows = pl.ds(pl.multiple_of(320 * yy, 64), 320)

        def store(tile, values):
            for side in range(2):
                total[yy, tile, side] = jnp.concatenate(
                    [values[40 * i : 40 * i + 40] for i in range(side, 8, 2)], axis=0
                ).astype(BF16)

        @pl.when(c == 0)
        def _():
            part = dot(nt[0, rows], local[0]) + dot(nt[1, rows], other[...])
            for t in range(5):
                store(t, part[:, 128 * t : 128 * t + 128])

        @pl.when(c == 1)
        def _():
            value_part = dot(nt[1, rows], local[1, :, 0:384]) + dot(nt[0, rows], other[:, 0:384])
            out_part = dot(agt[0, rows], attp_s[0]) + dot(agt[1, rows], attp_s[1])
            store(0, value_part[:, 0:128])
            store(1, value_part[:, 128:256])
            store(2, out_part[:, 0:128])
            store(3, out_part[:, 128:256])
            store(4, value_part[:, 256:384] + out_part[:, 256:384])

        for p in WAVES[0]:
            slots = {"A": (0, 1, None, None), "B": (0, None, 1, None)}.get(PARTS[p][3][0], (0, 1, 2, 3))
            if slots[turn] is not None:
                flying[p, 0] += begin(p, 0, slots[turn])
    z_copies = []

    def last_exchange(wave):
        tiles, first, count = Z_GROUPS[wave]
        fill = count - 40 * len(tiles)
        for j in range(4):
            pieces = [final[t, 40 * j : 40 * j + 40] for t in tiles]
            if fill:
                pieces.append(jnp.zeros((fill, 128), F32))
            z_s[j, first : first + count] = jnp.concatenate(pieces, axis=0).astype(BF16)
        for k in (1, 2, 3):
            copy = pltpu.make_async_remote_copy(
                src_ref=z_s.at[zp ^ k, pl.ds(first, count)],
                dst_ref=z_r.at[k - 1, pl.ds(first, count)],
                send_sem=z_send.at[wave, k - 1],
                recv_sem=z_recv.at[wave, k - 1],
                device_id=z_peers[k - 1],
                device_id_type=MESH,
            )
            copy.start()
            z_copies.append(copy)
            started.append(copy)

    def step(wave, number):
        for p in WAVES[wave]:
            end(p, number - 1, flying[p, number - 1])
            if number < 3:
                flying[p, number] = begin(p, number)

    for p in WAVES[1]:
        flying[p, 0] = begin(p, 0)
    step(0, 1)
    step(1, 1)
    step(0, 2)
    step(1, 2)
    embed_copies = start_embeds()
    step(0, 3)
    last_exchange(0)
    step(1, 3)
    last_exchange(1)
    embeds_copy = finish_embeds(embed_copies)
    arrive(z_copies)
    mine = z_s[zp].astype(F32)
    for k in range(3):
        mine = mine + z_r[k].astype(F32)
    first_core = c == 0
    own_tiles = []
    f_s[...] = jnp.zeros_like(f_s)
    for t in range(5):
        rows = mine[TILE_ROWS[t] : TILE_ROWS[t] + 40]
        early, late = rows[0:20], rows[20:40]
        own_tiles.append(jnp.where(first_core, early, late))
        f_s[t, 0:20] = jnp.where(first_core, late, early).astype(BF16)
    arrive([to_core(4, f_s, f_r)])
    for t in range(5):
        got = f_r[t, 0:20].astype(F32)
        left = jnp.where(first_core, own_tiles[t], got)
        right = jnp.where(first_core, got, own_tiles[t])
        if t < 2:
            cols = slice(128 * t, 128 * t + 128)
            grad_qkv[0, :, cols] = left
            grad_qkv[2, :, cols] = right
        elif t < 4:
            cols = slice(128 * t - 256, 128 * t - 128)
            grad_qkv[1, :, cols] = left
            grad_out[:, cols] = right
        else:
            grad_qkv[0, :, 256:320] = left[:, 0:64]
            grad_qkv[1, :, 256:320] = left[:, 64:128]
            grad_qkv[2, :, 256:320] = right[:, 0:64]
            grad_out[:, 256:320] = right[:, 64:128]
    embeds_copy.wait()
    for copy in started:
        copy.wait_send()


def call(counts, lengths, positions, audio, cotangent, w_qkv, w_out, w_proj):
    vmem, dma = pltpu.VMEM, pltpu.SemaphoreType.DMA
    scratch = [
        vmem((3, 320, 1280), BF16),
        vmem((320, 1280), BF16),
        vmem((1280, 896), BF16),
        vmem((3, 128, 384), F32),
        vmem((4, 3, 272, 128), BF16),
        vmem((4, 288, 128), BF16),
        vmem((4, 288, 128), BF16),
        vmem((4, 80, 640), BF16),
        vmem((3, 80, 640), BF16),
        vmem((4, 80, 640), BF16),
        vmem((3, 80, 640), BF16),
        vmem((4, 80, 640), BF16),
        vmem((4, 80, 640), BF16),
        vmem((4, 288, 128), BF16),
        vmem((4, 288, 128), BF16),
        vmem((40, 3584), BF16),
        vmem((3, 100, 320), BF16),
        vmem((40, 3584), BF16),
        vmem((336, 1280), BF16),
        vmem((2, 1280, 336), BF16),
        vmem((3, 112, 384), F32),
        vmem((3, 2, 224, 128), BF16),
        vmem((3, 112, 128), BF16),
        vmem((3, 112, 384), BF16),
        vmem((3, 112, 384), BF16),
        vmem((3, 3, 224, 112), F32),
        vmem((2, 160, 384), BF16),
        vmem((2, 1280, 160), BF16),
        vmem((160, 384), BF16),
        vmem((2, 336, 640), BF16),
        vmem((336, 640), BF16),
        vmem((4, 5, 2, 160, 128), BF16),
        vmem((5, 160, 128), F32),
        vmem((3, 3, 112, 224), F32),
        vmem((3, 112, 160), BF16),
        vmem((4, 208, 128), BF16),
        vmem((3, 208, 128), BF16),
        vmem((5, 32, 128), BF16),
        vmem((5, 32, 128), BF16),
        dma((6,)),
        dma((9, 3)),
        dma((9, 3)),
        dma((5,)),
        dma((5,)),
        dma((len(PARTS), 3, 4)),
        dma((len(PARTS), 3, 4)),
        dma((2, 3)),
        dma((2, 3)),
    ]
    assert len(scratch) == 48
    scratch += [vmem(received_shape(part, step), BF16) for part in PARTS for step in range(3)]
    in_vmem = pl.BlockSpec(memory_space=pltpu.VMEM)
    in_smem = pl.BlockSpec(memory_space=pltpu.SMEM)
    anywhere = pl.BlockSpec(memory_space=pl.ANY)
    return pl.pallas_call(
        kernel,
        out_shape=(
            jax.ShapeDtypeStruct((40, 3584), BF16),
            jax.ShapeDtypeStruct((3, 20, 320), F32),
            jax.ShapeDtypeStruct((20, 320), F32),
        ),
        in_specs=[in_smem, in_smem, in_vmem] + [anywhere] * 5,
        out_specs=(anywhere, in_vmem, in_vmem),
        scratch_shapes=scratch,
        compiler_params=pltpu.CompilerParams(
            collective_id=0, has_side_effects=True, vmem_limit_bytes=60 * 2**20
        ),
        name="sublayer",
    )(counts, lengths, positions, audio, cotangent, w_qkv, w_out, w_proj)


def write_out(*refs):
    for source, target in zip(refs[:3], refs[3:]):
        target[...] = source[...]


def results(*parts):
    in_vmem = pl.BlockSpec(memory_space=pltpu.VMEM)
    return pl.pallas_call(
        write_out,
        out_shape=tuple(jax.ShapeDtypeStruct(part.shape, part.dtype) for part in parts),
        in_specs=[in_vmem] * 3,
        out_specs=(in_vmem,) * 3,
        name="results",
    )(*parts)


def shards(audio, counts, lengths, positions, w_qkv, w_out, w_proj, cotangent):
    embeds, grad_qkv, grad_out = call(
        counts, lengths, positions, audio, cotangent, jnp.swapaxes(w_qkv, 1, 2), w_out, w_proj
    )
    embeds, grad_qkv, grad_out = results(embeds, grad_qkv, grad_out)
    return embeds, grad_qkv, grad_out.T


def solution(mesh):
    in_specs = (
        P("dp", None, "seq"),
        P("dp"),
        P("dp"),
        P("dp", None),
        P(None, None, "seq"),
        P("seq", None),
        P(None, "seq"),
        P(("dp", "seq"), None),
    )
    out_specs = (P(("dp", "seq"), None), P(None, "dp", "seq"), P("seq", "dp"))
    return jax.shard_map(shards, mesh=mesh, in_specs=in_specs, out_specs=out_specs, check_vma=False)
```

```python
import jax
import jax.numpy as jnp
from jax import lax
from jax.experimental import pallas as pl
from jax.experimental.pallas import tpu as pltpu
from jax.sharding import PartitionSpec as P

MESH = pl.DeviceIdType.MESH
F32 = jnp.float32
BF16 = jnp.bfloat16
EPSILON = 1e-05
SCALING = 0.125
PARTS = (
    (0, 0, 160, "ABa"),
    (1, 0, 160, "BAb"),
    (4, 0, 80, "AaB"),
    (4, 80, 80, "BbA"),
    (2, 0, 160, "aAB"),
    (3, 0, 160, "bBA"),
)
WAVES = ((0, 1, 2, 3, 4, 5), ())
Z_GROUPS = (((0, 1, 4), 0, 128), ((2, 3), 128, 80))
TILE_ROWS = {0: 0, 1: 40, 4: 80, 2: 128, 3: 168}


def dot(a, b):
    return jnp.dot(a, b, preferred_element_type=F32)


def dot_nt(a, b):
    return lax.dot_general(a, b, (((1,), (1,)), ((), ())), preferred_element_type=F32)


def dot_tn(a, b):
    return lax.dot_general(a, b, (((0,), (0,)), ((), ())), preferred_element_type=F32)


def fold(rows, width, extra):
    pieces = [rows[:, i : i + width] for i in range(0, rows.shape[1], width)]
    if extra:
        pieces.append(jnp.zeros((extra, width), F32))
    return jnp.concatenate(pieces, axis=0).astype(BF16)


def unfold(folded, count):
    wide = folded.astype(F32)
    return jnp.concatenate([wide[40 * i : 40 * i + 40] for i in range(count)], axis=1)


def normalize(rows):
    centred = rows - jnp.mean(rows, axis=-1, keepdims=True)
    inverse = lax.rsqrt(jnp.mean(centred * centred, axis=-1, keepdims=True) + EPSILON)
    return centred * inverse, inverse


def received_shape(part, step):
    _, _, rows, order = part
    before = order[:step]
    y_done = sum(letter in "AB" for letter in before)
    z_done = any(letter in "ab" for letter in before)
    if order[step] in "AB":
        return (2 if y_done == 0 else 1, 1 if z_done else 2, rows, 128)
    return ((4, 2, 1)[y_done], 1, rows, 128)


def kernel(*refs):
    (counts, lengths, positions, audio, cotangent, w_qkv, w_out, w_proj) = refs[:8]
    embeds, grad_qkv, grad_out = refs[8:11]
    (
        wq, wo, wp, tmp, aud, cot_s, cot_r, gt_s, gt_r, t_s, t_r, ag_a, ad_a, e_s, e_r, cot_v, aud_v, emb,
        nb, nt, pj, q2s, qr_s, k_s, v_s, prob, attp_s, agt, mgp, local, other, total, final, prob_t, up_s,
        z_s, z_r, f_s, f_r, w_sem, x_send, x_recv, c_send, c_recv, r_send, r_recv, z_send, z_recv,
    ) = refs[11 : 11 + 48]
    r_bufs = refs[11 + 48 :]

    dp = lax.axis_index("dp")
    x = lax.axis_index("seq")
    y = dp // 16
    z = (dp // 2) % 8
    c = dp % 2
    par = z % 2
    zp = z // 2

    def at(yy, zz, cc):
        return (yy * 16 + zz * 2 + cc, x)

    peers = [(dp, (x + k) % 4) for k in (1, 2, 3)]
    partner = {
        "A": at(y ^ 1, z, c),
        "B": at(y ^ 3, z, c),
        "a": at(y, z ^ 1, c),
        "b": at(y, (z + 7 + 2 * par) % 8, c),
    }
    core_peer = at(y, z, 1 - c)
    z_peers = [at(y, z ^ (2 * k), c) for k in (1, 2, 3)]

    input_copies = [
        pltpu.make_async_copy(src, dst, w_sem.at[3 + i])
        for i, (src, dst) in enumerate(((cotangent, cot_v), (audio, aud_v)))
    ]
    weight_copies = [
        pltpu.make_async_copy(src, dst, w_sem.at[i])
        for i, (src, dst) in enumerate(((w_qkv, wq), (w_out, wo), (w_proj, wp)))
    ]
    for copy in input_copies:
        copy.start()

    barrier = pltpu.get_barrier_semaphore()
    everyone = peers + [core_peer] + list(partner.values()) + z_peers
    for device in everyone:
        pl.semaphore_signal(barrier, inc=1, device_id=device, device_id_type=MESH)

    for i in (2, 0, 1):
        weight_copies[i].start()

    lane = lax.broadcasted_iota(jnp.int32, (112, 128), 1)
    low = lane < 64
    tmp[...] = jnp.zeros_like(tmp)
    pj[...] = jnp.zeros_like(pj)
    mgp[...] = jnp.zeros_like(mgp)
    local[1, :, 384:640] = jnp.zeros((336, 256), BF16)
    input_copies[0].wait()
    cot_rows = cot_v[...].astype(F32)
    for t in range(4):
        cot_s[t] = fold(cot_rows[:, 896 * t : 896 * t + 896], 128, 8)
    cot_r[x] = cot_s[x]

    def pack_audio(b):
        tmp[b, 0:100, 0:320] = aud_v[b].astype(F32)
        first, second, third = (tmp[b, 0:104, 128 * i : 128 * i + 128] for i in range(3))
        second_turned = pltpu.roll(second, 64, 1)
        blank = jnp.zeros((8, 128), F32)
        even_low = jnp.concatenate([third[56:104], blank], axis=0)
        odd_low = jnp.concatenate([first[56:104], blank], axis=0)
        packed = third[0:56] + pltpu.roll(even_low, 64, 1)
        packed_odd = jnp.where(low[0:56], first[0:56], pltpu.roll(odd_low, 64, 1))
        even = jnp.concatenate([first, second, packed, blank], axis=0)
        odd = jnp.concatenate(
            [
                jnp.where(low[0:104], pltpu.roll(first, 64, 1), second_turned),
                jnp.where(low[0:104], second_turned, pltpu.roll(third, 64, 1)),
                packed_odd,
                blank,
            ],
            axis=0,
        )
        aud[x, b] = jnp.where(x % 2 == 0, even, odd).astype(BF16)

    input_copies[1].wait()
    pack_audio(0)

    pl.semaphore_wait(barrier, len(everyone))

    started = []
    def to_peers(slot, source, target):
        copies = []
        for k in (1, 2, 3):
            there = (x + k) % 4
            copy = pltpu.make_async_remote_copy(
                src_ref=source(there),
                dst_ref=target(k),
                send_sem=x_send.at[slot, k - 1],
                recv_sem=x_recv.at[slot, k - 1],
                device_id=(dp, there),
                device_id_type=MESH,
            )
            copy.start()
            copies.append(copy)
        started.extend(copies)
        return copies

    def to_core(slot, source, target):
        copy = pltpu.make_async_remote_copy(
            src_ref=source,
            dst_ref=target,
            send_sem=c_send.at[slot],
            recv_sem=c_recv.at[slot],
            device_id=core_peer,
            device_id_type=MESH,
        )
        copy.start()
        started.append(copy)
        return copy

    def leave(copies):
        for copy in copies:
            copy.wait_send()
            started[:] = [other_copy for other_copy in started if other_copy is not copy]

    def arrive(copies):
        for copy in copies:
            copy.wait_recv()

    audio_copies = []
    cot_copies = to_peers(3, lambda there: cot_s.at[there], lambda k: cot_r.at[x])

    def send_audio(b):
        block = aud.at[x, b]
        audio_copies.append(to_peers(b, lambda there: block, lambda k: block))

    send_audio(0)
    pack_audio(1)
    pack_audio(2)
    leave(cot_copies)
    send_audio(1)
    send_audio(2)

    pos_pad = jnp.concatenate([positions[...].astype(F32), jnp.zeros((13, 50), F32)], axis=0).astype(BF16)
    frame_row = lax.broadcasted_iota(jnp.int32, (50, 112), 0)
    frame_col = lax.broadcasted_iota(jnp.int32, (50, 112), 1)
    spread = jnp.where(frame_row == frame_col // 2, 1.0, 0.0).astype(BF16)
    pos_lanes = dot(pos_pad, spread)
    frame_row_t = lax.broadcasted_iota(jnp.int32, (112, 50), 0)
    frame_col_t = lax.broadcasted_iota(jnp.int32, (112, 50), 1)
    spread_t = jnp.where(frame_row_t // 2 == frame_col_t, 1.0, 0.0).astype(BF16)
    pos_sub = dot_nt(spread_t, pos_pad)
    lives = [jnp.where(b < counts[0], lengths[b], 0) for b in range(3)]

    def place(b, first, count):
        row = lax.broadcasted_iota(jnp.int32, (count, 112), 0) + first
        frame = lax.broadcasted_iota(jnp.int32, (count, 112), 1)
        hit = (row.astype(F32) == pos_lanes[b : b + 1, :]) & (frame < lives[b])
        return jnp.where(hit, 1.0, 0.0).astype(BF16)

    def unplace(b):
        frame = lax.broadcasted_iota(jnp.int32, (112, 160), 0)
        row = lax.broadcasted_iota(jnp.int32, (112, 160), 1)
        hit = (row.astype(F32) == pos_sub[:, b : b + 1]) & (frame < lives[b])
        return jnp.where(hit, 1.0, 0.0).astype(BF16)

    def split_heads(tile):
        return jnp.concatenate([jnp.where(low, tile, 0.0), jnp.where(low, 0.0, tile)], axis=0).astype(BF16)

    weight_copies[0].wait()

    attp = [jnp.zeros((160, 128), F32) for _ in range(3)]
    pooled_audio = jnp.zeros((40, 1280), F32)

    def forward(b, attp, pooled_audio):
        arrive(audio_copies[b])
        tiles = []
        for s in (0, 2):
            left = aud[s, b].astype(F32)
            right = aud[s + 1, b].astype(F32)
            left_rest, right_rest = left[208:264], right[208:264]
            top = jnp.where(low[0:56], left_rest, pltpu.roll(right_rest, 64, 1))
            bottom = jnp.where(low[0:56], pltpu.roll(left_rest, 64, 1), right_rest)
            middle = jnp.concatenate([top, bottom[0:48]], axis=0)
            for tile in (left[0:104], left[104:208], middle, right[0:104], right[104:208]):
                tiles.append(jnp.concatenate([tile, jnp.zeros((8, 128), F32)], axis=0))
        frames = jnp.concatenate(tiles, axis=1)
        pooled_audio = pooled_audio + dot(place(b, 40 * x, 40), frames.astype(BF16))
        normed = normalize(frames)[0].astype(BF16)
        nb[112 * b : 112 * b + 112, :] = normed
        for j in range(3):
            pj[j, :, 0:320] = dot_nt(normed, wq[j])
        k_s[b] = pj[1].astype(BF16)
        v_s[b] = pj[2].astype(BF16)
        key_limit = jnp.maximum(lives[b], 1)
        placed = place(b, 0, 160)
        for g in range(3):
            cols = slice(128 * g, 128 * g + 128)
            q_tile = pj[0, :, cols]
            if g < 2:
                queries = split_heads(q_tile)
                q2s[b, g] = queries
            else:
                queries = q_tile.astype(BF16)
                qr_s[b] = queries
            rows = queries.shape[0]
            scores = dot_nt(queries, k_s[b, :, cols]) * SCALING
            key = lax.broadcasted_iota(jnp.int32, (rows, 112), 1)
            scores = jnp.where(key < key_limit, scores, -1e30)
            powered = jnp.exp(scores - jnp.max(scores, axis=-1, keepdims=True))
            weights = powered * (1.0 / jnp.sum(powered, axis=-1, keepdims=True))
            prob[b, g, 0:rows] = weights
            scores_t = dot_nt(k_s[b, :, cols], queries) * SCALING
            key_t = lax.broadcasted_iota(jnp.int32, (112, rows), 0)
            scores_t = jnp.where(key_t < key_limit, scores_t, -1e30)
            powered_t = jnp.exp(scores_t - jnp.max(scores_t, axis=0, keepdims=True))
            prob_t[b, g, :, 0:rows] = powered_t * (1.0 / jnp.sum(powered_t, axis=0, keepdims=True))
            mixed = dot(weights.astype(BF16), v_s[b, :, cols])
            if g < 2:
                mixed = jnp.where(low, mixed[0:112], mixed[112:224])
            attp[g] = attp[g] + dot(placed, mixed.astype(BF16))
        return attp, pooled_audio

    weight_copies[2].wait()
    arrive(cot_copies)
    row_grads = jnp.concatenate([unfold(cot_r[s], 7) for s in range(4)], axis=0).astype(BF16)
    adapter_terms = dot_nt(row_grads, wp[...])
    for t in range(4):
        gt_s[t] = fold(adapter_terms[40 * t : 40 * t + 40], 640, 0)
    attp, pooled_audio = forward(0, attp, pooled_audio)
    leave(audio_copies[1] + audio_copies[2])
    gt_copies = to_peers(4, lambda there: gt_s.at[there], lambda k: gt_r.at[k - 1])
    attp, pooled_audio = forward(1, attp, pooled_audio)
    attp, pooled_audio = forward(2, attp, pooled_audio)
    attp = [part.astype(BF16) for part in attp]
    for g in range(2):
        attp_s[c, :, 128 * g : 128 * g + 128] = attp[g]
    attp_s[c, :, 256:384] = pltpu.roll(attp[2].astype(F32), 64, 1).astype(BF16)
    weight_copies[1].wait()
    head_terms = (
        dot(attp[0], wo[0:128]) + dot(attp[1], wo[128:256]) + dot(attp[2][:, 0:64], wo[256:320])
    )
    for t in range(4):
        t_s[t] = fold(head_terms[40 * t : 40 * t + 40], 640, 0)
    t_copies = to_peers(5, lambda there: t_s.at[there], lambda k: t_r.at[k - 1])

    nt[c] = nb[...].T
    for b in range(3):
        up_s[b] = unplace(b)
    core_copies = [to_core(0, nt.at[c], nt.at[c]), to_core(1, attp_s.at[c], attp_s.at[c])]

    arrive(gt_copies)
    adapted_grad = gt_s[x].astype(F32)
    for k in range(3):
        adapted_grad = adapted_grad + gt_r[k].astype(F32)
    adapted_grad = unfold(adapted_grad.astype(BF16), 2)

    arrive(t_copies)
    attention = t_s[x].astype(F32)
    for k in range(3):
        attention = attention + t_r[k].astype(F32)
    attention = jnp.concatenate([attention[0:40], attention[40:80]], axis=1)
    normed_rows, inverse = normalize((pooled_audio + attention) * 0.5)
    pooled_grad = inverse * (
        adapted_grad
        - jnp.mean(adapted_grad, axis=-1, keepdims=True)
        - normed_rows * jnp.mean(adapted_grad * normed_rows, axis=-1, keepdims=True)
    )
    ag_a[x] = fold(pooled_grad * 0.5, 640, 0)
    ag_copies = to_peers(6, lambda there: ag_a.at[x], lambda k: ag_a.at[x])
    ad_a[x] = fold(normed_rows, 640, 0)
    arrive(ag_copies)
    attention_grad = jnp.concatenate([unfold(ag_a[s], 2) for s in range(4)], axis=0).astype(BF16)
    mgp[:, 0:320] = dot_nt(attention_grad, wo[...]).astype(BF16)
    pairs = [(b, g) for b in range(3) for g in range(3)]
    grads, prob_grads, prob_grads_t, halves, halves_t = {}, {}, {}, {}, {}
    for b in range(3):
        mixed_grad = dot(up_s[b], mgp[...])
        for g in range(3):
            tile = mixed_grad[:, 128 * g : 128 * g + 128]
            grads[b, g] = split_heads(tile) if g < 2 else tile.astype(BF16)
    for b, g in pairs:
        cols = slice(128 * g, 128 * g + 128)
        prob_grads[b, g] = dot_nt(grads[b, g], v_s[b, :, cols])
        prob_grads_t[b, g] = dot_nt(v_s[b, :, cols], grads[b, g])
    for b, g in pairs:
        count = 224 if g < 2 else 112
        weights, weights_t = prob[b, g, 0:count], prob_t[b, g, :, 0:count]
        inner = jnp.sum(weights * prob_grads[b, g], axis=-1, keepdims=True)
        inner_t = jnp.sum(weights_t * prob_grads_t[b, g], axis=0, keepdims=True)
        halves[b, g] = (weights * (prob_grads[b, g] - inner)).astype(BF16)
        halves_t[b, g] = (weights_t * (prob_grads_t[b, g] - inner_t)).astype(BF16)
    for b in range(3):
        rows = slice(112 * b, 112 * b + 112)
        for g in range(3):
            cols = slice(128 * g, 128 * g + 128)
            count = 224 if g < 2 else 112
            query_grad = dot(halves[b, g], k_s[b, :, cols])
            if g < 2:
                query_grad = jnp.where(low, query_grad[0:112], query_grad[112:224])
            query_grad = query_grad * SCALING
            key_grad = dot(halves_t[b, g], q2s[b, g] if g < 2 else qr_s[b]) * SCALING
            value_grad = dot(prob_t[b, g, :, 0:count].astype(BF16), grads[b, g])
            local[1, rows, cols] = value_grad.astype(BF16)
            if g < 2:
                local[0, rows, cols] = query_grad.astype(BF16)
                local[0, rows, 256 + 128 * g : 384 + 128 * g] = key_grad.astype(BF16)
            else:
                local[0, rows, 512:640] = (query_grad + pltpu.roll(key_grad, 64, 1)).astype(BF16)
    agt[c] = attention_grad.T
    core_copies.append(to_core(2, local.at[1 - c], other))
    core_copies.append(to_core(3, agt.at[c], agt.at[c]))
    ad_copies = to_peers(7, lambda there: ad_a.at[x], lambda k: ad_a.at[x])

    def start_embeds():
        arrive(ad_copies)
        adapted = jnp.concatenate([unfold(ad_a[s], 2) for s in range(4)], axis=0).astype(BF16)
        adapter_rows = dot(adapted, wp[...])
        for t in range(4):
            e_s[t] = fold(adapter_rows[40 * t : 40 * t + 40], 128, 8)
        e_r[x] = e_s[x]
        return to_peers(8, lambda there: e_s.at[there], lambda k: e_r.at[x])

    def finish_embeds(copies):
        arrive(copies)
        for s in range(4):
            emb[:, 896 * s : 896 * s + 896] = unfold(e_r[s], 7).astype(BF16)
        copy = pltpu.make_async_copy(emb, embeds, w_sem.at[5])
        copy.start()
        return copy

    def blocks(order, step):
        y_before = [letter for letter in order[:step] if letter in "AB"]
        z_done = any(letter in "ab" for letter in order[:step])
        letter = order[step]
        if letter in "AB":
            near = y ^ (1 if letter == "A" else 3)
            beyond = y ^ (3 if letter == "A" else 1)
            sides = (par, par) if z_done else (None, None)
            if y_before:
                return [near], [y], sides
            return [y ^ 2, near], [beyond, y], sides
        held = [y ^ 2, y ^ 1, y ^ 3, y]
        if len(y_before) == 1:
            held = [y ^ (3 if y_before[0] == "A" else 1), y]
        elif len(y_before) == 2:
            held = [y]
        return held, held, (1 - par, par)

    def begin(p, step, only=None):
        tile, row, count, order = PARTS[p]
        send, _, (side, _) = blocks(order, step)
        landing = r_bufs[3 * p + step]
        copies = []
        for i, block in enumerate(send):
            if only is not None and i != only:
                continue
            pick = pl.ds(0, 2) if side is None else pl.ds(side, 1)
            copy = pltpu.make_async_remote_copy(
                src_ref=total.at[block, tile, pick, pl.ds(row, count)],
                dst_ref=landing.at[i],
                send_sem=r_send.at[p, step, i],
                recv_sem=r_recv.at[p, step, i],
                device_id=partner[order[step]],
                device_id_type=MESH,
            )
            copy.start()
            copies.append(copy)
        started.extend(copies)
        return copies

    def end(p, step, copies):
        tile, row, count, order = PARTS[p]
        _, keep, (_, side) = blocks(order, step)
        landing = r_bufs[3 * p + step]
        rows = pl.ds(row, count)
        arrive(copies)
        for i, block in enumerate(keep):
            if step == 2:
                final[tile, rows] = total[block, tile, par, rows].astype(F32) + landing[i, 0].astype(F32)
            elif side is None:
                for k in range(2):
                    kept = total[block, tile, k, rows].astype(F32) + landing[i, k].astype(F32)
                    total[block, tile, k, rows] = kept.astype(BF16)
            else:
                kept = total[block, tile, side, rows].astype(F32) + landing[i, 0].astype(F32)
                total[block, tile, side, rows] = kept.astype(BF16)

    arrive(core_copies)
    flying = {(p, 0): [] for p in range(len(PARTS))}
    turns = (y ^ 2, y ^ 1, y ^ 3, y)
    for turn, yy in enumerate(turns):
        rows = pl.ds(pl.multiple_of(320 * yy, 64), 320)

        def store(tile, values):
            for side in range(2):
                total[yy, tile, side] = jnp.concatenate(
                    [values[40 * i : 40 * i + 40] for i in range(side, 8, 2)], axis=0
                ).astype(BF16)

        @pl.when(c == 0)
        def _():
            part = dot(nt[0, rows], local[0]) + dot(nt[1, rows], other[...])
            for t in range(5):
                store(t, part[:, 128 * t : 128 * t + 128])

        @pl.when(c == 1)
        def _():
            value_part = dot(nt[1, rows], local[1, :, 0:384]) + dot(nt[0, rows], other[:, 0:384])
            out_part = dot(agt[0, rows], attp_s[0]) + dot(agt[1, rows], attp_s[1])
            store(0, value_part[:, 0:128])
            store(1, value_part[:, 128:256])
            store(2, out_part[:, 0:128])
            store(3, out_part[:, 128:256])
            store(4, value_part[:, 256:384] + out_part[:, 256:384])

        for p in WAVES[0]:
            slots = {"A": (0, 1, None, None), "B": (0, None, 1, None)}.get(PARTS[p][3][0], (0, 1, 2, 3))
            if slots[turn] is not None:
                flying[p, 0] += begin(p, 0, slots[turn])
    z_copies = []

    def last_exchange(wave):
        tiles, first, count = Z_GROUPS[wave]
        fill = count - 40 * len(tiles)
        for j in range(4):
            pieces = [final[t, 40 * j : 40 * j + 40] for t in tiles]
            if fill:
                pieces.append(jnp.zeros((fill, 128), F32))
            z_s[j, first : first + count] = jnp.concatenate(pieces, axis=0).astype(BF16)
        for k in (1, 2, 3):
            copy = pltpu.make_async_remote_copy(
                src_ref=z_s.at[zp ^ k, pl.ds(first, count)],
                dst_ref=z_r.at[k - 1, pl.ds(first, count)],
                send_sem=z_send.at[wave, k - 1],
                recv_sem=z_recv.at[wave, k - 1],
                device_id=z_peers[k - 1],
                device_id_type=MESH,
            )
            copy.start()
            z_copies.append(copy)
            started.append(copy)

    def step(wave, number):
        for p in WAVES[wave]:
            end(p, number - 1, flying[p, number - 1])
            if number < 3:
                flying[p, number] = begin(p, number)

    for p in WAVES[1]:
        flying[p, 0] = begin(p, 0)
    step(0, 1)
    step(1, 1)
    step(0, 2)
    step(1, 2)
    embed_copies = start_embeds()
    step(0, 3)
    last_exchange(0)
    step(1, 3)
    last_exchange(1)
    embeds_copy = finish_embeds(embed_copies)
    arrive(z_copies)
    mine = z_s[zp].astype(F32)
    for k in range(3):
        mine = mine + z_r[k].astype(F32)
    first_core = c == 0
    own_tiles = []
    f_s[...] = jnp.zeros_like(f_s)
    for t in range(5):
        rows = mine[TILE_ROWS[t] : TILE_ROWS[t] + 40]
        early, late = rows[0:20], rows[20:40]
        own_tiles.append(jnp.where(first_core, early, late))
        f_s[t, 0:20] = jnp.where(first_core, late, early).astype(BF16)
    arrive([to_core(4, f_s, f_r)])
    for t in range(5):
        got = f_r[t, 0:20].astype(F32)
        left = jnp.where(first_core, own_tiles[t], got)
        right = jnp.where(first_core, got, own_tiles[t])
        if t < 2:
            cols = slice(128 * t, 128 * t + 128)
            grad_qkv[0, :, cols] = left
            grad_qkv[2, :, cols] = right
        elif t < 4:
            cols = slice(128 * t - 256, 128 * t - 128)
            grad_qkv[1, :, cols] = left
            grad_out[:, cols] = right
        else:
            grad_qkv[0, :, 256:320] = left[:, 0:64]
            grad_qkv[1, :, 256:320] = left[:, 64:128]
            grad_qkv[2, :, 256:320] = right[:, 0:64]
            grad_out[:, 256:320] = right[:, 64:128]
    embeds_copy.wait()
    for copy in started:
        copy.wait_send()


def call(counts, lengths, positions, audio, cotangent, w_qkv, w_out, w_proj):
    vmem, dma = pltpu.VMEM, pltpu.SemaphoreType.DMA
    scratch = [
        vmem((3, 320, 1280), BF16),
        vmem((320, 1280), BF16),
        vmem((1280, 896), BF16),
        vmem((3, 128, 384), F32),
        vmem((4, 3, 272, 128), BF16),
        vmem((4, 288, 128), BF16),
        vmem((4, 288, 128), BF16),
        vmem((4, 80, 640), BF16),
        vmem((3, 80, 640), BF16),
        vmem((4, 80, 640), BF16),
        vmem((3, 80, 640), BF16),
        vmem((4, 80, 640), BF16),
        vmem((4, 80, 640), BF16),
        vmem((4, 288, 128), BF16),
        vmem((4, 288, 128), BF16),
        vmem((40, 3584), BF16),
        vmem((3, 100, 320), BF16),
        vmem((40, 3584), BF16),
        vmem((336, 1280), BF16),
        vmem((2, 1280, 336), BF16),
        vmem((3, 112, 384), F32),
        vmem((3, 2, 224, 128), BF16),
        vmem((3, 112, 128), BF16),
        vmem((3, 112, 384), BF16),
        vmem((3, 112, 384), BF16),
        vmem((3, 3, 224, 112), F32),
        vmem((2, 160, 384), BF16),
        vmem((2, 1280, 160), BF16),
        vmem((160, 384), BF16),
        vmem((2, 336, 640), BF16),
        vmem((336, 640), BF16),
        vmem((4, 5, 2, 160, 128), BF16),
        vmem((5, 160, 128), F32),
        vmem((3, 3, 112, 224), F32),
        vmem((3, 112, 160), BF16),
        vmem((4, 208, 128), BF16),
        vmem((3, 208, 128), BF16),
        vmem((5, 32, 128), BF16),
        vmem((5, 32, 128), BF16),
        dma((6,)),
        dma((9, 3)),
        dma((9, 3)),
        dma((5,)),
        dma((5,)),
        dma((len(PARTS), 3, 4)),
        dma((len(PARTS), 3, 4)),
        dma((2, 3)),
        dma((2, 3)),
    ]
    assert len(scratch) == 48
    scratch += [vmem(received_shape(part, step), BF16) for part in PARTS for step in range(3)]
    in_vmem = pl.BlockSpec(memory_space=pltpu.VMEM)
    in_smem = pl.BlockSpec(memory_space=pltpu.SMEM)
    anywhere = pl.BlockSpec(memory_space=pl.ANY)
    return pl.pallas_call(
        kernel,
        out_shape=(
            jax.ShapeDtypeStruct((40, 3584), BF16),
            jax.ShapeDtypeStruct((3, 20, 320), F32),
            jax.ShapeDtypeStruct((20, 320), F32),
        ),
        in_specs=[in_smem, in_smem, in_vmem] + [anywhere] * 5,
        out_specs=(anywhere, in_vmem, in_vmem),
        scratch_shapes=scratch,
        compiler_params=pltpu.CompilerParams(
            collective_id=0, has_side_effects=True, vmem_limit_bytes=60 * 2**20
        ),
        name="sublayer",
    )(counts, lengths, positions, audio, cotangent, w_qkv, w_out, w_proj)


def write_out(*refs):
    sources, targets, held, sems = refs[:3], refs[3:6], refs[6:9], refs[9]
    arriving = [pltpu.make_async_copy(sources[i], held[i], sems.at[0, i]) for i in range(3)]
    leaving = [pltpu.make_async_copy(held[i], targets[i], sems.at[1, i]) for i in range(3)]
    for copy in arriving:
        copy.start()
    for i in (1, 2, 0):
        arriving[i].wait()
        leaving[i].start()
    for copy in leaving:
        copy.wait()


def results(*parts):
    anywhere = pl.BlockSpec(memory_space=pl.ANY)
    return pl.pallas_call(
        write_out,
        out_shape=tuple(jax.ShapeDtypeStruct(part.shape, part.dtype) for part in parts),
        in_specs=[anywhere] * 3,
        out_specs=(anywhere,) * 3,
        scratch_shapes=[pltpu.VMEM(part.shape, part.dtype) for part in parts]
        + [pltpu.SemaphoreType.DMA((2, 3))],
        compiler_params=pltpu.CompilerParams(vmem_limit_bytes=60 * 2**20),
        name="results",
    )(*parts)


def shards(audio, counts, lengths, positions, w_qkv, w_out, w_proj, cotangent):
    embeds, grad_qkv, grad_out = call(
        counts, lengths, positions, audio, cotangent, jnp.swapaxes(w_qkv, 1, 2), w_out, w_proj
    )
    embeds, grad_qkv, grad_out = results(embeds, grad_qkv, grad_out)
    return embeds, grad_qkv, grad_out.T


def solution(mesh):
    in_specs = (
        P("dp", None, "seq"),
        P("dp"),
        P("dp"),
        P("dp", None),
        P(None, None, "seq"),
        P("seq", None),
        P(None, "seq"),
        P(("dp", "seq"), None),
    )
    out_specs = (P(("dp", "seq"), None), P(None, "dp", "seq"), P("seq", "dp"))
    return jax.shard_map(shards, mesh=mesh, in_specs=in_specs, out_specs=out_specs, check_vma=False)
```
